32 devices in a mesh: grp: 1, gx: 8 (over z, core), gy: 4 (over y, x).
Axes of the slice: x: 2, y: 2, z: 4, core: 2. Of those that a mesh axis runs over, the one named last changes fastest.
Arguments:
- features: bfloat16 [20, 64, 128, 128], P(None, ('grp', 'gx'), 'gy'), may hold values from -6 to 6
- spectral_weight: float32 [2, 20, 20, 8, 128, 64], P(None, None, None, 'gy', 'gx'), may hold values from -6 to 6
- conv_weight: bfloat16 [3, 27, 20, 20], replicated, may hold values from -0.75 to 0.75
- point_weight: bfloat16 [20, 20], replicated, may hold values from -1.25 to 1.25
Outputs:
- layer_output: bfloat16 [20, 64, 128, 128], P(None, ('grp', 'gx'), 'gy')
The draws below stay inside these ranges and needn't reach their ends.
All inputs are finite; a program needn't handle non-finite values.
Results may differ from the reference program's by a relative error of at most 0.014.
Values may be sent and summed in bfloat16 or wider, within the bound.
No kernel may reach another device: no remote copies, remote signals or barrier semaphores. Data moves between devices by JAX's collectives and lax.ppermute only.
A program may use at most 128 MiB of HBM per device.

```python
import math
import jax
import jax.numpy as jnp
from jax import lax

C = 20
MY = 128
MZ = 8
NZ = 128
NX = 64
NY = 128
KX = 64


def block_scale(own_key, dims, shards, low, top_value):
    def one(dim, parts):
        draws = jax.random.uniform(jax.random.fold_in(jax.random.fold_in(own_key, 6), dim), (parts,), jnp.float32, low / len(shards), top_value / len(shards))
        return jnp.repeat(jnp.exp(draws), dims[dim] // parts).reshape((-1,) + (1,) * (len(dims) - dim - 1))

    level = one(*shards[0])
    for cut in shards[1:]:
        level = level * one(*cut)
    return level


def scatter_about(stream_key, shape, scale, limit, cuts=(), held_as=jnp.bfloat16):
    array = scale * jax.random.normal(stream_key, shape, jnp.float32)
    if cuts:
        array = array * block_scale(stream_key, shape, cuts, -0.22, 0.18)
    return jnp.clip(array, -limit, limit).astype(held_as)


def setup_inputs(seed: int = 0, part: int = 0) -> dict:
    arg_keys = jax.random.split(jax.random.key(seed), 5)
    part_keys = jax.random.split(jax.random.fold_in(arg_keys[4], part), 5)
    return {
        "features": scatter_about(part_keys[0], (C, NX, NY, NZ), 1.0, 6.0, ((1, 8), (2, 4))),
        "spectral_weight": scatter_about(arg_keys[1], (2, C, C, MZ, MY, KX), 1.0, 6.0, ((3, 4), (4, 8)), jnp.float32),
        "conv_weight": scatter_about(arg_keys[2], (3, 27, C, C), (3 * C) ** -0.5, 0.75),
        "point_weight": scatter_about(arg_keys[3], (C, C), C ** -0.5, 1.25),
    }


def signed_modes(count):
    position = jnp.arange(count, dtype=jnp.int32)
    return jnp.where(position < count // 2, position, position - count).astype(jnp.int32)


def phase_table(frequency, length):
    positions = jnp.arange(length, dtype=jnp.int32)
    product = jnp.mod(frequency[:, None] * positions[None, :], length)
    angle = product.astype(jnp.float32) * (2.0 * math.pi / length)
    return jnp.cos(angle).astype(jnp.bfloat16), jnp.sin(angle).astype(jnp.bfloat16)


def expand(form, left, right):
    return jnp.einsum(form, left.astype(jnp.float32), right.astype(jnp.float32), precision=lax.Precision.HIGHEST)


def convolve(volume, kernel):
    size_x, size_y, size_z = volume.shape[1], volume.shape[2], volume.shape[3]
    padded = jnp.pad(volume.astype(jnp.float32), ((0, 0), (1, 1), (1, 1), (1, 1)))
    summed_taps = jnp.zeros((kernel.shape[1], size_x, size_y, size_z), jnp.float32)
    for tap_index in range(27):
        shift_x = tap_index // 9
        shift_y = (tap_index // 3) % 3
        shift_z = tap_index % 3
        window = padded[:, shift_x:shift_x + size_x, shift_y:shift_y + size_y, shift_z:shift_z + size_z]
        summed_taps = summed_taps + jnp.einsum('oi,ixyz->oxyz', kernel[tap_index].astype(jnp.float32), window, precision=lax.Precision.HIGHEST)
    return summed_taps


def reference(features, spectral_weight, conv_weight, point_weight):
    values = features.astype(jnp.float32)
    freq_z = jnp.arange(MZ, dtype=jnp.int32)
    cos_z, sin_z = phase_table(freq_z, NZ)
    cos_y, sin_y = phase_table(signed_modes(MY), NY)
    cos_x, sin_x = phase_table(signed_modes(KX), NX)
    zr = expand('cxyz,kz->kcxy', features, cos_z).astype(jnp.bfloat16)
    zi = (-expand('cxyz,kz->kcxy', features, sin_z)).astype(jnp.bfloat16)
    yr = (expand('kcxy,jy->kcxj', zr, cos_y) + expand('kcxy,jy->kcxj', zi, sin_y)).astype(jnp.bfloat16)
    yi = (expand('kcxy,jy->kcxj', zi, cos_y) - expand('kcxy,jy->kcxj', zr, sin_y)).astype(jnp.bfloat16)
    xr = expand('kcxj,mx->kcjm', yr, cos_x) + expand('kcxj,mx->kcjm', yi, sin_x)
    xi = expand('kcxj,mx->kcjm', yi, cos_x) - expand('kcxj,mx->kcjm', yr, sin_x)
    highest = lax.Precision.HIGHEST
    form = 'kijm,iokjm->kojm'
    wr = spectral_weight[0]
    wi = spectral_weight[1]
    mr = (jnp.einsum(form, xr, wr, precision=highest) - jnp.einsum(form, xi, wi, precision=highest)).astype(jnp.bfloat16)
    mi = (jnp.einsum(form, xr, wi, precision=highest) + jnp.einsum(form, xi, wr, precision=highest)).astype(jnp.bfloat16)
    br = (expand('kojm,mx->koxj', mr, cos_x) - expand('kojm,mx->koxj', mi, sin_x)).astype(jnp.bfloat16)
    bi = (expand('kojm,mx->koxj', mi, cos_x) + expand('kojm,mx->koxj', mr, sin_x)).astype(jnp.bfloat16)
    lr = (expand('koxj,jy->koxy', br, cos_y) - expand('koxj,jy->koxy', bi, sin_y)).astype(jnp.bfloat16)
    li = (expand('koxj,jy->koxy', bi, cos_y) + expand('koxj,jy->koxy', br, sin_y)).astype(jnp.bfloat16)
    scale_z = jnp.where(freq_z == 0, 1.0, 2.0).astype(jnp.float32) / float(NX * NY * NZ)
    spectral = jnp.einsum('koxy,kz->oxyz', lr.astype(jnp.float32), cos_z.astype(jnp.float32) * scale_z[:, None], precision=highest)
    spectral = spectral - jnp.einsum('koxy,kz->oxyz', li.astype(jnp.float32), sin_z.astype(jnp.float32) * scale_z[:, None], precision=highest)
    coarse = values.reshape(C, NX // 2, 2, NY // 2, 2, NZ // 2, 2).mean(axis=(2, 4, 6)).astype(jnp.bfloat16)
    first = jax.nn.gelu(convolve(coarse, conv_weight[0]), approximate=False).astype(jnp.bfloat16)
    second = jax.nn.gelu(convolve(first, conv_weight[1]), approximate=False).astype(jnp.bfloat16)
    third = convolve(second, conv_weight[2]).astype(jnp.bfloat16)
    upsampled = jnp.repeat(jnp.repeat(jnp.repeat(third, 2, axis=1), 2, axis=2), 2, axis=3)
    pointwise = jnp.einsum('io,ixyz->oxyz', point_weight.astype(jnp.float32), values, precision=highest)
    return jax.nn.gelu(spectral + pointwise + upsampled.astype(jnp.float32), approximate=False).astype(jnp.bfloat16)
```

```python
import functools
import math

import jax
import jax.numpy as jnp
import numpy as np
from jax import lax
from jax.experimental import pallas as pl
from jax.experimental.pallas import tpu as pltpu
from jax.sharding import PartitionSpec as P

LANES = 128
BF16 = jnp.bfloat16
F32 = jnp.float32
MIB = 1024 * 1024


def dot(left, right):
    return jnp.dot(left, right, preferred_element_type=F32)


def signed_modes(count):
    position = np.arange(count)
    return np.where(position < count // 2, position, position - count)


def phase(frequency, length):
    index = np.mod(frequency[:, None] * np.arange(length)[None, :], length)
    angle = index.astype(np.float32) * np.float32(2.0 * math.pi / length)
    return (
        np.cos(angle).astype(BF16).astype(np.float32),
        np.sin(angle).astype(BF16).astype(np.float32),
    )


def const(array):
    return np.asarray(array, np.float32).astype(BF16)


class Plan:
    def __init__(self, features, spectral_weight, devices_x, devices_y):
        self.channels, self.cx, self.cy, self.cz = features
        self.dx, self.dy = devices_x, devices_y
        self.kz, self.ky, self.kx = spectral_weight[3:]
        self.gx, self.gy = self.cx * self.dx, self.cy * self.dy
        self.my = self.ky * self.dx
        self.mz = self.kz * self.dy
        self.unit = 2 * self.kz * self.cx
        self.groups = LANES // self.unit
        self.cg = self.channels // self.groups

    def forward_z(self):
        cos, sin = phase(np.arange(self.mz), self.cz)
        table = np.stack([cos, -sin], 0).reshape(2, self.dy, self.kz, self.cz)
        out = np.einsum("pdkz,xw->xzdpkw", table, np.eye(self.cx))
        return const(out.reshape(self.cx * self.cz, self.dy * self.unit))

    def inverse_z(self):
        cos, sin = phase(np.arange(self.mz), self.cz)
        scale = np.where(np.arange(self.mz) == 0, 1.0, 2.0) / float(self.gx * self.gy * self.cz)
        table = np.stack([cos, -sin], 0) * scale[None, :, None]
        table = table.reshape(2, self.dy, self.kz, self.cz)
        out = np.einsum("pdkz,xw->dpkxwz", table, np.eye(self.cx))
        return const(out.reshape(self.dy * self.unit, self.cx * self.cz))

    def regroup(self, outer, inner):
        out = np.einsum("ac,bd,lm->abldcm", np.eye(outer), np.eye(inner), np.eye(self.unit))
        size = outer * inner * self.unit
        return const(out.reshape(size, size))

    def swap(self, sign):
        turn = np.array([[0.0, -sign], [sign, 0.0]])
        half = self.unit // 2
        return const(np.kron(np.eye(self.groups), np.kron(turn, np.eye(half))))

    def forward_y(self):
        cos, sin = phase(signed_modes(self.my), self.gy)
        return const(np.concatenate([cos, sin], 1))

    def inverse_y(self):
        cos, sin = phase(signed_modes(self.my), self.gy)
        return const(np.concatenate([cos.T, sin.T], 1))

    def forward_x(self):
        cos, sin = phase(signed_modes(self.kx), self.gx)
        turn = np.stack([np.stack([cos, -sin]), np.stack([sin, cos])])
        turn = turn.reshape(2, 2, self.kx, self.dx, self.cx)
        out = np.einsum("pqjsx,gh,kl->sgpkxhlqj", turn, np.eye(self.groups), np.eye(self.kz))
        return const(out.reshape(self.dx * LANES, self.groups * self.kz * 2 * self.kx))

    def inverse_x(self):
        cos, sin = phase(signed_modes(self.kx), self.gx)
        turn = np.stack([np.stack([cos, sin]), np.stack([-sin, cos])])
        turn = turn.reshape(2, 2, self.kx, self.dx, self.cx)
        out = np.einsum("pqjsx,gh,kl->gkpjshqlx", turn, np.eye(self.groups), np.eye(self.kz))
        return const(out.reshape(self.groups * self.kz * 2 * self.kx, self.dx * LANES))


VMEM = pl.BlockSpec(memory_space=pltpu.VMEM)
SMEM = pl.BlockSpec(memory_space=pltpu.SMEM)


def call(body, outs, inputs, scratch=(), specs=None, vmem=8, flops=1e9, moved=1e6, **kw):
    return pl.pallas_call(
        body,
        out_shape=outs,
        in_specs=specs or [VMEM] * len(inputs),
        out_specs=kw.pop("out_specs", jax.tree.map(lambda _: VMEM, outs)),
        scratch_shapes=scratch,
        compiler_params=pltpu.CompilerParams(vmem_limit_bytes=vmem * MIB),
        cost_estimate=pl.CostEstimate(
            flops=int(flops), bytes_accessed=int(moved), transcendentals=0
        ),
        **kw,
    )(*inputs)


def z_body(plan, field, table, regroup, out):
    rows = plan.channels * plan.cy
    lhs = jnp.concatenate(
        [field[:, x].reshape(rows, plan.cz) for x in range(plan.cx)], axis=1
    )
    modes = dot(lhs, table[...]).astype(BF16)
    part = plan.cg * plan.cy
    lanes = jnp.concatenate(
        [modes[g * part : (g + 1) * part] for g in range(plan.groups)], axis=1
    )
    result = dot(lanes, regroup[...]).astype(BF16)
    for d in range(plan.dy):
        out[d] = result[:, d * LANES : (d + 1) * LANES].reshape(plan.cg, plan.cy, LANES)


def y_body(plan, line, table, swap, out):
    sources, _, rows, _ = line.shape
    targets = out.shape[0]
    rows_out = out.shape[2]
    columns = []
    for c in range(plan.cg):
        value = jnp.concatenate([line[s, c] for s in range(sources)], axis=0)
        turned = dot(value, swap[...]).astype(BF16)
        columns.append(jnp.concatenate([value, turned], axis=0))
    result = dot(table[...], jnp.concatenate(columns, axis=1)).astype(BF16)
    for d in range(targets):
        for c in range(plan.cg):
            out[d, c] = result[
                d * rows_out : (d + 1) * rows_out, c * LANES : (c + 1) * LANES
            ]


def mix(plan, spec, weight, mixed):
    def step(o, carry):
        for k in range(plan.kz):
            real = jnp.zeros((plan.ky, plan.kx), F32)
            imag = jnp.zeros((plan.ky, plan.kx), F32)
            for i in range(plan.channels):
                wr = weight[0, i, o, k]
                wi = weight[1, i, o, k]
                xr = spec[0, k, i]
                xi = spec[1, k, i]
                real += xr * wr - xi * wi
                imag += xr * wi + xi * wr
            mixed[k, o] = jnp.concatenate([real, imag], axis=1)
        return carry

    lax.fori_loop(0, plan.channels, step, 0)


def x_body(plan, pencil, forward, weight, inverse, out, spec, mixed):
    rows = plan.cg * plan.ky
    kx = plan.kx
    lhs = jnp.concatenate([pencil[s].reshape(rows, LANES) for s in range(plan.dx)], axis=1)
    spectrum = dot(lhs, forward[...])
    for g in range(plan.groups):
        for k in range(plan.kz):
            for p in range(2):
                start = ((g * plan.kz + k) * 2 + p) * kx
                block = spectrum[:, start : start + kx]
                for c in range(plan.cg):
                    spec[p, k, g * plan.cg + c] = block[c * plan.ky : (c + 1) * plan.ky]
    mix(plan, spec, weight, mixed)
    back = jnp.concatenate(
        [
            mixed[k, g * plan.cg : (g + 1) * plan.cg].reshape(rows, 2 * kx).astype(BF16)
            for g in range(plan.groups)
            for k in range(plan.kz)
        ],
        axis=1,
    )
    result = dot(back, inverse[...]).astype(BF16)
    for d in range(plan.dx):
        out[d] = result[:, d * LANES : (d + 1) * LANES].reshape(plan.cg, plan.ky, LANES)


def x_stage_general(plan, pencil, weight):
    groups, cg, ky, kz, kx = plan.groups, plan.cg, plan.ky, plan.kz, plan.kx
    lhs = jnp.transpose(pencil, (1, 2, 0, 3)).reshape(cg * ky, plan.dx * LANES)
    spectrum = dot(lhs, plan.forward_x()).reshape(cg, ky, groups, kz, 2, kx)
    spectrum = jnp.transpose(spectrum, (4, 3, 2, 0, 1, 5)).reshape(2, kz, groups * cg, ky, kx)
    mixed = call(
        functools.partial(mix, plan),
        jax.ShapeDtypeStruct((kz, groups * cg, ky, 2 * kx), F32),
        (spectrum, weight),
        vmem=32,
    )
    back = jnp.transpose(mixed.reshape(kz, groups, cg, ky, 2 * kx), (2, 3, 1, 0, 4))
    back = back.reshape(cg * ky, groups * kz * 2 * kx).astype(BF16)
    back = dot(back, plan.inverse_x()).astype(BF16).reshape(cg, ky, plan.dx, LANES)
    return jnp.transpose(back, (2, 0, 1, 3))


CP = 24


def gelu(value):
    return 0.5 * value * (1.0 + lax.erf(value * (0.5**0.5)))


def pool_tables(plan):
    half = plan.cy // 2
    quarter = half // 2
    rows = np.einsum(
        "cC,yY->ycCY", np.eye(CP)[:, : plan.channels], np.kron(np.eye(quarter), np.ones((1, 2)))
    ).reshape(quarter * CP, plan.channels * half)
    rows = np.concatenate([rows, rows], 1)
    pairs = np.kron(np.eye(plan.cz), np.full((2, 1), 0.125))
    return const(rows), const(pairs)


def pool_body(plan, field, rows_table, pair_table, out):
    half = plan.cy // 2
    quarter = half // 2
    cells = plan.channels * half
    for h in range(2):
        columns = []
        for x in range(plan.cx // 2):
            columns.append(
                jnp.concatenate(
                    [
                        field[:, 2 * x + e, h * half : (h + 1) * half].reshape(cells, plan.cz)
                        for e in range(2)
                    ],
                    axis=0,
                )
            )
        summed = dot(rows_table[...], jnp.concatenate(columns, axis=1))
        blocks = []
        for x in range(plan.cx // 2):
            for j in range(quarter // 2):
                blocks.append(
                    jnp.concatenate(
                        [
                            summed[
                                (2 * j + e) * CP : (2 * j + e + 1) * CP,
                                x * plan.cz : (x + 1) * plan.cz,
                            ]
                            for e in range(2)
                        ],
                        axis=1,
                    )
                )
        block = jnp.concatenate(blocks, axis=0)
        high = block.astype(BF16)
        low = (block - high.astype(F32)).astype(BF16)
        result = dot(high, pair_table[...]) + dot(low, pair_table[...])
        index = 0
        for x in range(plan.cx // 2):
            for j in range(quarter // 2):
                out[x, h * (quarter // 2) + j] = result[index * CP : (index + 1) * CP].astype(BF16)
                index += 1


def conv_body(
    plan, flags, own, y_low, y_high, x_low, x_high, filters, point, spread, pick_o, pick_i, diag,
    fixed, third, lift, volume, partial,
):
    nx = plan.cx // 2
    ny = plan.cy // 4
    wide = ny + 4
    lane = lax.broadcasted_iota(jnp.int32, (CP, LANES), 1)
    z = lane % (LANES // 2)
    lower = lane < LANES // 2
    first_z = z == 0
    last_z = z == LANES // 2 - 1
    zero = jnp.zeros((CP, LANES), F32)

    expanded = dot(dot(pick_o[...], point[...]).astype(BF16), pick_i[...]).astype(BF16)
    wide_cols = expanded.shape[1]
    lift[:, :wide_cols] = expanded * diag[...]
    lift[:, wide_cols:] = fixed[...]

    def tile(x, j):
        if x < 3:
            return x_low[x, j]
        if x >= 3 + nx:
            return x_high[x - 3 - nx, j]
        if j < 2:
            return y_low[x - 3, j]
        if j >= 2 + ny:
            return y_high[x - 3, j - 2 - ny]
        return own[x - 3, j - 2]

    for x in range(nx + 6):
        for j in range(wide):
            volume[x, j] = tile(x, j).astype(F32)

    def layer(number, planes, tiles):
        def multiply(x, carry):
            shifted = {}
            for j in range(tiles[0] - 1, tiles[1] + 1):
                value = volume[x, j]
                versions = (
                    jnp.where(first_z, 0.0, pltpu.roll(value, 1, 1)),
                    value,
                    jnp.where(last_z, 0.0, pltpu.roll(value, LANES - 1, 1)),
                )
                shifted[j] = (versions, [pltpu.roll(v, LANES // 2, 1) for v in versions])
            columns = []
            for j in range(tiles[0], tiles[1]):
                pieces = []
                for e in range(3):
                    pieces.append(jnp.where(lower, shifted[j - 1][1][e], shifted[j][1][e]))
                for e in range(3):
                    pieces.append(shifted[j][0][e])
                for e in range(3):
                    pieces.append(jnp.where(lower, shifted[j][1][e], shifted[j + 1][1][e]))
                columns.append(jnp.concatenate(pieces, axis=0).astype(BF16))
            partial[x, :, : (tiles[1] - tiles[0]) * LANES] = dot(
                filters[number], jnp.concatenate(columns, axis=1)
            )
            return carry

        lax.fori_loop(0, planes, multiply, 0)

        def combine(x, carry):
            margin = (planes - 2 - nx) // 2
            inside = jnp.where(x < margin, flags[0], 1.0) * jnp.where(
                x >= margin + nx, flags[1], 1.0
            )
            for j in range(tiles[0], tiles[1]):
                cols = slice((j - tiles[0]) * LANES, (j - tiles[0] + 1) * LANES)
                total = (
                    partial[x, 0:CP, cols]
                    + partial[x + 1, CP : 2 * CP, cols]
                    + partial[x + 2, 2 * CP : 3 * CP, cols]
                )
                if number < 2:
                    scale = inside
                    if j < 2:
                        scale = scale * flags[2]
                    if j >= 2 + ny:
                        scale = scale * flags[3]
                    total = gelu(total).astype(BF16).astype(F32) * scale
                    volume[x, j] = total
                else:
                    up = dot(total.astype(BF16), spread[...]).astype(BF16)
                    third[x, 2 * (j - 2)] = up[:, : plan.cz]
                    third[x, 2 * (j - 2) + 1] = up[:, plan.cz :]
            return carry

        lax.fori_loop(0, planes - 2, combine, 0)

    layer(0, nx + 6, (1, ny + 3))
    for x in range(nx + 4):
        volume[x, 0] = zero
        volume[x, wide - 1] = zero
    layer(1, nx + 4, (1, ny + 3))
    layer(2, nx + 2, (2, ny + 2))


def final_body(plan, field, third, line, lift, regroup, inverse, out, lanes):
    step = pl.program_id(0)
    half = plan.cy // 2
    part = plan.cg * plan.cy

    @pl.when(step == 0)
    def _():
        gathered = jnp.concatenate(
            [line[s].reshape(part, LANES) for s in range(plan.dy)], axis=1
        )
        result = dot(gathered, regroup[...]).astype(BF16)
        width = plan.dy * plan.unit
        for g in range(plan.groups):
            lanes[g * part : (g + 1) * part] = result[:, g * width : (g + 1) * width]

    cells = plan.channels * half
    columns = []
    for e in range(2):
        for h in range(2):
            cols = third[0, h * (half // 2) : (h + 1) * (half // 2)]
            columns.append(
                jnp.concatenate(
                    [
                        field[:, e, h * half : (h + 1) * half].reshape(cells, plan.cz),
                        cols.astype(F32).reshape(half // 2 * CP, plan.cz).astype(BF16),
                    ],
                    axis=0,
                )
            )
    local = dot(lift[...], jnp.concatenate(columns, axis=1))
    spectral = dot(lanes[...], inverse[...]).reshape(plan.channels, plan.cy, 2 * plan.cz)
    for e in range(2):
        for h in range(2):
            index = e * 2 + h
            total = local[:, index * plan.cz : (index + 1) * plan.cz].reshape(
                plan.channels, half, plan.cz
            ) + spectral[:, h * half : (h + 1) * half, e * plan.cz : (e + 1) * plan.cz]
            out[:, e, h * half : (h + 1) * half] = gelu(total).astype(BF16)


def aligned(rows):
    return rows % 16 == 0


def on_device(features, spectral_weight, conv_weight, point_weight):
    devices_x = lax.axis_size("gx")
    devices_y = lax.axis_size("gy")
    plan = Plan(features.shape, spectral_weight.shape, devices_x, devices_y)
    channels, cx, cy, cz = features.shape
    shape = jax.ShapeDtypeStruct
    cg = plan.cg

    z_spec = call(
        functools.partial(z_body, plan),
        shape((devices_y, cg, cy, LANES), BF16),
        (features, plan.forward_z(), plan.regroup(plan.groups, devices_y)),
    )
    lines = lax.all_to_all(z_spec, "gy", 0, 0, tiled=True)

    rows_table, pair_table = pool_tables(plan)
    coarse = call(
        functools.partial(pool_body, plan),
        shape((cx // 2, cy // 4, CP, cz), BF16),
        (features, rows_table, pair_table),
    )
    up_y = [(i, i + 1) for i in range(devices_y - 1)]
    down_y = [(t, s) for s, t in up_y]
    y_low = lax.ppermute(coarse[:, -2:], "gy", up_y)
    y_high = lax.ppermute(coarse[:, :2], "gy", down_y)
    up_x = [(i, i + 1) for i in range(devices_x - 1)]
    down_x = [(t, s) for s, t in up_x]
    x_low = lax.ppermute(
        jnp.concatenate([y_low[-3:], coarse[-3:], y_high[-3:]], axis=1), "gx", up_x
    )
    x_high = lax.ppermute(
        jnp.concatenate([y_low[:3], coarse[:3], y_high[:3]], axis=1), "gx", down_x
    )
    here_x = lax.axis_index("gx")
    here_y = lax.axis_index("gy")
    flags = jnp.stack(
        [here_x > 0, here_x < devices_x - 1, here_y > 0, here_y < devices_y - 1]
    ).astype(F32)

    filters = jnp.pad(
        conv_weight.reshape(3, 3, 9, channels, channels),
        ((0, 0), (0, 0), (0, 0), (0, CP - channels), (0, CP - channels)),
    )
    filters = jnp.transpose(filters, (0, 1, 3, 2, 4)).reshape(3, 3 * CP, 9 * CP)
    half = cy // 2
    pick_o = const(np.kron(np.eye(channels), np.ones((half, 1))))
    pick_i = const(np.kron(np.eye(channels), np.ones((1, half))))
    diag = const(np.kron(np.ones((channels, channels)), np.eye(half)))
    fixed = const(
        np.einsum(
            "oO,yY->oyYO", np.eye(CP)[:channels], np.kron(np.eye(half // 2), np.ones((2, 1)))
        ).reshape(channels * half, half // 2 * CP)
    )
    spread = const(np.kron(np.eye(cz), np.ones((1, 2))))
    third, lift = call(
        functools.partial(conv_body, plan),
        (
            shape((cx // 2, cy // 2, CP, cz), BF16),
            shape((channels * half, channels * half + half // 2 * CP), BF16),
        ),
        (
            flags, coarse, y_low, y_high, x_low, x_high, filters, jnp.transpose(point_weight),
            spread, pick_o, pick_i, diag, fixed,
        ),
        scratch=[
            pltpu.VMEM((cx // 2 + 6, cy // 4 + 4, CP, LANES), F32),
            pltpu.VMEM((cx // 2 + 6, 3 * CP, (cy // 4 + 2) * LANES), F32),
        ],
        specs=[SMEM] + [VMEM] * 12,
        vmem=16,
        flops=6e9,
        moved=6e6,
    )

    split = aligned(plan.ky)
    y_out = (devices_x, cg, plan.ky) if split else (1, cg, plan.my)
    y_spec = call(
        functools.partial(y_body, plan),
        shape(y_out + (LANES,), BF16),
        (lines, plan.forward_y(), plan.swap(1.0)),
    )
    if not split:
        y_spec = jnp.transpose(y_spec.reshape(cg, devices_x, plan.ky, LANES), (1, 0, 2, 3))
    pencil = lax.all_to_all(y_spec, "gx", 0, 0, tiled=True)

    if split:
        back = call(
            functools.partial(x_body, plan),
            shape((devices_x, cg, plan.ky, LANES), BF16),
            (pencil, plan.forward_x(), spectral_weight, plan.inverse_x()),
            scratch=[
                pltpu.VMEM((2, plan.kz, channels, plan.ky, plan.kx), F32),
                pltpu.VMEM((plan.kz, channels, plan.ky, 2 * plan.kx), F32),
            ],
            vmem=26,
        )
    else:
        back = x_stage_general(plan, pencil, spectral_weight)
    back = lax.all_to_all(back, "gx", 0, 0, tiled=True)
    if not split:
        back = jnp.transpose(back, (1, 0, 2, 3)).reshape(1, cg, plan.my, LANES)
    y_cells = call(
        functools.partial(y_body, plan),
        shape((devices_y, cg, cy, LANES), BF16),
        (back, plan.inverse_y(), plan.swap(-1.0)),
    )
    y_cells = lax.all_to_all(y_cells, "gy", 0, 0, tiled=True)

    full = lambda array: pl.BlockSpec(array.shape, lambda s: (0,) * array.ndim)
    regroup = plan.regroup(devices_y, plan.groups)
    return call(
        functools.partial(final_body, plan),
        shape(features.shape, BF16),
        (features, third, y_cells, lift, regroup, plan.inverse_z()),
        grid=(cx // 2,),
        specs=[
            pl.BlockSpec((channels, 2, cy, cz), lambda s: (0, s, 0, 0)),
            pl.BlockSpec((1, cy // 2, CP, cz), lambda s: (s, 0, 0, 0)),
            full(y_cells),
            full(lift),
            full(regroup),
            pl.BlockSpec((devices_y * plan.unit, 2 * cz), lambda s: (0, s)),
        ],
        out_specs=pl.BlockSpec((channels, 2, cy, cz), lambda s: (0, s, 0, 0)),
        scratch=[pltpu.VMEM((channels * cy, devices_y * plan.unit), BF16)],
        vmem=12,
    )


def solution(mesh):
    in_specs = (P(None, ("grp", "gx"), "gy", None), P(None, None, None, "gy", "gx", None), P(), P())
    out_specs = P(None, ("grp", "gx"), "gy", None)
    return jax.shard_map(
        on_device, mesh=mesh, in_specs=in_specs, out_specs=out_specs, check_vma=False
    )
```

```python
import functools
import math

import jax
import jax.numpy as jnp
import numpy as np
from jax import lax
from jax.experimental import pallas as pl
from jax.experimental.pallas import tpu as pltpu
from jax.sharding import PartitionSpec as P

LANES = 128
CP = 24
BF16 = jnp.bfloat16
F32 = jnp.float32
MIB = 1024 * 1024


def dot(left, right):
    return jnp.dot(left, right, preferred_element_type=F32)


def signed_modes(count):
    position = np.arange(count)
    return np.where(position < count // 2, position, position - count)


def phase(frequency, length):
    index = np.mod(frequency[:, None] * np.arange(length)[None, :], length)
    angle = index.astype(np.float32) * np.float32(2.0 * math.pi / length)
    return (
        np.cos(angle).astype(BF16).astype(np.float32),
        np.sin(angle).astype(BF16).astype(np.float32),
    )


def const(array):
    return np.asarray(array, np.float32).astype(BF16)


class Plan:
    def __init__(self, features, spectral_weight, devices_x, devices_y):
        self.channels, self.cx, self.cy, self.cz = features
        self.dx, self.dy = devices_x, devices_y
        self.kz, self.ky, self.kx = spectral_weight[3:]
        self.gx, self.gy = self.cx * self.dx, self.cy * self.dy
        self.my = self.ky * self.dx
        self.mz = self.kz * self.dy
        self.unit = 2 * self.kz * self.cx
        self.groups = LANES // self.unit
        self.cg = self.channels // self.groups

    def forward_z(self):
        cos, sin = phase(np.arange(self.mz), self.cz)
        table = np.stack([cos, -sin], 0).reshape(2, self.dy, self.kz, self.cz)
        out = np.einsum("pdkz,xw->xzdpkw", table, np.eye(self.cx))
        return const(out.reshape(self.cx * self.cz, self.dy * self.unit))

    def inverse_z(self):
        cos, sin = phase(np.arange(self.mz), self.cz)
        scale = np.where(np.arange(self.mz) == 0, 1.0, 2.0) / float(self.gx * self.gy * self.cz)
        table = np.stack([cos, -sin], 0) * scale[None, :, None]
        table = table.reshape(2, self.dy, self.kz, self.cz)
        out = np.einsum("pdkz,xw->dpkxwz", table, np.eye(self.cx))
        return const(out.reshape(self.dy * self.unit, self.cx * self.cz))

    def regroup(self, outer, inner):
        out = np.einsum("ac,bd,lm->abldcm", np.eye(outer), np.eye(inner), np.eye(self.unit))
        size = outer * inner * self.unit
        return const(out.reshape(size, size))

    def swap(self, sign):
        turn = np.array([[0.0, -sign], [sign, 0.0]])
        half = self.unit // 2
        return const(np.kron(np.eye(self.groups), np.kron(turn, np.eye(half))))

    def forward_y(self):
        cos, sin = phase(signed_modes(self.my), self.gy)
        return const(np.concatenate([cos, sin], 1))

    def inverse_y(self):
        cos, sin = phase(signed_modes(self.my), self.gy)
        return const(np.concatenate([cos.T, sin.T], 1))

    def forward_x(self):
        cos, sin = phase(signed_modes(self.kx), self.gx)
        turn = np.stack([np.stack([cos, -sin]), np.stack([sin, cos])])
        turn = turn.reshape(2, 2, self.kx, self.dx, self.cx)
        out = np.einsum("pqjsx,gh,kl->sgpkxhqlj", turn, np.eye(self.groups), np.eye(self.kz))
        return const(out.reshape(self.dx * LANES, self.groups * self.kz * 2 * self.kx))

    def inverse_x(self):
        cos, sin = phase(signed_modes(self.kx), self.gx)
        turn = np.stack([np.stack([cos, sin]), np.stack([-sin, cos])])
        turn = turn.reshape(2, 2, self.kx, self.dx, self.cx)
        out = np.einsum("pqjsx,gh,kl->gpkjshqlx", turn, np.eye(self.groups), np.eye(self.kz))
        return const(out.reshape(self.groups * self.kz * 2 * self.kx, self.dx * LANES))


VMEM = pl.BlockSpec(memory_space=pltpu.VMEM)
PLAIN = pl.BlockSpec(memory_space=pltpu.VMEM)
FAR = pl.BlockSpec(memory_space=pltpu.VMEM)


ANY = pl.BlockSpec(memory_space=pl.ANY)
HBM = pl.BlockSpec(memory_space=pltpu.HBM)


def pinned(value, spec):
    if spec is HBM or spec is FAR:
        return pltpu.with_memory_space_constraint(jnp.asarray(value), pltpu.HBM)
    if spec is ANY or spec is PLAIN or isinstance(value, np.ndarray):
        return value
    return pltpu.with_memory_space_constraint(value, pltpu.VMEM)


def call(
    body, outs, inputs, scratch=(), specs=None, out_specs=None, vmem=8, flops=1e9, moved=1e6,
    pin=True, **kw,
):
    single = not isinstance(outs, (tuple, list))
    outs = [outs] if single else list(outs)
    specs = specs or [VMEM] * len(inputs)
    out_specs = out_specs or [VMEM] * len(outs)
    if pin:
        inputs = [pinned(value, spec) for value, spec in zip(inputs, specs)]
        outs = [
            pltpu.VMEM(o.shape, o.dtype)
            if spec is VMEM
            else pltpu.HBM(o.shape, o.dtype) if spec is FAR else o
            for o, spec in zip(outs, out_specs)
        ]
    result = pl.pallas_call(
        body,
        out_shape=outs,
        in_specs=specs,
        out_specs=out_specs,
        scratch_shapes=scratch,
        compiler_params=pltpu.CompilerParams(vmem_limit_bytes=vmem * MIB),
        cost_estimate=pl.CostEstimate(
            flops=int(flops), bytes_accessed=int(moved), transcendentals=0
        ),
        **kw,
    )(*inputs)
    return result[0] if single else result


def turn(index, shift, count):
    return lax.rem(index + shift + count, count)


def first_body(
    plan, field_in, table_in, regroup_in, rows_in, pair_in, ytable_in, swap_in,
    own, low_message, high_message, *rest,
):
    middle = rest[: plan.dy - 3]
    coarse, ytable, swap, field, table, regroup, rows_table, pair_table, chunks, sems = rest[
        plan.dy - 3 :
    ]
    sources = (field_in, table_in, regroup_in, rows_in, pair_in, ytable_in, swap_in)
    targets = (field, table, regroup, rows_table, pair_table, ytable, swap)
    copies = [
        pltpu.make_async_copy(s, t, sems.at[n]) for n, (s, t) in enumerate(zip(sources, targets))
    ]
    for copy in copies:
        copy.start()
    for copy in copies[:3]:
        copy.wait()
    rows = plan.channels * plan.cy
    lhs = jnp.concatenate(
        [field[:, x].reshape(rows, plan.cz) for x in range(plan.cx)], axis=1
    )
    modes = dot(lhs, table[...]).astype(BF16)
    part = plan.cg * plan.cy
    lanes = jnp.concatenate(
        [modes[g * part : (g + 1) * part] for g in range(plan.groups)], axis=1
    )
    result = dot(lanes, regroup[...]).astype(BF16)
    for d in range(plan.dy):
        chunks[d] = result[:, d * LANES : (d + 1) * LANES]
    for copy in copies[3:]:
        copy.wait()
    pool_body(plan, field, rows_table, pair_table, coarse)
    here = lax.axis_index("gy")
    own[...] = chunks[here]
    low_message[:part] = chunks[turn(here, 1, plan.dy)]
    high_message[:part] = chunks[turn(here, plan.dy - 1, plan.dy)]
    for s, message in enumerate(middle):
        message[...] = chunks[turn(here, s + 2, plan.dy)]
    tiles = plan.cy // 4
    index = 0
    for x in range(plan.cx // 2):
        for j in range(2):
            at = slice(part + index * CP, part + (index + 1) * CP)
            low_message[at] = coarse[x, tiles - 2 + j]
            high_message[at] = coarse[x, j]
            index += 1


def y_transform(plan, line, table, swap):
    columns = []
    for value in line:
        turned = dot(value, swap[...]).astype(BF16)
        columns.append(jnp.concatenate([value, turned], axis=0))
    return dot(table[...], jnp.concatenate(columns, axis=1)).astype(BF16)


def forward_y_body(plan, own, low_message, high_message, *rest):
    middle = rest[: plan.dy - 3]
    coarse, table, swap, out, up, down, volume, line = rest[plan.dy - 3 :]
    part = plan.cg * plan.cy
    here = lax.axis_index("gy")
    line[here] = own[...]
    line[turn(here, -1, plan.dy)] = low_message[:part]
    line[turn(here, 1, plan.dy)] = high_message[:part]
    for s, message in enumerate(middle):
        line[turn(here, -(s + 2), plan.dy)] = message[...]
    values = [
        jnp.concatenate(
            [line[s, c * plan.cy : (c + 1) * plan.cy] for s in range(plan.dy)], axis=0
        )
        for c in range(plan.cg)
    ]
    result = y_transform(plan, values, table, swap)
    targets, _, rows_out, _ = out.shape
    for d in range(targets):
        for c in range(plan.cg):
            out[d, c] = result[
                d * rows_out : (d + 1) * rows_out, c * LANES : (c + 1) * LANES
            ]
    nx = plan.cx // 2
    tiles = plan.cy // 4
    for x in range(nx):
        planes = [volume.at[x]]
        if x < 3:
            planes.append(down.at[x])
        if x >= nx - 3:
            planes.append(up.at[x - nx + 3])
        for j in range(2):
            at = slice(part + (x * 2 + j) * CP, part + (x * 2 + j + 1) * CP)
            low = jnp.where(here > 0, low_message[at], jnp.zeros((CP, LANES), BF16))
            high = jnp.where(here < plan.dy - 1, high_message[at], jnp.zeros((CP, LANES), BF16))
            for plane in planes:
                plane[j] = low
                plane[2 + tiles + j] = high
        for j in range(tiles):
            for plane in planes:
                plane[2 + j] = coarse[x, j]


def inverse_y_body(plan, line, table_in, swap_in, own, *rest):
    messages = rest[: plan.dy - 1]
    table, swap, chunks, sems = rest[plan.dy - 1 :]
    copies = [
        pltpu.make_async_copy(swap_in, swap, sems.at[0]),
        pltpu.make_async_copy(table_in, table, sems.at[1]),
    ]
    for copy in copies:
        copy.start()
    for copy in copies:
        copy.wait()
    sources = line.shape[0]
    values = [
        jnp.concatenate([line[s, c] for s in range(sources)], axis=0) for c in range(plan.cg)
    ]
    result = y_transform(plan, values, table, swap)
    for d in range(plan.dy):
        for c in range(plan.cg):
            chunks[d, c * plan.cy : (c + 1) * plan.cy] = result[
                d * plan.cy : (d + 1) * plan.cy, c * LANES : (c + 1) * LANES
            ]
    here = lax.axis_index("gy")
    own[...] = chunks[here]
    for s, message in enumerate(messages):
        message[...] = chunks[turn(here, s + 1, plan.dy)]


def mix(plan, spec, weight, mixed):
    def step(o, carry):
        for k in range(plan.kz):
            real = jnp.zeros((plan.ky, plan.kx), F32)
            imag = jnp.zeros((plan.ky, plan.kx), F32)
            for i in range(plan.channels):
                wr = weight[0, i, o, k]
                wi = weight[1, i, o, k]
                xr = spec[0, k, i]
                xi = spec[1, k, i]
                real += xr * wr - xi * wi
                imag += xr * wi + xi * wr
            mixed[k, o] = jnp.concatenate([real, imag], axis=1)
        return carry

    lax.fori_loop(0, plan.channels, step, 0)


def window_body(
    plan, steps, after, volume_in, filters, point, weight, packed, partial, lift, held, held_sems,
):
    c = plan.channels
    loads = [
        pltpu.make_async_copy(
            weight.at[:, :, pl.ds(n * steps, steps)],
            held.at[:, :, pl.ds(n * steps, steps)],
            held_sems.at[n],
        )
        for n in range(c // steps)
    ]
    for load in loads:
        load.start()
    conv_own_body(plan, volume_in, filters, point, partial, lift)
    for n, load in enumerate(loads):
        load.wait()
        for o in range(n * steps, (n + 1) * steps):
            for p in range(2):
                for i in range(c):
                    packed[o, p, i] = jnp.concatenate(
                        [held[p, i, o, k] for k in range(plan.kz)], axis=1
                    ).astype(BF16)


def x_body(
    plan, pencil, forward_in, packed_in, inverse_in, out, forward, packed, inverse, sems, spec, mixed
):
    halves = 2
    block = plan.channels // halves
    copies = [pltpu.make_async_copy(forward_in, forward, sems.at[0])]
    for n in range(halves):
        at = pl.ds(n * block, block)
        copies.append(pltpu.make_async_copy(packed_in.at[at], packed.at[at], sems.at[n + 1]))
    copies.append(pltpu.make_async_copy(inverse_in, inverse, sems.at[halves + 1]))
    for copy in copies:
        copy.start()
    copies[0].wait()
    rows = plan.cg * plan.ky
    wide = plan.kz * plan.kx
    lhs = jnp.concatenate([pencil[s].reshape(rows, LANES) for s in range(plan.dx)], axis=1)
    spectrum = dot(lhs, forward[...])
    for g in range(plan.groups):
        for p in range(2):
            start = (g * 2 + p) * wide
            modes = spectrum[:, start : start + wide].reshape(plan.cg, plan.ky, wide)
            spec[p, g * plan.cg : (g + 1) * plan.cg] = modes

    def step(o, carry):
        real = jnp.zeros((plan.ky, wide), F32)
        imag = jnp.zeros((plan.ky, wide), F32)
        for i in range(plan.channels):
            wr = packed[o, 0, i].astype(F32)
            wi = packed[o, 1, i].astype(F32)
            xr = spec[0, i]
            xi = spec[1, i]
            real += xr * wr - xi * wi
            imag += xr * wi + xi * wr
        mixed[0, o] = real
        mixed[1, o] = imag
        return carry

    for n in range(halves):
        copies[n + 1].wait()
        lax.fori_loop(n * block, (n + 1) * block, step, 0)
    copies[-1].wait()
    back = jnp.concatenate(
        [
            mixed[p, g * plan.cg : (g + 1) * plan.cg].reshape(rows, wide).astype(BF16)
            for g in range(plan.groups)
            for p in range(2)
        ],
        axis=1,
    )
    result = dot(back, inverse[...]).astype(BF16)
    for d in range(plan.dx):
        out[d] = result[:, d * LANES : (d + 1) * LANES].reshape(plan.cg, plan.ky, LANES)


def x_stage_general(plan, pencil, weight):
    groups, cg, ky, kz, kx = plan.groups, plan.cg, plan.ky, plan.kz, plan.kx
    lhs = jnp.transpose(pencil, (1, 2, 0, 3)).reshape(cg * ky, plan.dx * LANES)
    spectrum = dot(lhs, plan.forward_x()).reshape(cg, ky, groups, 2, kz, kx)
    spectrum = jnp.transpose(spectrum, (3, 4, 2, 0, 1, 5)).reshape(2, kz, groups * cg, ky, kx)
    mixed = call(
        functools.partial(mix, plan),
        jax.ShapeDtypeStruct((kz, groups * cg, ky, 2 * kx), F32),
        (spectrum, weight),
        vmem=32,
        pin=False,
    )
    back = jnp.transpose(mixed.reshape(kz, groups, cg, ky, 2, kx), (2, 3, 1, 4, 0, 5))
    back = back.reshape(cg * ky, groups * kz * 2 * kx).astype(BF16)
    back = dot(back, plan.inverse_x()).astype(BF16).reshape(cg, ky, plan.dx, LANES)
    return jnp.transpose(back, (2, 0, 1, 3))


def gelu(value):
    return 0.5 * value * (1.0 + lax.erf(value * (0.5**0.5)))


def pool_tables(plan):
    half = plan.cy // 2
    quarter = half // 2
    rows = np.einsum(
        "cC,yY->ycCY", np.eye(CP)[:, : plan.channels], np.kron(np.eye(quarter), np.ones((1, 2)))
    ).reshape(quarter * CP, plan.channels * half)
    rows = np.concatenate([rows, rows], 1)
    pairs = np.kron(np.eye(plan.cz), np.full((2, 1), 0.125))
    return const(rows), const(pairs)


def pool_body(plan, field, rows_table, pair_table, out):
    half = plan.cy // 2
    quarter = half // 2
    cells = plan.channels * half
    for h in range(2):
        columns = []
        for x in range(plan.cx // 2):
            columns.append(
                jnp.concatenate(
                    [
                        field[:, 2 * x + e, h * half : (h + 1) * half].reshape(cells, plan.cz)
                        for e in range(2)
                    ],
                    axis=0,
                )
            )
        summed = dot(rows_table[...], jnp.concatenate(columns, axis=1))
        blocks = []
        for x in range(plan.cx // 2):
            for j in range(quarter // 2):
                blocks.append(
                    jnp.concatenate(
                        [
                            summed[
                                (2 * j + e) * CP : (2 * j + e + 1) * CP,
                                x * plan.cz : (x + 1) * plan.cz,
                            ]
                            for e in range(2)
                        ],
                        axis=1,
                    )
                )
        block = jnp.concatenate(blocks, axis=0)
        high = block.astype(BF16)
        low = (block - high.astype(F32)).astype(BF16)
        result = dot(high, pair_table[...]) + dot(low, pair_table[...])
        index = 0
        for x in range(plan.cx // 2):
            for j in range(quarter // 2):
                out[x, h * (quarter // 2) + j] = result[index * CP : (index + 1) * CP].astype(BF16)
                index += 1


def tap_columns(volume, x, tiles):
    lane = lax.broadcasted_iota(jnp.int32, (CP, LANES), 1)
    z = lane % (LANES // 2)
    lower = lane < LANES // 2
    shifted = {}
    for j in range(tiles[0] - 1, tiles[1] + 1):
        value = volume[x, j].astype(F32)
        versions = (
            jnp.where(z == 0, 0.0, pltpu.roll(value, 1, 1)),
            value,
            jnp.where(z == LANES // 2 - 1, 0.0, pltpu.roll(value, LANES - 1, 1)),
        )
        shifted[j] = (versions, [pltpu.roll(v, LANES // 2, 1) for v in versions])
    columns = []
    for j in range(tiles[0], tiles[1]):
        pieces = []
        for e in range(3):
            pieces.append(jnp.where(lower, shifted[j - 1][1][e], shifted[j][1][e]))
        for e in range(3):
            pieces.append(shifted[j][0][e])
        for e in range(3):
            pieces.append(jnp.where(lower, shifted[j][1][e], shifted[j + 1][1][e]))
        columns.append(jnp.concatenate(pieces, axis=0).astype(BF16))
    return jnp.concatenate(columns, axis=1)


def combined(partial, x, cols):
    return (
        partial[x, 0:CP, cols]
        + partial[x + 1, CP : 2 * CP, cols]
        + partial[x + 2, 2 * CP : 3 * CP, cols]
    )


def activate(plan, planes, tiles, partial, volume):
    nx = plan.cx // 2
    ny = plan.cy // 4
    here_x = lax.axis_index("gx")
    here_y = lax.axis_index("gy")
    one = jnp.float32(1.0)
    zero = jnp.float32(0.0)
    below_x = jnp.where(here_x > 0, one, zero)
    above_x = jnp.where(here_x < plan.dx - 1, one, zero)
    below_y = jnp.where(here_y > 0, one, zero)
    above_y = jnp.where(here_y < plan.dy - 1, one, zero)
    margin = (planes - nx) // 2

    def body(x, carry):
        inside = jnp.where(x < margin, below_x, one) * jnp.where(x >= margin + nx, above_x, one)
        for j in range(tiles[0], tiles[1]):
            cols = slice((j - tiles[0]) * LANES, (j - tiles[0] + 1) * LANES)
            scale = inside
            if j < 2:
                scale = scale * below_y
            if j >= 2 + ny:
                scale = scale * above_y
            value = gelu(combined(partial, x, cols)) * scale
            volume[x, j] = value.astype(volume.dtype)
        return carry

    lax.fori_loop(0, planes, body, 0)


def where_bf16(mask):
    return jnp.where(mask, 1.0, 0.0).astype(BF16)


def iota(shape, dim):
    return lax.broadcasted_iota(jnp.int32, shape, dim)


def make_lift(plan, point, lift):
    half = plan.cy // 2
    cells = plan.channels * half
    tall = (cells, plan.channels)
    flat = (plan.channels, cells)
    square = (cells, cells)
    pick_o = where_bf16(iota(tall, 0) // half == iota(tall, 1))
    pick_i = where_bf16(iota(flat, 1) // half == iota(flat, 0))
    expanded = dot(dot(pick_o, point[...]).astype(BF16), pick_i)
    diagonal = iota(square, 0) % half == iota(square, 1) % half
    lift[:, :cells] = jnp.where(diagonal, expanded, 0.0).astype(BF16)
    coarse = (cells, half // 2 * CP)
    row, col = iota(coarse, 0), iota(coarse, 1)
    lift[:, cells:] = where_bf16(
        (row // half == col % CP) & ((row % half) // 2 == col // CP)
    )


def conv_own_body(plan, volume_in, filters, point, partial, lift):
    nx = plan.cx // 2
    ny = plan.cy // 4
    make_lift(plan, point, lift)

    def body(x, carry):
        partial[x] = dot(filters[0], tap_columns(volume_in, x, (1, ny + 3)))
        return carry

    lax.fori_loop(0, nx, body, 0)


def conv_middle_body(plan, after, x_low, x_high, own, filters, second, partial, volume):
    nx = plan.cx // 2
    ny = plan.cy // 4
    wide = ny + 4
    tiles = (1, ny + 3)

    def edges(x, carry):
        partial[x] = dot(filters[0], tap_columns(x_low, x, tiles))
        partial[x + 3 + nx] = dot(filters[0], tap_columns(x_high, x, tiles))
        return carry

    lax.fori_loop(0, 3, edges, 0)
    for x in range(nx):
        partial[x + 3] = own[x]
    activate(plan, nx + 4, tiles, partial, volume)
    zero = jnp.zeros((CP, LANES), volume.dtype)
    for x in range(nx + 4):
        volume[x, 0] = zero
        volume[x, wide - 1] = zero

    def body(x, carry):
        partial[x] = dot(filters[1], tap_columns(volume, x, tiles))
        return carry

    lax.fori_loop(0, nx + 4, body, 0)
    activate(plan, nx + 2, tiles, partial, second)


def conv_last_body(plan, after, second, filters, third, partial):
    nx = plan.cx // 2
    ny = plan.cy // 4
    tiles = (2, ny + 2)

    def body(x, carry):
        partial[x] = dot(filters[2], tap_columns(second, x, tiles))
        return carry

    lax.fori_loop(0, nx + 2, body, 0)

    square = (LANES, 2 * LANES)
    spread = where_bf16(iota(square, 1) // 2 == iota(square, 0))

    def up(x, carry):
        for j in range(ny):
            total = combined(partial, x, slice(j * LANES, (j + 1) * LANES))
            wide = dot(total.astype(BF16), spread).astype(BF16)
            third[x, 2 * j] = wide[:, : plan.cz]
            third[x, 2 * j + 1] = wide[:, plan.cz :]
        return carry

    lax.fori_loop(0, nx, up, 0)


def final_body(plan, field, third, lift, regroup, inverse, own, *rest):
    messages = rest[: plan.dy - 1]
    out, line, lanes = rest[plan.dy - 1 :]
    step = pl.program_id(0)
    half = plan.cy // 2
    part = plan.cg * plan.cy

    @pl.when(step == 0)
    def _():
        here = lax.axis_index("gy")
        line[here] = own[...]
        for s, message in enumerate(messages):
            line[turn(here, -(s + 1), plan.dy)] = message[...]
        gathered = jnp.concatenate([line[s] for s in range(plan.dy)], axis=1)
        result = dot(gathered, regroup[...]).astype(BF16)
        width = plan.dy * plan.unit
        for g in range(plan.groups):
            lanes[g * part : (g + 1) * part] = result[:, g * width : (g + 1) * width]

    cells = plan.channels * half
    columns = []
    for e in range(2):
        for h in range(2):
            cols = third[0, h * (half // 2) : (h + 1) * (half // 2)]
            columns.append(
                jnp.concatenate(
                    [
                        field[:, e, h * half : (h + 1) * half].reshape(cells, plan.cz),
                        cols.astype(F32).reshape(half // 2 * CP, plan.cz).astype(BF16),
                    ],
                    axis=0,
                )
            )
    local = dot(lift[...], jnp.concatenate(columns, axis=1))
    spectral = dot(lanes[...], inverse[...]).reshape(plan.channels, plan.cy, 2 * plan.cz)
    for e in range(2):
        for h in range(2):
            index = e * 2 + h
            total = local[:, index * plan.cz : (index + 1) * plan.cz].reshape(
                plan.channels, half, plan.cz
            ) + spectral[:, h * half : (h + 1) * half, e * plan.cz : (e + 1) * plan.cz]
            out[:, e, h * half : (h + 1) * half] = gelu(total).astype(BF16)


def after(values, marker):
    return lax.optimization_barrier((values, marker))[0]


def ring(value, axis, shift):
    count = lax.axis_size(axis)
    return lax.ppermute(value, axis, [(i, (i + shift) % count) for i in range(count)])


def on_device(features, spectral_weight, conv_weight, point_weight):
    devices_x = lax.axis_size("gx")
    devices_y = lax.axis_size("gy")
    plan = Plan(features.shape, spectral_weight.shape, devices_x, devices_y)
    channels, cx, cy, cz = features.shape
    shape = jax.ShapeDtypeStruct
    cg = plan.cg
    nx, ny = cx // 2, cy // 4
    part = cg * cy
    split = plan.ky % 16 == 0 and plan.kz * plan.kx == LANES
    half = cy // 2

    rows_table, pair_table = pool_tables(plan)
    tables = (
        plan.forward_z(), plan.regroup(plan.groups, devices_y), rows_table, pair_table,
        plan.forward_y(), plan.swap(1.0),
    )
    chunk = shape((part, LANES), BF16)
    message = shape((part + nx * 2 * CP, LANES), BF16)
    outs = [chunk, message, message] + [chunk] * (devices_y - 3)
    outs += [shape((nx, ny, CP, cz), BF16)] + [shape(t.shape, BF16) for t in tables[4:]]
    first = call(
        functools.partial(first_body, plan),
        outs,
        (features,) + tables,
        scratch=[pltpu.VMEM(features.shape, BF16)]
        + [pltpu.VMEM(t.shape, BF16) for t in tables[:4]]
        + [pltpu.VMEM((devices_y, part, LANES), BF16), pltpu.SemaphoreType.DMA((7,))],
        specs=[HBM] * 7,
        vmem=16,
    )
    own, to_up, to_down = first[:3]
    middle = first[3:-3]
    coarse, y_table, y_swap = first[-3:]
    low_message = ring(to_up, "gy", 1)
    high_message = ring(to_down, "gy", -1)
    middle = [ring(m, "gy", s + 2) for s, m in enumerate(middle)]

    y_out = (devices_x, cg, plan.ky) if split else (1, cg, plan.my)
    planes = shape((3, ny + 4, CP, LANES), BF16)
    y_spec, up, down, volume = call(
        functools.partial(forward_y_body, plan),
        (shape(y_out + (LANES,), BF16), planes, planes, shape((nx, ny + 4, CP, LANES), BF16)),
        (own, low_message, high_message, *middle, coarse, y_table, y_swap),
        out_specs=[PLAIN, FAR, FAR, VMEM],
        scratch=[pltpu.VMEM((devices_y, part, LANES), BF16)],
    )
    if not split:
        y_spec = jnp.transpose(y_spec.reshape(cg, devices_x, plan.ky, LANES), (1, 0, 2, 3))
    pencil = lax.all_to_all(y_spec, "gx", 0, 0, tiled=True)

    filters = jnp.pad(
        conv_weight.reshape(3, 3, 9, channels, channels),
        ((0, 0), (0, 0), (0, 0), (0, CP - channels), (0, CP - channels)),
    )
    filters = jnp.transpose(filters, (0, 1, 3, 2, 4)).reshape(3, 3 * CP, 9 * CP)
    wide = (ny + 2) * LANES
    small = (
        shape((nx, 3 * CP, wide), F32),
        shape((channels * half, channels * half + half // 2 * CP), BF16),
    )
    local = (volume, filters, jnp.transpose(point_weight))
    if split:
        steps = 2 if channels % 2 == 0 else 1
        forward_x = plan.forward_x()
        inverse_x = plan.inverse_x()
        packed, partial_own, lift = call(
            functools.partial(window_body, plan, steps),
            (shape((channels, 2, channels, plan.ky, LANES), BF16),) + small,
            (y_spec,) + local + (spectral_weight,),
            specs=[ANY] + [VMEM, PLAIN, PLAIN] + [HBM],
            out_specs=[FAR, FAR, FAR],
            scratch=[
                pltpu.VMEM(spectral_weight.shape, F32),
                pltpu.SemaphoreType.DMA((channels // steps,)),
            ],
            vmem=24,
            flops=4e9,
            moved=16e6,
        )
    else:
        partial_own, lift = call(
            functools.partial(conv_own_body, plan),
            small,
            local,
            specs=[VMEM, PLAIN, PLAIN],
            out_specs=[FAR, FAR],
            flops=2e9,
        )
    up, down = after((up, down), lift)
    x_low = lax.ppermute(up, "gx", [(i, i + 1) for i in range(devices_x - 1)])
    x_high = lax.ppermute(down, "gx", [(i + 1, i) for i in range(devices_x - 1)])

    if split:
        back = call(
            functools.partial(x_body, plan),
            shape((devices_x, cg, plan.ky, LANES), BF16),
            (pencil, forward_x, packed, inverse_x),
            specs=[VMEM, HBM, HBM, HBM],
            out_specs=[PLAIN],
            scratch=[
                pltpu.VMEM(forward_x.shape, BF16),
                pltpu.VMEM(packed.shape, BF16),
                pltpu.VMEM(inverse_x.shape, BF16),
                pltpu.SemaphoreType.DMA((4,)),
                pltpu.VMEM((2, channels, plan.ky, LANES), F32),
                pltpu.VMEM((2, channels, plan.ky, LANES), F32),
            ],
            vmem=14,
        )
    else:
        back = x_stage_general(plan, pencil, spectral_weight)
    line = lax.all_to_all(back, "gx", 0, 0, tiled=True)

    second = call(
        functools.partial(conv_middle_body, plan),
        shape((nx + 2, ny + 4, CP, LANES), F32),
        (back, x_low, x_high, partial_own, filters),
        scratch=[
            pltpu.VMEM((nx + 6, 3 * CP, wide), F32),
            pltpu.VMEM((nx + 4, ny + 4, CP, LANES), F32),
        ],
        specs=[ANY, PLAIN, PLAIN, FAR, PLAIN],
        out_specs=[PLAIN],
        vmem=7,
        flops=6e9,
    )
    if not split:
        line = jnp.transpose(line, (1, 0, 2, 3)).reshape(1, cg, plan.my, LANES)
    own, *messages = call(
        functools.partial(inverse_y_body, plan),
        [chunk] * devices_y,
        (line, plan.inverse_y(), plan.swap(-1.0)),
        specs=[VMEM, HBM, HBM],
        scratch=[
            pltpu.VMEM((plan.gy, 2 * plan.my), BF16),
            pltpu.VMEM((LANES, LANES), BF16),
            pltpu.VMEM((devices_y, part, LANES), BF16),
            pltpu.SemaphoreType.DMA((2,)),
        ],
    )
    arrived = [ring(m, "gy", s + 1) for s, m in enumerate(messages)]
    third = call(
        functools.partial(conv_last_body, plan),
        shape((nx, 2 * ny, CP, cz), BF16),
        (own, second, filters),
        scratch=[pltpu.VMEM((nx + 2, 3 * CP, ny * LANES), F32)],
        specs=[ANY, PLAIN, PLAIN],
        out_specs=[PLAIN],
        flops=3e9,
    )

    full = lambda array: pl.BlockSpec(array.shape, lambda s: (0,) * array.ndim)
    regroup = plan.regroup(devices_y, plan.groups)
    inverse_z = plan.inverse_z()
    far = lambda array: pltpu.with_memory_space_constraint(jnp.asarray(array), pltpu.HBM)
    return call(
        functools.partial(final_body, plan),
        shape(features.shape, BF16),
        (far(features), third, far(lift), far(regroup), far(inverse_z), own, *arrived),
        pin=False,
        grid=(nx,),
        specs=[
            pl.BlockSpec((channels, 2, cy, cz), lambda s: (0, s, 0, 0)),
            pl.BlockSpec((1, cy // 2, CP, cz), lambda s: (s, 0, 0, 0)),
            full(lift),
            full(regroup),
            pl.BlockSpec((devices_y * plan.unit, 2 * cz), lambda s: (0, s)),
        ]
        + [full(own)] * devices_y,
        out_specs=[pl.BlockSpec((channels, 2, cy, cz), lambda s: (0, s, 0, 0))],
        scratch=[
            pltpu.VMEM((devices_y, part, LANES), BF16),
            pltpu.VMEM((channels * cy, devices_y * plan.unit), BF16),
        ],
        vmem=12,
    )


def solution(mesh):
    in_specs = (P(None, ("grp", "gx"), "gy", None), P(None, None, None, "gy", "gx", None), P(), P())
    out_specs = P(None, ("grp", "gx"), "gy", None)
    return jax.shard_map(
        on_device, mesh=mesh, in_specs=in_specs, out_specs=out_specs, check_vma=False
    )
```

```python
import functools
import math

import jax
import jax.numpy as jnp
import numpy as np
from jax import lax
from jax.experimental import pallas as pl
from jax.experimental.pallas import tpu as pltpu
from jax.sharding import PartitionSpec as P

LANES = 128
CP = 24
BF16 = jnp.bfloat16
F32 = jnp.float32
MIB = 1024 * 1024


def dot(left, right):
    return jnp.dot(left, right, preferred_element_type=F32)


def signed_modes(count):
    position = np.arange(count)
    return np.where(position < count // 2, position, position - count)


def phase(frequency, length):
    index = np.mod(frequency[:, None] * np.arange(length)[None, :], length)
    angle = index.astype(np.float32) * np.float32(2.0 * math.pi / length)
    return (
        np.cos(angle).astype(BF16).astype(np.float32),
        np.sin(angle).astype(BF16).astype(np.float32),
    )


def const(array):
    return np.asarray(array, np.float32).astype(BF16)


class Plan:
    def __init__(self, features, spectral_weight, devices_x, devices_y):
        self.channels, self.cx, self.cy, self.cz = features
        self.dx, self.dy = devices_x, devices_y
        self.kz, self.ky, self.kx = spectral_weight[3:]
        self.gx, self.gy = self.cx * self.dx, self.cy * self.dy
        self.my = self.ky * self.dx
        self.mz = self.kz * self.dy
        self.unit = 2 * self.kz * self.cx
        self.groups = LANES // self.unit
        self.cg = self.channels // self.groups

    def forward_z(self):
        cos, sin = phase(np.arange(self.mz), self.cz)
        table = np.stack([cos, -sin], 0).reshape(2, self.dy, self.kz, self.cz)
        out = np.einsum("pdkz,xw->xzdpkw", table, np.eye(self.cx))
        return const(out.reshape(self.cx * self.cz, self.dy * self.unit))

    def inverse_z(self):
        cos, sin = phase(np.arange(self.mz), self.cz)
        scale = np.where(np.arange(self.mz) == 0, 1.0, 2.0) / float(self.gx * self.gy * self.cz)
        table = np.stack([cos, -sin], 0) * scale[None, :, None]
        table = table.reshape(2, self.dy, self.kz, self.cz)
        out = np.einsum("pdkz,xw->dpkxwz", table, np.eye(self.cx))
        return const(out.reshape(self.dy * self.unit, self.cx * self.cz))

    def regroup(self, outer, inner):
        out = np.einsum("ac,bd,lm->abldcm", np.eye(outer), np.eye(inner), np.eye(self.unit))
        size = outer * inner * self.unit
        return const(out.reshape(size, size))

    def swap(self, sign):
        turn = np.array([[0.0, -sign], [sign, 0.0]])
        half = self.unit // 2
        return const(np.kron(np.eye(self.groups), np.kron(turn, np.eye(half))))

    def forward_y(self):
        cos, sin = phase(signed_modes(self.my), self.gy)
        return const(np.concatenate([cos, sin], 1))

    def inverse_y(self):
        cos, sin = phase(signed_modes(self.my), self.gy)
        return const(np.concatenate([cos.T, sin.T], 1))

    def turn_x(self, sign):
        cos, sin = phase(signed_modes(self.kx), self.gx)
        turn = np.stack([np.stack([cos, -sign * sin]), np.stack([sign * sin, cos])])
        return turn.reshape(2, 2, self.kx, self.dx, self.cx)

    def forward_x(self):
        out = np.einsum("pqjsx,g,kl->sgpkxqlj", self.turn_x(1.0), np.ones(self.groups), np.eye(self.kz))
        return const(out.reshape(self.dx * LANES, self.kz * 2 * self.kx))

    def inverse_x(self):
        out = np.einsum("pqjsx,h,kl->pkjshqlx", self.turn_x(-1.0), np.ones(self.groups), np.eye(self.kz))
        return const(out.reshape(self.kz * 2 * self.kx, self.dx * LANES))


VMEM = pl.BlockSpec(memory_space=pltpu.VMEM)
PLAIN = pl.BlockSpec(memory_space=pltpu.VMEM)
FAR = pl.BlockSpec(memory_space=pltpu.VMEM)


ANY = pl.BlockSpec(memory_space=pl.ANY)
HBM = pl.BlockSpec(memory_space=pltpu.HBM)


def pinned(value, spec):
    if spec is HBM or spec is FAR:
        return pltpu.with_memory_space_constraint(jnp.asarray(value), pltpu.HBM)
    if spec is ANY or spec is PLAIN or isinstance(value, np.ndarray):
        return value
    return pltpu.with_memory_space_constraint(value, pltpu.VMEM)


def call(
    body, outs, inputs, scratch=(), specs=None, out_specs=None, vmem=8, flops=1e9, moved=1e6,
    pin=True, **kw,
):
    single = not isinstance(outs, (tuple, list))
    outs = [outs] if single else list(outs)
    specs = specs or [VMEM] * len(inputs)
    out_specs = out_specs or [VMEM] * len(outs)
    if pin:
        inputs = [pinned(value, spec) for value, spec in zip(inputs, specs)]
        outs = [
            pltpu.VMEM(o.shape, o.dtype)
            if spec is VMEM
            else pltpu.HBM(o.shape, o.dtype) if spec is FAR else o
            for o, spec in zip(outs, out_specs)
        ]
    result = pl.pallas_call(
        body,
        out_shape=outs,
        in_specs=specs,
        out_specs=out_specs,
        scratch_shapes=scratch,
        compiler_params=pltpu.CompilerParams(vmem_limit_bytes=vmem * MIB),
        cost_estimate=pl.CostEstimate(
            flops=int(flops), bytes_accessed=int(moved), transcendentals=0
        ),
        **kw,
    )(*inputs)
    return result[0] if single else result


def turn(index, shift, count):
    return lax.rem(index + shift + count, count)


def first_body(
    plan, field_in, table_in, regroup_in, rows_in, pair_in, ytable_in, swap_in, *rest
):
    weight = held = None
    if len(rest) > plan.dy + 11:
        weight, *rest, held, held_sems = rest
        packed = rest.pop(plan.dy + 3)
    own, low_message, high_message, *rest = rest
    middle = rest[: plan.dy - 3]
    coarse, ytable, swap, field, table, regroup, rows_table, pair_table, chunks, sems = rest[
        plan.dy - 3 :
    ]
    sources = (field_in, table_in, regroup_in, rows_in, pair_in, ytable_in, swap_in)
    targets = (field, table, regroup, rows_table, pair_table, ytable, swap)
    copies = [
        pltpu.make_async_copy(s, t, sems.at[n]) for n, (s, t) in enumerate(zip(sources, targets))
    ]
    for copy in copies:
        copy.start()
    if held is not None:
        start_weights(weight, held, held_sems, 0)
    for copy in copies[:3]:
        copy.wait()
    rows = plan.channels * plan.cy
    lhs = jnp.concatenate(
        [field[:, x].reshape(rows, plan.cz) for x in range(plan.cx)], axis=1
    )
    modes = dot(lhs, table[...]).astype(BF16)
    part = plan.cg * plan.cy
    lanes = jnp.concatenate(
        [modes[g * part : (g + 1) * part] for g in range(plan.groups)], axis=1
    )
    result = dot(lanes, regroup[...]).astype(BF16)
    for d in range(plan.dy):
        chunks[d] = result[:, d * LANES : (d + 1) * LANES]
    for copy in copies[3:]:
        copy.wait()
    pool_body(plan, field, rows_table, pair_table, coarse)
    here = lax.axis_index("gy")
    own[...] = chunks[here]
    low_message[:part] = chunks[turn(here, 1, plan.dy)]
    high_message[:part] = chunks[turn(here, plan.dy - 1, plan.dy)]
    for s, message in enumerate(middle):
        message[...] = chunks[turn(here, s + 2, plan.dy)]
    tiles = plan.cy // 4
    index = 0
    for x in range(plan.cx // 2):
        for j in range(2):
            at = slice(part + index * CP, part + (index + 1) * CP)
            low_message[at] = coarse[x, tiles - 2 + j]
            high_message[at] = coarse[x, j]
            index += 1
    if held is not None:
        pack_weights(plan, weight, held, held_sems, 0, packed)


def y_transform(plan, line, table, swap):
    columns = []
    for value in line:
        turned = dot(value, swap[...]).astype(BF16)
        columns.append(jnp.concatenate([value, turned], axis=0))
    return dot(table[...], jnp.concatenate(columns, axis=1)).astype(BF16)


def forward_y_body(plan, own, low_message, high_message, *rest):
    middle = rest[: plan.dy - 3]
    coarse, table, swap, out, near, far, volume, line = rest[plan.dy - 3 :]
    part = plan.cg * plan.cy
    here = lax.axis_index("gy")
    line[here] = own[...]
    line[turn(here, -1, plan.dy)] = low_message[:part]
    line[turn(here, 1, plan.dy)] = high_message[:part]
    for s, message in enumerate(middle):
        line[turn(here, -(s + 2), plan.dy)] = message[...]
    values = [
        jnp.concatenate(
            [line[s, c * plan.cy : (c + 1) * plan.cy] for s in range(plan.dy)], axis=0
        )
        for c in range(plan.cg)
    ]
    result = y_transform(plan, values, table, swap)
    targets, _, rows_out, _ = out.shape
    for d in range(targets):
        for c in range(plan.cg):
            out[d, c] = result[
                d * rows_out : (d + 1) * rows_out, c * LANES : (c + 1) * LANES
            ]
    nx = plan.cx // 2
    tiles = plan.cy // 4
    for x in range(nx):
        for j in range(2):
            at = slice(part + (x * 2 + j) * CP, part + (x * 2 + j + 1) * CP)
            none = jnp.zeros((CP, LANES), BF16)
            volume[x, j] = jnp.where(here > 0, low_message[at], none)
            volume[x, 2 + tiles + j] = jnp.where(here < plan.dy - 1, high_message[at], none)
        for j in range(tiles):
            volume[x, 2 + j] = coarse[x, j]
    even = lax.rem(lax.axis_index("gx"), 2) == 0
    first_plane = jnp.where(even, nx - 3, 0)
    last_plane = jnp.where(even, 0, nx - 3)
    for x in range(3):
        near[x] = volume[first_plane + x]
        far[x] = volume[last_plane + x]


def inverse_y_body(plan, line, table, swap, own, *rest):
    messages = rest[: plan.dy - 1]
    chunks = rest[plan.dy - 1]
    sources = line.shape[0]
    values = [
        jnp.concatenate([line[s, c] for s in range(sources)], axis=0) for c in range(plan.cg)
    ]
    result = y_transform(plan, values, table, swap)
    for d in range(plan.dy):
        for c in range(plan.cg):
            chunks[d, c * plan.cy : (c + 1) * plan.cy] = result[
                d * plan.cy : (d + 1) * plan.cy, c * LANES : (c + 1) * LANES
            ]
    here = lax.axis_index("gy")
    own[...] = chunks[here]
    for s, message in enumerate(messages):
        message[...] = chunks[turn(here, s + 1, plan.dy)]


def mix(plan, spec, weight, mixed):
    def step(o, carry):
        for k in range(plan.kz):
            real = jnp.zeros((plan.ky, plan.kx), F32)
            imag = jnp.zeros((plan.ky, plan.kx), F32)
            for i in range(plan.channels):
                wr = weight[0, i, o, k]
                wi = weight[1, i, o, k]
                xr = spec[0, k, i]
                xi = spec[1, k, i]
                real += xr * wr - xi * wi
                imag += xr * wi + xi * wr
            mixed[k, o] = jnp.concatenate([real, imag], axis=1)
        return carry

    lax.fori_loop(0, plan.channels, step, 0)


def weight_copy(weight, held, sems, begin, n):
    return pltpu.make_async_copy(weight.at[:, begin + n], held.at[n], sems.at[n])


def start_weights(weight, held, sems, begin):
    def one(n, carry):
        weight_copy(weight, held, sems, begin, n).start()
        return carry

    lax.fori_loop(0, held.shape[0], one, 0)


def pack_weights(plan, weight, held, sems, begin, packed):
    def one(n, carry):
        weight_copy(weight, held, sems, begin, n).wait()
        for p in range(2):
            for o in range(plan.channels):
                packed[n, p, o] = jnp.concatenate(
                    [held[n, p, o, k] for k in range(plan.kz)], axis=1
                ).astype(BF16)
        return carry

    lax.fori_loop(0, held.shape[0], one, 0)


def window_body(
    plan, begin, after, volume, filters, point, weight, forward_in, inverse_in,
    packed, partial, lift, forward, inverse, held, sems, table_sems,
):
    copies = prefetches((forward_in, inverse_in), (forward, inverse), table_sems)
    for copy in copies:
        copy.start()
    start_weights(weight, held, sems, begin)
    conv_own_body(plan, volume, filters, point, partial, lift)
    pack_weights(plan, weight, held, sems, begin, packed)
    for copy in copies:
        copy.wait()


def lane_group(plan, shape):
    return (lax.broadcasted_iota(jnp.int32, shape, 1) % LANES) // plan.unit


def by_group(plan, lanes):
    owner = lane_group(plan, lanes.shape)
    return jnp.concatenate(
        [jnp.where(owner == g, lanes, jnp.zeros_like(lanes)) for g in range(plan.groups)], axis=0
    )


def one_group(plan, stacked):
    rows = stacked.shape[0] // plan.groups
    owner = lane_group(plan, (rows, stacked.shape[1]))
    result = stacked[:rows]
    for g in range(1, plan.groups):
        result = jnp.where(owner == g, stacked[g * rows : (g + 1) * rows], result)
    return result


def x_body(
    plan, pencil, forward, packed_early, packed_late, inverse, weight, out,
    packed, sems, held, held_sems, spec, mixed,
):
    early = packed_early.shape[0]
    ready = packed.shape[0]
    copies = [
        pltpu.make_async_copy(packed_early, packed.at[pl.ds(0, early)], sems.at[0]),
        pltpu.make_async_copy(packed_late, packed.at[pl.ds(early, ready - early)], sems.at[1]),
    ]
    for copy in copies:
        copy.start()
    start_weights(weight, held, held_sems, ready)
    rows = plan.cg * plan.ky
    wide = plan.kz * plan.kx
    lhs = jnp.concatenate([pencil[s].reshape(rows, LANES) for s in range(plan.dx)], axis=1)
    spectrum = dot(by_group(plan, lhs), forward[...])
    for g in range(plan.groups):
        for p in range(2):
            modes = spectrum[g * rows : (g + 1) * rows, p * wide : (p + 1) * wide]
            spec[p, g * plan.cg : (g + 1) * plan.cg] = modes.reshape(plan.cg, plan.ky, wide)

    def step(o, carry):
        real = jnp.zeros((plan.ky, wide), F32)
        imag = jnp.zeros((plan.ky, wide), F32)
        for i in range(ready):
            wr = packed[i, 0, o].astype(F32)
            wi = packed[i, 1, o].astype(F32)
            xr = spec[0, i]
            xi = spec[1, i]
            real += xr * wr - xi * wi
            imag += xr * wi + xi * wr
        mixed[0, o] = real
        mixed[1, o] = imag
        return carry

    def streamed(n, carry):
        weight_copy(weight, held, held_sems, ready, n).wait()
        xr = spec[0, ready + n]
        xi = spec[1, ready + n]
        for o in range(plan.channels):
            wr, wi = (
                jnp.concatenate([held[n, p, o, k] for k in range(plan.kz)], axis=1)
                for p in range(2)
            )
            mixed[0, o] += xr * wr - xi * wi
            mixed[1, o] += xr * wi + xi * wr
        return carry

    for copy in copies:
        copy.wait()
    lax.fori_loop(0, plan.channels, step, 0, unroll=2)
    lax.fori_loop(0, plan.channels - ready, streamed, 0)
    back = jnp.concatenate(
        [
            jnp.concatenate(
                [
                    mixed[p, g * plan.cg : (g + 1) * plan.cg].reshape(rows, wide).astype(BF16)
                    for p in range(2)
                ],
                axis=1,
            )
            for g in range(plan.groups)
        ],
        axis=0,
    )
    result = one_group(plan, dot(back, inverse[...])).astype(BF16)
    for d in range(plan.dx):
        out[d] = result[:, d * LANES : (d + 1) * LANES].reshape(plan.cg, plan.ky, LANES)


def x_stage_general(plan, pencil, weight):
    groups, cg, ky, kz, kx = plan.groups, plan.cg, plan.ky, plan.kz, plan.kx
    lhs = jnp.transpose(pencil, (1, 2, 0, 3)).reshape(cg * ky, plan.dx * LANES)
    spectrum = dot(by_group(plan, lhs), plan.forward_x()).reshape(groups, cg, ky, 2, kz, kx)
    spectrum = jnp.transpose(spectrum, (3, 4, 0, 1, 2, 5)).reshape(2, kz, groups * cg, ky, kx)
    mixed = call(
        functools.partial(mix, plan),
        jax.ShapeDtypeStruct((kz, groups * cg, ky, 2 * kx), F32),
        (spectrum, weight),
        vmem=32,
        pin=False,
    )
    back = jnp.transpose(mixed.reshape(kz, groups, cg, ky, 2, kx), (1, 2, 3, 4, 0, 5))
    back = back.reshape(groups * cg * ky, kz * 2 * kx).astype(BF16)
    back = one_group(plan, dot(back, plan.inverse_x())).astype(BF16)
    back = back.reshape(cg, ky, plan.dx, LANES)
    return jnp.transpose(back, (2, 0, 1, 3))


def gelu(value):
    return 0.5 * value * (1.0 + lax.erf(value * (0.5**0.5)))


def pool_tables(plan):
    half = plan.cy // 2
    quarter = half // 2
    rows = np.einsum(
        "cC,yY->ycCY", np.eye(CP)[:, : plan.channels], np.kron(np.eye(quarter), np.ones((1, 2)))
    ).reshape(quarter * CP, plan.channels * half)
    rows = np.concatenate([rows, rows], 1)
    pairs = np.kron(np.eye(plan.cz), np.full((2, 1), 0.125))
    return const(rows), const(pairs)


def pool_body(plan, field, rows_table, pair_table, out):
    half = plan.cy // 2
    quarter = half // 2
    cells = plan.channels * half
    for h in range(2):
        columns = []
        for x in range(plan.cx // 2):
            columns.append(
                jnp.concatenate(
                    [
                        field[:, 2 * x + e, h * half : (h + 1) * half].reshape(cells, plan.cz)
                        for e in range(2)
                    ],
                    axis=0,
                )
            )
        summed = dot(rows_table[...], jnp.concatenate(columns, axis=1))
        blocks = []
        for x in range(plan.cx // 2):
            for j in range(quarter // 2):
                blocks.append(
                    jnp.concatenate(
                        [
                            summed[
                                (2 * j + e) * CP : (2 * j + e + 1) * CP,
                                x * plan.cz : (x + 1) * plan.cz,
                            ]
                            for e in range(2)
                        ],
                        axis=1,
                    )
                )
        block = jnp.concatenate(blocks, axis=0)
        high = block.astype(BF16)
        low = (block - high.astype(F32)).astype(BF16)
        result = dot(high, pair_table[...]) + dot(low, pair_table[...])
        index = 0
        for x in range(plan.cx // 2):
            for j in range(quarter // 2):
                out[x, h * (quarter // 2) + j] = result[index * CP : (index + 1) * CP].astype(BF16)
                index += 1


def tap_columns(volume, x, tiles):
    lane = lax.broadcasted_iota(jnp.int32, (CP, LANES), 1)
    z = lane % (LANES // 2)
    lower = lane < LANES // 2
    shifted = {}
    for j in range(tiles[0] - 1, tiles[1] + 1):
        value = volume[x, j].astype(F32)
        versions = (
            jnp.where(z == 0, 0.0, pltpu.roll(value, 1, 1)),
            value,
            jnp.where(z == LANES // 2 - 1, 0.0, pltpu.roll(value, LANES - 1, 1)),
        )
        shifted[j] = (versions, [pltpu.roll(v, LANES // 2, 1) for v in versions])
    columns = []
    for j in range(tiles[0], tiles[1]):
        pieces = []
        for e in range(3):
            pieces.append(jnp.where(lower, shifted[j - 1][1][e], shifted[j][1][e]))
        for e in range(3):
            pieces.append(shifted[j][0][e])
        for e in range(3):
            pieces.append(jnp.where(lower, shifted[j][1][e], shifted[j + 1][1][e]))
        columns.append(jnp.concatenate(pieces, axis=0).astype(BF16))
    return jnp.concatenate(columns, axis=1)


def combined(partial, x, cols):
    return (
        partial[x, 0:CP, cols]
        + partial[x + 1, CP : 2 * CP, cols]
        + partial[x + 2, 2 * CP : 3 * CP, cols]
    )


def activate(plan, planes, tiles, partial, volume):
    nx = plan.cx // 2
    ny = plan.cy // 4
    here_x = lax.axis_index("gx")
    here_y = lax.axis_index("gy")
    one = jnp.float32(1.0)
    zero = jnp.float32(0.0)
    below_x = jnp.where(here_x > 0, one, zero)
    above_x = jnp.where(here_x < plan.dx - 1, one, zero)
    below_y = jnp.where(here_y > 0, one, zero)
    above_y = jnp.where(here_y < plan.dy - 1, one, zero)
    margin = (planes - nx) // 2

    def body(x, carry):
        inside = jnp.where(x < margin, below_x, one) * jnp.where(x >= margin + nx, above_x, one)
        for j in range(tiles[0], tiles[1]):
            cols = slice((j - tiles[0]) * LANES, (j - tiles[0] + 1) * LANES)
            scale = inside
            if j < 2:
                scale = scale * below_y
            if j >= 2 + ny:
                scale = scale * above_y
            value = gelu(combined(partial, x, cols)) * scale
            volume[x, j] = value.astype(volume.dtype)
        return carry

    lax.fori_loop(0, planes, body, 0, unroll=2)


def where_bf16(mask):
    return jnp.where(mask, 1.0, 0.0).astype(BF16)


def iota(shape, dim):
    return lax.broadcasted_iota(jnp.int32, shape, dim)


def make_lift(plan, point, lift):
    half = plan.cy // 2
    cells = plan.channels * half
    tall = (cells, plan.channels)
    flat = (plan.channels, cells)
    square = (cells, cells)
    pick_o = where_bf16(iota(tall, 0) // half == iota(tall, 1))
    pick_i = where_bf16(iota(flat, 1) // half == iota(flat, 0))
    expanded = dot(dot(pick_o, point[...]).astype(BF16), pick_i)
    diagonal = iota(square, 0) % half == iota(square, 1) % half
    lift[:, :cells] = jnp.where(diagonal, expanded, 0.0).astype(BF16)
    coarse = (cells, half // 2 * CP)
    row, col = iota(coarse, 0), iota(coarse, 1)
    lift[:, cells:] = where_bf16(
        (row // half == col % CP) & ((row % half) // 2 == col // CP)
    )


def conv_own_body(plan, volume_in, filters, point, partial, lift):
    nx = plan.cx // 2
    ny = plan.cy // 4
    make_lift(plan, point, lift)

    def body(x, carry):
        partial[x] = dot(filters[0], tap_columns(volume_in, x, (1, ny + 3)))
        return carry

    lax.fori_loop(0, nx, body, 0, unroll=2)


def prefetches(sources, targets, sems):
    return [
        pltpu.make_async_copy(s, t, sems.at[n]) for n, (s, t) in enumerate(zip(sources, targets))
    ]


def conv_middle_body(
    plan, after, near, far, own, filters, table_in, swap_in,
    second, table, swap, partial, volume, sems,
):
    copies = prefetches((table_in, swap_in), (table, swap), sems)
    for copy in copies:
        copy.start()
    nx = plan.cx // 2
    ny = plan.cy // 4
    wide = ny + 4
    tiles = (1, ny + 3)

    even = lax.rem(lax.axis_index("gx"), 2) == 0
    near_at = jnp.where(even, 3 + nx, 0)
    far_at = jnp.where(even, 0, 3 + nx)

    def edges(x, carry):
        partial[near_at + x] = dot(filters[0], tap_columns(near, x, tiles))
        partial[far_at + x] = dot(filters[0], tap_columns(far, x, tiles))
        return carry

    lax.fori_loop(0, 3, edges, 0)
    for x in range(nx):
        partial[x + 3] = own[x]
    activate(plan, nx + 4, tiles, partial, volume)
    zero = jnp.zeros((CP, LANES), volume.dtype)
    for x in range(nx + 4):
        volume[x, 0] = zero
        volume[x, wide - 1] = zero

    def body(x, carry):
        partial[x] = dot(filters[1], tap_columns(volume, x, tiles))
        return carry

    lax.fori_loop(0, nx + 4, body, 0, unroll=2)
    activate(plan, nx + 2, tiles, partial, second)
    for copy in copies:
        copy.wait()


def conv_last_body(plan, after, second, filters, *rest):
    sources, third, targets, partial, sems = rest[:4], rest[4], rest[5:9], rest[9], rest[10]
    copies = prefetches(sources, targets, sems)
    for copy in copies:
        copy.start()
    nx = plan.cx // 2
    ny = plan.cy // 4
    tiles = (2, ny + 2)

    def body(x, carry):
        partial[x] = dot(filters[2], tap_columns(second, x, tiles))
        return carry

    lax.fori_loop(0, nx + 2, body, 0, unroll=True)

    square = (LANES, 2 * LANES)
    spread = where_bf16(iota(square, 1) // 2 == iota(square, 0))

    def up(x, carry):
        for j in range(ny):
            total = combined(partial, x, slice(j * LANES, (j + 1) * LANES))
            wide = dot(total.astype(BF16), spread).astype(BF16)
            third[x, 2 * j] = wide[:, : plan.cz]
            third[x, 2 * j + 1] = wide[:, plan.cz :]
        return carry

    lax.fori_loop(0, nx, up, 0, unroll=True)
    for copy in copies:
        copy.wait()


def final_body(plan, field, third, lift, regroup, inverse, own, *rest):
    messages = rest[: plan.dy - 1]
    out, line, lanes = rest[plan.dy - 1 :]
    step = pl.program_id(0)
    half = plan.cy // 2
    part = plan.cg * plan.cy

    @pl.when(step == 0)
    def _():
        here = lax.axis_index("gy")
        line[here] = own[...]
        for s, message in enumerate(messages):
            line[turn(here, -(s + 1), plan.dy)] = message[...]
        gathered = jnp.concatenate([line[s] for s in range(plan.dy)], axis=1)
        result = dot(gathered, regroup[...]).astype(BF16)
        width = plan.dy * plan.unit
        for g in range(plan.groups):
            lanes[g * part : (g + 1) * part] = result[:, g * width : (g + 1) * width]

    cells = plan.channels * half
    columns = []
    for e in range(2):
        for h in range(2):
            cols = third[0, h * (half // 2) : (h + 1) * (half // 2)]
            columns.append(
                jnp.concatenate(
                    [
                        field[:, e, h * half : (h + 1) * half].reshape(cells, plan.cz),
                        cols.astype(F32).reshape(half // 2 * CP, plan.cz).astype(BF16),
                    ],
                    axis=0,
                )
            )
    local = dot(lift[...], jnp.concatenate(columns, axis=1))
    spectral = dot(lanes[...], inverse[...]).reshape(plan.channels, plan.cy, 2 * plan.cz)
    for e in range(2):
        for h in range(2):
            index = e * 2 + h
            total = local[:, index * plan.cz : (index + 1) * plan.cz].reshape(
                plan.channels, half, plan.cz
            ) + spectral[:, h * half : (h + 1) * half, e * plan.cz : (e + 1) * plan.cz]
            out[:, e, h * half : (h + 1) * half] = gelu(total).astype(BF16)


def after(values, marker):
    return lax.optimization_barrier((values, marker))[0]


def ring(value, axis, shift):
    count = lax.axis_size(axis)
    return lax.ppermute(value, axis, [(i, (i + shift) % count) for i in range(count)])


def on_device(features, spectral_weight, conv_weight, point_weight):
    devices_x = lax.axis_size("gx")
    devices_y = lax.axis_size("gy")
    plan = Plan(features.shape, spectral_weight.shape, devices_x, devices_y)
    channels, cx, cy, cz = features.shape
    shape = jax.ShapeDtypeStruct
    cg = plan.cg
    nx, ny = cx // 2, cy // 4
    part = cg * cy
    split = plan.ky % 16 == 0 and plan.kz * plan.kx == LANES
    half = cy // 2

    rows_table, pair_table = pool_tables(plan)
    tables = (
        plan.forward_z(), plan.regroup(plan.groups, devices_y), rows_table, pair_table,
        plan.forward_y(), plan.swap(1.0),
    )
    chunk = shape((part, LANES), BF16)
    message = shape((part + nx * 2 * CP, LANES), BF16)
    outs = [chunk, message, message] + [chunk] * (devices_y - 3)
    outs += [shape((nx, ny, CP, cz), BF16)] + [shape(t.shape, BF16) for t in tables[4:]]
    if split:
        early, late = channels // 10, 3 * channels // 10
        pack = lambda n: shape((n, 2, channels, plan.ky, LANES), BF16)
        hold = lambda n: [
            pltpu.VMEM((n, 2) + spectral_weight.shape[2:], F32), pltpu.SemaphoreType.DMA((n,))
        ]
    packs = [pack(early)] if split else []
    first = call(
        functools.partial(first_body, plan),
        outs + packs,
        (features,) + tables + ((spectral_weight,) if split else ()),
        out_specs=[VMEM] * len(outs) + [FAR] * len(packs),
        scratch=[pltpu.VMEM(features.shape, BF16)]
        + [pltpu.VMEM(t.shape, BF16) for t in tables[:4]]
        + [pltpu.VMEM((devices_y, part, LANES), BF16), pltpu.SemaphoreType.DMA((7,))]
        + (hold(early) if split else []),
        specs=[HBM] * (7 + len(packs)),
        vmem=16,
    )
    packed_early = first[-1]
    first = first[: len(outs)]
    own, to_up, to_down = first[:3]
    middle = first[3:-3]
    coarse, y_table, y_swap = first[-3:]
    low_message = ring(to_up, "gy", 1)
    high_message = ring(to_down, "gy", -1)
    middle = [ring(m, "gy", s + 2) for s, m in enumerate(middle)]

    y_out = (devices_x, cg, plan.ky) if split else (1, cg, plan.my)
    planes = shape((3, ny + 4, CP, LANES), BF16)
    y_spec, near, far, volume = call(
        functools.partial(forward_y_body, plan),
        (shape(y_out + (LANES,), BF16), planes, planes, shape((nx, ny + 4, CP, LANES), BF16)),
        (own, low_message, high_message, *middle, coarse, y_table, y_swap),
        out_specs=[PLAIN, FAR, FAR, VMEM],
        scratch=[pltpu.VMEM((devices_y, part, LANES), BF16)],
    )
    if not split:
        y_spec = jnp.transpose(y_spec.reshape(cg, devices_x, plan.ky, LANES), (1, 0, 2, 3))
    pencil = lax.all_to_all(y_spec, "gx", 0, 0, tiled=True)

    filters = jnp.pad(
        conv_weight.reshape(3, 3, 9, channels, channels),
        ((0, 0), (0, 0), (0, 0), (0, CP - channels), (0, CP - channels)),
    )
    filters = jnp.transpose(filters, (0, 1, 3, 2, 4)).reshape(3, 3 * CP, 9 * CP)
    wide = (ny + 2) * LANES
    small = (
        shape((nx, 3 * CP, wide), F32),
        shape((channels * half, channels * half + half // 2 * CP), BF16),
    )
    local = (volume, filters, jnp.transpose(point_weight))
    if split:
        tables = (plan.forward_x(), plan.inverse_x())
        packed_late, partial_own, lift, forward_x, inverse_x = call(
            functools.partial(window_body, plan, early),
            (pack(late),) + small + tuple(shape(t.shape, BF16) for t in tables),
            (y_spec,) + local + (spectral_weight,) + tables,
            specs=[ANY] + [VMEM, PLAIN, PLAIN] + [HBM] * 3,
            out_specs=[FAR, FAR, FAR, VMEM, VMEM],
            scratch=hold(late) + [pltpu.SemaphoreType.DMA((2,))],
            vmem=12,
            flops=4e9,
            moved=8e6,
        )
    else:
        partial_own, lift = call(
            functools.partial(conv_own_body, plan),
            small,
            local,
            specs=[VMEM, PLAIN, PLAIN],
            out_specs=[FAR, FAR],
            flops=2e9,
        )
    near, far = after((near, far), partial_own)
    pairs = [(i, i ^ 1) for i in range(devices_x)]
    near = lax.ppermute(near, "gx", pairs)
    pairs = [(i, i + 1) for i in range(1, devices_x - 1, 2)]
    far = lax.ppermute(far, "gx", pairs + [(t, s) for s, t in pairs])

    if split:
        back = call(
            functools.partial(x_body, plan),
            shape((devices_x, cg, plan.ky, LANES), BF16),
            (pencil, forward_x, packed_early, packed_late, inverse_x, spectral_weight),
            specs=[VMEM, VMEM, HBM, HBM, VMEM, HBM],
            out_specs=[PLAIN],
            scratch=[
                pltpu.VMEM((early + late, 2, channels, plan.ky, LANES), BF16),
                pltpu.SemaphoreType.DMA((2,)),
            ]
            + hold(channels - early - late)
            + [pltpu.VMEM((2, channels, plan.ky, LANES), F32)] * 2,
            vmem=20,
        )
    else:
        back = x_stage_general(plan, pencil, spectral_weight)
    line = lax.all_to_all(back, "gx", 0, 0, tiled=True)

    tables = (plan.inverse_y(), plan.swap(-1.0))
    second, inverse_table, inverse_swap = call(
        functools.partial(conv_middle_body, plan),
        [shape((nx + 2, ny + 4, CP, LANES), F32)] + [shape(t.shape, BF16) for t in tables],
        (back, near, far, partial_own, filters) + tables,
        scratch=[
            pltpu.VMEM((nx + 6, 3 * CP, wide), F32),
            pltpu.VMEM((nx + 4, ny + 4, CP, LANES), F32),
            pltpu.SemaphoreType.DMA((2,)),
        ],
        specs=[ANY, PLAIN, PLAIN, FAR, PLAIN, HBM, HBM],
        out_specs=[PLAIN, VMEM, VMEM],
        vmem=8,
        flops=6e9,
    )
    if not split:
        line = jnp.transpose(line, (1, 0, 2, 3)).reshape(1, cg, plan.my, LANES)
    own, *messages = call(
        functools.partial(inverse_y_body, plan),
        [chunk] * devices_y,
        (line, inverse_table, inverse_swap),
        scratch=[pltpu.VMEM((devices_y, part, LANES), BF16)],
    )
    arrived = [ring(m, "gy", s + 1) for s, m in enumerate(messages)]
    tables = (features, lift, plan.regroup(devices_y, plan.groups), plan.inverse_z())
    third, *tables = call(
        functools.partial(conv_last_body, plan),
        [shape((nx, 2 * ny, CP, cz), BF16)] + [shape(t.shape, BF16) for t in tables],
        (own, second, filters) + tables,
        scratch=[
            pltpu.VMEM((nx + 2, 3 * CP, ny * LANES), F32), pltpu.SemaphoreType.DMA((4,))
        ],
        specs=[ANY, PLAIN, PLAIN] + [HBM] * 4,
        out_specs=[PLAIN] + [VMEM] * 4,
        flops=3e9,
    )
    near = lambda array: pltpu.with_memory_space_constraint(array, pltpu.VMEM)
    field, lift, regroup, inverse_z = (near(t) for t in tables)

    full = lambda array: pl.BlockSpec(array.shape, lambda s: (0,) * array.ndim)
    return call(
        functools.partial(final_body, plan),
        shape(features.shape, BF16),
        (field, third, lift, regroup, inverse_z, own, *arrived),
        pin=False,
        grid=(nx,),
        specs=[
            pl.BlockSpec((channels, 2, cy, cz), lambda s: (0, s, 0, 0)),
            pl.BlockSpec((1, cy // 2, CP, cz), lambda s: (s, 0, 0, 0)),
            full(lift),
            full(regroup),
            pl.BlockSpec((devices_y * plan.unit, 2 * cz), lambda s: (0, s)),
        ]
        + [full(own)] * devices_y,
        out_specs=[pl.BlockSpec((channels, 2, cy, cz), lambda s: (0, s, 0, 0))],
        scratch=[
            pltpu.VMEM((devices_y, part, LANES), BF16),
            pltpu.VMEM((channels * cy, devices_y * plan.unit), BF16),
        ],
        vmem=12,
    )


def solution(mesh):
    in_specs = (P(None, ("grp", "gx"), "gy", None), P(None, None, None, "gy", "gx", None), P(), P())
    out_specs = P(None, ("grp", "gx"), "gy", None)
    return jax.shard_map(
        on_device, mesh=mesh, in_specs=in_specs, out_specs=out_specs, check_vma=False
    )
```

```python
import functools
import math

import jax
import jax.numpy as jnp
import numpy as np
from jax import lax
from jax.experimental import pallas as pl
from jax.experimental.pallas import tpu as pltpu
from jax.sharding import PartitionSpec as P

LANES = 128
CP = 24
BF16 = jnp.bfloat16
F32 = jnp.float32
MIB = 1024 * 1024


def dot(left, right):
    return jnp.dot(left, right, preferred_element_type=F32)


def signed_modes(count):
    position = np.arange(count)
    return np.where(position < count // 2, position, position - count)


def phase(frequency, length):
    index = np.mod(frequency[:, None] * np.arange(length)[None, :], length)
    angle = index.astype(np.float32) * np.float32(2.0 * math.pi / length)
    return (
        np.cos(angle).astype(BF16).astype(np.float32),
        np.sin(angle).astype(BF16).astype(np.float32),
    )


def const(array):
    return np.asarray(array, np.float32).astype(BF16)


class Plan:
    def __init__(self, features, spectral_weight, devices_x, devices_y):
        self.channels, self.cx, self.cy, self.cz = features
        self.dx, self.dy = devices_x, devices_y
        self.kz, self.ky, self.kx = spectral_weight[3:]
        self.gx, self.gy = self.cx * self.dx, self.cy * self.dy
        self.my = self.ky * self.dx
        self.mz = self.kz * self.dy
        self.unit = 2 * self.kz * self.cx
        self.groups = LANES // self.unit
        self.cg = self.channels // self.groups

    def forward_z(self):
        cos, sin = phase(np.arange(self.mz), self.cz)
        table = np.stack([cos, -sin], 0).reshape(2, self.dy, self.kz, self.cz)
        out = np.einsum("pdkz,xw->xzdpkw", table, np.eye(self.cx))
        return const(out.reshape(self.cx * self.cz, self.dy * self.unit))

    def inverse_z(self):
        cos, sin = phase(np.arange(self.mz), self.cz)
        scale = np.where(np.arange(self.mz) == 0, 1.0, 2.0) / float(self.gx * self.gy * self.cz)
        table = np.stack([cos, -sin], 0) * scale[None, :, None]
        table = table.reshape(2, self.dy, self.kz, self.cz)
        out = np.einsum("pdkz,xw->dpkxwz", table, np.eye(self.cx))
        return const(out.reshape(self.dy * self.unit, self.cx * self.cz))

    def regroup(self, outer, inner):
        out = np.einsum("ac,bd,lm->abldcm", np.eye(outer), np.eye(inner), np.eye(self.unit))
        size = outer * inner * self.unit
        return const(out.reshape(size, size))

    def swap(self, sign):
        turn = np.array([[0.0, -sign], [sign, 0.0]])
        half = self.unit // 2
        return const(np.kron(np.eye(self.groups), np.kron(turn, np.eye(half))))

    def forward_y(self):
        cos, sin = phase(signed_modes(self.my), self.gy)
        return const(np.concatenate([cos, sin], 1))

    def inverse_y(self):
        cos, sin = phase(signed_modes(self.my), self.gy)
        return const(np.concatenate([cos.T, sin.T], 1))

    def turn_x(self, sign):
        cos, sin = phase(signed_modes(self.kx), self.gx)
        turn = np.stack([np.stack([cos, -sign * sin]), np.stack([sign * sin, cos])])
        return turn.reshape(2, 2, self.kx, self.dx, self.cx)

    def forward_x(self):
        out = np.einsum("pqjsx,g,kl->sgpkxqlj", self.turn_x(1.0), np.ones(self.groups), np.eye(self.kz))
        return const(out.reshape(self.dx * LANES, self.kz * 2 * self.kx))

    def inverse_x(self):
        out = np.einsum("pqjsx,h,kl->pkjshqlx", self.turn_x(-1.0), np.ones(self.groups), np.eye(self.kz))
        return const(out.reshape(self.kz * 2 * self.kx, self.dx * LANES))


VMEM = pl.BlockSpec(memory_space=pltpu.VMEM)
PLAIN = pl.BlockSpec(memory_space=pltpu.VMEM)
FAR = pl.BlockSpec(memory_space=pltpu.VMEM)


ANY = pl.BlockSpec(memory_space=pl.ANY)
HBM = pl.BlockSpec(memory_space=pltpu.HBM)


def pinned(value, spec):
    if spec is HBM or spec is FAR:
        return pltpu.with_memory_space_constraint(jnp.asarray(value), pltpu.HBM)
    if spec is ANY or spec is PLAIN or isinstance(value, np.ndarray):
        return value
    return pltpu.with_memory_space_constraint(value, pltpu.VMEM)


def call(
    body, outs, inputs, scratch=(), specs=None, out_specs=None, vmem=8, flops=1e9, moved=1e6,
    pin=True, **kw,
):
    single = not isinstance(outs, (tuple, list))
    outs = [outs] if single else list(outs)
    specs = specs or [VMEM] * len(inputs)
    out_specs = out_specs or [VMEM] * len(outs)
    if pin:
        inputs = [pinned(value, spec) for value, spec in zip(inputs, specs)]
        outs = [
            pltpu.VMEM(o.shape, o.dtype)
            if spec is VMEM
            else pltpu.HBM(o.shape, o.dtype) if spec is FAR else o
            for o, spec in zip(outs, out_specs)
        ]
    result = pl.pallas_call(
        body,
        out_shape=outs,
        in_specs=specs,
        out_specs=out_specs,
        scratch_shapes=scratch,
        compiler_params=pltpu.CompilerParams(vmem_limit_bytes=vmem * MIB),
        cost_estimate=pl.CostEstimate(
            flops=int(flops), bytes_accessed=int(moved), transcendentals=0
        ),
        **kw,
    )(*inputs)
    return result[0] if single else result


def turn(index, shift, count):
    return lax.rem(index + shift + count, count)


def first_body(
    plan, field_in, table_in, regroup_in, rows_in, pair_in, ytable_in, swap_in, *rest
):
    own, low_message, high_message, *rest = rest
    middle = rest[: plan.dy - 3]
    coarse, ytable, swap, field, table, regroup, rows_table, pair_table, chunks, sems = rest[
        plan.dy - 3 :
    ]
    middle_channel = plan.channels // 2
    lower = pl.ds(0, middle_channel)
    upper = pl.ds(middle_channel, plan.channels - middle_channel)
    sources = (
        table_in, field_in.at[lower], field_in.at[upper],
        regroup_in, rows_in, pair_in, ytable_in, swap_in,
    )
    targets = (
        table, field.at[lower], field.at[upper], regroup, rows_table, pair_table, ytable, swap
    )
    copies = [
        pltpu.make_async_copy(s, t, sems.at[n]) for n, (s, t) in enumerate(zip(sources, targets))
    ]
    for copy in copies:
        copy.start()
    copies[0].wait()
    pieces = []
    for n, (low, high) in enumerate(((0, middle_channel), (middle_channel, plan.channels))):
        copies[1 + n].wait()
        rows = (high - low) * plan.cy
        lhs = jnp.concatenate(
            [field[low:high, x].reshape(rows, plan.cz) for x in range(plan.cx)], axis=1
        )
        pieces.append(dot(lhs, table[...]).astype(BF16))
    modes = jnp.concatenate(pieces, axis=0)
    copies[3].wait()
    part = plan.cg * plan.cy
    lanes = jnp.concatenate(
        [modes[g * part : (g + 1) * part] for g in range(plan.groups)], axis=1
    )
    result = dot(lanes, regroup[...]).astype(BF16)
    for d in range(plan.dy):
        chunks[d] = result[:, d * LANES : (d + 1) * LANES]
    for copy in copies[4:]:
        copy.wait()
    pool_body(plan, field, rows_table, pair_table, coarse)
    here = lax.axis_index("gy")
    own[...] = chunks[here]
    low_message[:part] = chunks[turn(here, 1, plan.dy)]
    high_message[:part] = chunks[turn(here, plan.dy - 1, plan.dy)]
    for s, message in enumerate(middle):
        message[...] = chunks[turn(here, s + 2, plan.dy)]
    tiles = plan.cy // 4
    index = 0
    for x in range(plan.cx // 2):
        for j in range(2):
            at = slice(part + index * CP, part + (index + 1) * CP)
            low_message[at] = coarse[x, tiles - 2 + j]
            high_message[at] = coarse[x, j]
            index += 1


def y_transform(plan, line, table, swap):
    columns = []
    for value in line:
        turned = dot(value, swap[...]).astype(BF16)
        columns.append(jnp.concatenate([value, turned], axis=0))
    return dot(table[...], jnp.concatenate(columns, axis=1)).astype(BF16)


def forward_y_body(plan, own, low_message, high_message, *rest):
    middle = rest[: plan.dy - 3]
    coarse, table, swap, out, near, far, volume, line = rest[plan.dy - 3 :]
    part = plan.cg * plan.cy
    here = lax.axis_index("gy")
    line[here] = own[...]
    line[turn(here, -1, plan.dy)] = low_message[:part]
    line[turn(here, 1, plan.dy)] = high_message[:part]
    for s, message in enumerate(middle):
        line[turn(here, -(s + 2), plan.dy)] = message[...]
    values = [
        jnp.concatenate(
            [line[s, c * plan.cy : (c + 1) * plan.cy] for s in range(plan.dy)], axis=0
        )
        for c in range(plan.cg)
    ]
    result = y_transform(plan, values, table, swap)
    targets, _, rows_out, _ = out.shape
    for d in range(targets):
        for c in range(plan.cg):
            out[d, c] = result[
                d * rows_out : (d + 1) * rows_out, c * LANES : (c + 1) * LANES
            ]
    nx = plan.cx // 2
    tiles = plan.cy // 4
    for x in range(nx):
        for j in range(2):
            at = slice(part + (x * 2 + j) * CP, part + (x * 2 + j + 1) * CP)
            none = jnp.zeros((CP, LANES), BF16)
            volume[x, j] = jnp.where(here > 0, low_message[at], none)
            volume[x, 2 + tiles + j] = jnp.where(here < plan.dy - 1, high_message[at], none)
        for j in range(tiles):
            volume[x, 2 + j] = coarse[x, j]
    even = lax.rem(lax.axis_index("gx"), 2) == 0
    first_plane = jnp.where(even, nx - 3, 0)
    last_plane = jnp.where(even, 0, nx - 3)
    for x in range(3):
        near[x] = volume[first_plane + x]
        far[x] = volume[last_plane + x]


def inverse_y_body(plan, line, table, swap, own, *rest):
    messages = rest[: plan.dy - 1]
    chunks = rest[plan.dy - 1]
    sources = line.shape[0]
    values = [
        jnp.concatenate([line[s, c] for s in range(sources)], axis=0) for c in range(plan.cg)
    ]
    result = y_transform(plan, values, table, swap)
    for d in range(plan.dy):
        for c in range(plan.cg):
            chunks[d, c * plan.cy : (c + 1) * plan.cy] = result[
                d * plan.cy : (d + 1) * plan.cy, c * LANES : (c + 1) * LANES
            ]
    here = lax.axis_index("gy")
    own[...] = chunks[here]
    for s, message in enumerate(messages):
        message[...] = chunks[turn(here, s + 1, plan.dy)]


def mix(plan, spec, weight, mixed):
    def step(o, carry):
        for k in range(plan.kz):
            real = jnp.zeros((plan.ky, plan.kx), F32)
            imag = jnp.zeros((plan.ky, plan.kx), F32)
            for i in range(plan.channels):
                wr = weight[0, i, o, k]
                wi = weight[1, i, o, k]
                xr = spec[0, k, i]
                xi = spec[1, k, i]
                real += xr * wr - xi * wi
                imag += xr * wi + xi * wr
            mixed[k, o] = jnp.concatenate([real, imag], axis=1)
        return carry

    lax.fori_loop(0, plan.channels, step, 0)


def weight_copy(weight, held, sems, begin, n):
    return pltpu.make_async_copy(weight.at[:, begin + n], held.at[n], sems.at[n])


def start_weights(weight, held, sems, begin):
    def one(n, carry):
        weight_copy(weight, held, sems, begin, n).start()
        return carry

    lax.fori_loop(0, held.shape[0], one, 0)


def pack_weights(plan, weight, held, sems, begin, packed):
    def one(n, carry):
        weight_copy(weight, held, sems, begin, n).wait()
        for p in range(2):
            for o in range(plan.channels):
                packed[n, p, o] = jnp.concatenate(
                    [held[n, p, o, k] for k in range(plan.kz)], axis=1
                ).astype(BF16)
        return carry

    lax.fori_loop(0, held.shape[0], one, 0)


def early_body(plan, after, weight, packed, held, sems):
    start_weights(weight, held, sems, 0)
    pack_weights(plan, weight, held, sems, 0, packed)


def window_body(
    plan, begin, after, volume, filters, point, weight, forward_in, inverse_in,
    packed, partial, lift, forward, inverse, held, sems, table_sems,
):
    copies = prefetches((forward_in, inverse_in), (forward, inverse), table_sems)
    for copy in copies:
        copy.start()
    start_weights(weight, held, sems, begin)
    conv_own_body(plan, volume, filters, point, partial, lift)
    pack_weights(plan, weight, held, sems, begin, packed)
    for copy in copies:
        copy.wait()


def lane_group(plan, shape):
    return (lax.broadcasted_iota(jnp.int32, shape, 1) % LANES) // plan.unit


def by_group(plan, lanes):
    owner = lane_group(plan, lanes.shape)
    return jnp.concatenate(
        [jnp.where(owner == g, lanes, jnp.zeros_like(lanes)) for g in range(plan.groups)], axis=0
    )


def one_group(plan, stacked):
    rows = stacked.shape[0] // plan.groups
    owner = lane_group(plan, (rows, stacked.shape[1]))
    result = stacked[:rows]
    for g in range(1, plan.groups):
        result = jnp.where(owner == g, stacked[g * rows : (g + 1) * rows], result)
    return result


def x_body(
    plan, pencil, forward, packed_early, packed_late, inverse, weight, out,
    packed, sems, held, held_sems, spec, mixed,
):
    early = packed_early.shape[0]
    ready = packed.shape[0]
    copies = [
        pltpu.make_async_copy(packed_early, packed.at[pl.ds(0, early)], sems.at[0]),
        pltpu.make_async_copy(packed_late, packed.at[pl.ds(early, ready - early)], sems.at[1]),
    ]
    for copy in copies:
        copy.start()
    start_weights(weight, held, held_sems, ready)
    rows = plan.cg * plan.ky
    wide = plan.kz * plan.kx
    lhs = jnp.concatenate([pencil[s].reshape(rows, LANES) for s in range(plan.dx)], axis=1)
    spectrum = dot(by_group(plan, lhs), forward[...])
    for g in range(plan.groups):
        for p in range(2):
            modes = spectrum[g * rows : (g + 1) * rows, p * wide : (p + 1) * wide]
            spec[p, g * plan.cg : (g + 1) * plan.cg] = modes.reshape(plan.cg, plan.ky, wide)

    def step(o, carry):
        real = jnp.zeros((plan.ky, wide), F32)
        imag = jnp.zeros((plan.ky, wide), F32)
        for i in range(ready):
            wr = packed[i, 0, o].astype(F32)
            wi = packed[i, 1, o].astype(F32)
            xr = spec[0, i]
            xi = spec[1, i]
            real += xr * wr - xi * wi
            imag += xr * wi + xi * wr
        mixed[0, o] = real
        mixed[1, o] = imag
        return carry

    def streamed(n, carry):
        weight_copy(weight, held, held_sems, ready, n).wait()
        xr = spec[0, ready + n]
        xi = spec[1, ready + n]
        for o in range(plan.channels):
            wr, wi = (
                jnp.concatenate([held[n, p, o, k] for k in range(plan.kz)], axis=1)
                for p in range(2)
            )
            mixed[0, o] += xr * wr - xi * wi
            mixed[1, o] += xr * wi + xi * wr
        return carry

    for copy in copies:
        copy.wait()
    lax.fori_loop(0, plan.channels, step, 0, unroll=2)
    lax.fori_loop(0, plan.channels - ready, streamed, 0)
    back = jnp.concatenate(
        [
            jnp.concatenate(
                [
                    mixed[p, g * plan.cg : (g + 1) * plan.cg].reshape(rows, wide).astype(BF16)
                    for p in range(2)
                ],
                axis=1,
            )
            for g in range(plan.groups)
        ],
        axis=0,
    )
    result = one_group(plan, dot(back, inverse[...])).astype(BF16)
    for d in range(plan.dx):
        out[d] = result[:, d * LANES : (d + 1) * LANES].reshape(plan.cg, plan.ky, LANES)


def x_stage_general(plan, pencil, weight):
    groups, cg, ky, kz, kx = plan.groups, plan.cg, plan.ky, plan.kz, plan.kx
    lhs = jnp.transpose(pencil, (1, 2, 0, 3)).reshape(cg * ky, plan.dx * LANES)
    spectrum = dot(by_group(plan, lhs), plan.forward_x()).reshape(groups, cg, ky, 2, kz, kx)
    spectrum = jnp.transpose(spectrum, (3, 4, 0, 1, 2, 5)).reshape(2, kz, groups * cg, ky, kx)
    mixed = call(
        functools.partial(mix, plan),
        jax.ShapeDtypeStruct((kz, groups * cg, ky, 2 * kx), F32),
        (spectrum, weight),
        vmem=32,
        pin=False,
    )
    back = jnp.transpose(mixed.reshape(kz, groups, cg, ky, 2, kx), (1, 2, 3, 4, 0, 5))
    back = back.reshape(groups * cg * ky, kz * 2 * kx).astype(BF16)
    back = one_group(plan, dot(back, plan.inverse_x())).astype(BF16)
    back = back.reshape(cg, ky, plan.dx, LANES)
    return jnp.transpose(back, (2, 0, 1, 3))


def gelu(value):
    return 0.5 * value * (1.0 + lax.erf(value * (0.5**0.5)))


def pool_tables(plan):
    half = plan.cy // 2
    quarter = half // 2
    rows = np.einsum(
        "cC,yY->ycCY", np.eye(CP)[:, : plan.channels], np.kron(np.eye(quarter), np.ones((1, 2)))
    ).reshape(quarter * CP, plan.channels * half)
    rows = np.concatenate([rows, rows], 1)
    pairs = np.kron(np.eye(plan.cz), np.full((2, 1), 0.125))
    return const(rows), const(pairs)


def pool_body(plan, field, rows_table, pair_table, out):
    half = plan.cy // 2
    quarter = half // 2
    cells = plan.channels * half
    for h in range(2):
        columns = []
        for x in range(plan.cx // 2):
            columns.append(
                jnp.concatenate(
                    [
                        field[:, 2 * x + e, h * half : (h + 1) * half].reshape(cells, plan.cz)
                        for e in range(2)
                    ],
                    axis=0,
                )
            )
        summed = dot(rows_table[...], jnp.concatenate(columns, axis=1))
        blocks = []
        for x in range(plan.cx // 2):
            for j in range(quarter // 2):
                blocks.append(
                    jnp.concatenate(
                        [
                            summed[
                                (2 * j + e) * CP : (2 * j + e + 1) * CP,
                                x * plan.cz : (x + 1) * plan.cz,
                            ]
                            for e in range(2)
                        ],
                        axis=1,
                    )
                )
        block = jnp.concatenate(blocks, axis=0)
        high = block.astype(BF16)
        low = (block - high.astype(F32)).astype(BF16)
        result = dot(high, pair_table[...]) + dot(low, pair_table[...])
        index = 0
        for x in range(plan.cx // 2):
            for j in range(quarter // 2):
                out[x, h * (quarter // 2) + j] = result[index * CP : (index + 1) * CP].astype(BF16)
                index += 1


def tap_columns(volume, x, tiles):
    lane = lax.broadcasted_iota(jnp.int32, (CP, LANES), 1)
    z = lane % (LANES // 2)
    lower = lane < LANES // 2
    shifted = {}
    for j in range(tiles[0] - 1, tiles[1] + 1):
        value = volume[x, j].astype(F32)
        versions = (
            jnp.where(z == 0, 0.0, pltpu.roll(value, 1, 1)),
            value,
            jnp.where(z == LANES // 2 - 1, 0.0, pltpu.roll(value, LANES - 1, 1)),
        )
        shifted[j] = (versions, [pltpu.roll(v, LANES // 2, 1) for v in versions])
    columns = []
    for j in range(tiles[0], tiles[1]):
        pieces = []
        for e in range(3):
            pieces.append(jnp.where(lower, shifted[j - 1][1][e], shifted[j][1][e]))
        for e in range(3):
            pieces.append(shifted[j][0][e])
        for e in range(3):
            pieces.append(jnp.where(lower, shifted[j][1][e], shifted[j + 1][1][e]))
        columns.append(jnp.concatenate(pieces, axis=0).astype(BF16))
    return jnp.concatenate(columns, axis=1)


def combined(partial, x, cols):
    return (
        partial[x, 0:CP, cols]
        + partial[x + 1, CP : 2 * CP, cols]
        + partial[x + 2, 2 * CP : 3 * CP, cols]
    )


def activate(plan, planes, tiles, partial, volume):
    nx = plan.cx // 2
    ny = plan.cy // 4
    here_x = lax.axis_index("gx")
    here_y = lax.axis_index("gy")
    one = jnp.float32(1.0)
    zero = jnp.float32(0.0)
    below_x = jnp.where(here_x > 0, one, zero)
    above_x = jnp.where(here_x < plan.dx - 1, one, zero)
    below_y = jnp.where(here_y > 0, one, zero)
    above_y = jnp.where(here_y < plan.dy - 1, one, zero)
    margin = (planes - nx) // 2

    def body(x, carry):
        inside = jnp.where(x < margin, below_x, one) * jnp.where(x >= margin + nx, above_x, one)
        for j in range(tiles[0], tiles[1]):
            cols = slice((j - tiles[0]) * LANES, (j - tiles[0] + 1) * LANES)
            scale = inside
            if j < 2:
                scale = scale * below_y
            if j >= 2 + ny:
                scale = scale * above_y
            value = gelu(combined(partial, x, cols)) * scale
            volume[x, j] = value.astype(volume.dtype)
        return carry

    lax.fori_loop(0, planes, body, 0, unroll=2)


def where_bf16(mask):
    return jnp.where(mask, 1.0, 0.0).astype(BF16)


def iota(shape, dim):
    return lax.broadcasted_iota(jnp.int32, shape, dim)


def make_lift(plan, point, lift):
    half = plan.cy // 2
    cells = plan.channels * half
    tall = (cells, plan.channels)
    flat = (plan.channels, cells)
    square = (cells, cells)
    pick_o = where_bf16(iota(tall, 0) // half == iota(tall, 1))
    pick_i = where_bf16(iota(flat, 1) // half == iota(flat, 0))
    expanded = dot(dot(pick_o, point[...]).astype(BF16), pick_i)
    diagonal = iota(square, 0) % half == iota(square, 1) % half
    lift[:, :cells] = jnp.where(diagonal, expanded, 0.0).astype(BF16)
    coarse = (cells, half // 2 * CP)
    row, col = iota(coarse, 0), iota(coarse, 1)
    lift[:, cells:] = where_bf16(
        (row // half == col % CP) & ((row % half) // 2 == col // CP)
    )


def conv_own_body(plan, volume_in, filters, point, partial, lift):
    nx = plan.cx // 2
    ny = plan.cy // 4
    make_lift(plan, point, lift)

    def body(x, carry):
        partial[x] = dot(filters[0], tap_columns(volume_in, x, (1, ny + 3)))
        return carry

    lax.fori_loop(0, nx, body, 0, unroll=2)


def prefetches(sources, targets, sems):
    return [
        pltpu.make_async_copy(s, t, sems.at[n]) for n, (s, t) in enumerate(zip(sources, targets))
    ]


def conv_middle_body(
    plan, after, near, far, own, filters, table_in, swap_in,
    second, table, swap, partial, volume, sems,
):
    copies = prefetches((table_in, swap_in), (table, swap), sems)
    for copy in copies:
        copy.start()
    nx = plan.cx // 2
    ny = plan.cy // 4
    wide = ny + 4
    tiles = (1, ny + 3)

    even = lax.rem(lax.axis_index("gx"), 2) == 0
    near_at = jnp.where(even, 3 + nx, 0)
    far_at = jnp.where(even, 0, 3 + nx)

    def edges(x, carry):
        partial[near_at + x] = dot(filters[0], tap_columns(near, x, tiles))
        partial[far_at + x] = dot(filters[0], tap_columns(far, x, tiles))
        return carry

    lax.fori_loop(0, 3, edges, 0)
    for x in range(nx):
        partial[x + 3] = own[x]
    activate(plan, nx + 4, tiles, partial, volume)
    zero = jnp.zeros((CP, LANES), volume.dtype)
    for x in range(nx + 4):
        volume[x, 0] = zero
        volume[x, wide - 1] = zero

    def body(x, carry):
        partial[x] = dot(filters[1], tap_columns(volume, x, tiles))
        return carry

    lax.fori_loop(0, nx + 4, body, 0, unroll=2)
    activate(plan, nx + 2, tiles, partial, second)
    for copy in copies:
        copy.wait()


def conv_last_body(plan, after, second, filters, *rest):
    sources, third, targets, partial, sems = rest[:4], rest[4], rest[5:9], rest[9], rest[10]
    copies = prefetches(sources, targets, sems)
    for copy in copies:
        copy.start()
    nx = plan.cx // 2
    ny = plan.cy // 4
    tiles = (2, ny + 2)

    def body(x, carry):
        partial[x] = dot(filters[2], tap_columns(second, x, tiles))
        return carry

    lax.fori_loop(0, nx + 2, body, 0, unroll=True)

    square = (LANES, 2 * LANES)
    spread = where_bf16(iota(square, 1) // 2 == iota(square, 0))

    def up(x, carry):
        for j in range(ny):
            total = combined(partial, x, slice(j * LANES, (j + 1) * LANES))
            wide = dot(total.astype(BF16), spread).astype(BF16)
            third[x, 2 * j] = wide[:, : plan.cz]
            third[x, 2 * j + 1] = wide[:, plan.cz :]
        return carry

    lax.fori_loop(0, nx, up, 0, unroll=True)
    for copy in copies:
        copy.wait()


def final_body(plan, field, third, lift, regroup, inverse, own, *rest):
    messages = rest[: plan.dy - 1]
    out, line, lanes = rest[plan.dy - 1 :]
    step = pl.program_id(0)
    half = plan.cy // 2
    part = plan.cg * plan.cy

    @pl.when(step == 0)
    def _():
        here = lax.axis_index("gy")
        line[here] = own[...]
        for s, message in enumerate(messages):
            line[turn(here, -(s + 1), plan.dy)] = message[...]
        gathered = jnp.concatenate([line[s] for s in range(plan.dy)], axis=1)
        result = dot(gathered, regroup[...]).astype(BF16)
        width = plan.dy * plan.unit
        for g in range(plan.groups):
            lanes[g * part : (g + 1) * part] = result[:, g * width : (g + 1) * width]

    cells = plan.channels * half
    columns = []
    for e in range(2):
        for h in range(2):
            cols = third[step, h * (half // 2) : (h + 1) * (half // 2)]
            columns.append(
                jnp.concatenate(
                    [
                        field[:, 2 * step + e, h * half : (h + 1) * half].reshape(cells, plan.cz),
                        cols.astype(F32).reshape(half // 2 * CP, plan.cz).astype(BF16),
                    ],
                    axis=0,
                )
            )
    local = dot(lift[...], jnp.concatenate(columns, axis=1))
    at = pl.multiple_of(step * 2 * plan.cz, 2 * plan.cz)
    spectral = dot(lanes[...], inverse[:, pl.ds(at, 2 * plan.cz)]).reshape(plan.channels, plan.cy, 2 * plan.cz)
    for e in range(2):
        for h in range(2):
            index = e * 2 + h
            total = local[:, index * plan.cz : (index + 1) * plan.cz].reshape(
                plan.channels, half, plan.cz
            ) + spectral[:, h * half : (h + 1) * half, e * plan.cz : (e + 1) * plan.cz]
            out[:, e, h * half : (h + 1) * half] = gelu(total).astype(BF16)


def after(values, marker):
    return lax.optimization_barrier((values, marker))[0]


def ring(value, axis, shift):
    count = lax.axis_size(axis)
    return lax.ppermute(value, axis, [(i, (i + shift) % count) for i in range(count)])


def on_device(features, spectral_weight, conv_weight, point_weight):
    devices_x = lax.axis_size("gx")
    devices_y = lax.axis_size("gy")
    plan = Plan(features.shape, spectral_weight.shape, devices_x, devices_y)
    channels, cx, cy, cz = features.shape
    shape = jax.ShapeDtypeStruct
    cg = plan.cg
    nx, ny = cx // 2, cy // 4
    part = cg * cy
    split = plan.ky % 16 == 0 and plan.kz * plan.kx == LANES
    half = cy // 2

    rows_table, pair_table = pool_tables(plan)
    tables = (
        plan.forward_z(), plan.regroup(plan.groups, devices_y), rows_table, pair_table,
        plan.forward_y(), plan.swap(1.0),
    )
    chunk = shape((part, LANES), BF16)
    message = shape((part + nx * 2 * CP, LANES), BF16)
    outs = [chunk, message, message] + [chunk] * (devices_y - 3)
    outs += [shape((nx, ny, CP, cz), BF16)] + [shape(t.shape, BF16) for t in tables[4:]]
    if split:
        early, late = channels // 6, channels // 4
        pack = lambda n: shape((n, 2, channels, plan.ky, LANES), BF16)
        hold = lambda n: [
            pltpu.VMEM((n, 2) + spectral_weight.shape[2:], F32), pltpu.SemaphoreType.DMA((n,))
        ]
    first = call(
        functools.partial(first_body, plan),
        outs,
        (features,) + tables,
        scratch=[pltpu.VMEM(features.shape, BF16)]
        + [pltpu.VMEM(t.shape, BF16) for t in tables[:4]]
        + [pltpu.VMEM((devices_y, part, LANES), BF16), pltpu.SemaphoreType.DMA((8,))],
        specs=[HBM] * 7,
        vmem=16,
    )
    own, to_up, to_down = first[:3]
    middle = first[3:-3]
    coarse, y_table, y_swap = first[-3:]
    low_message = ring(to_up, "gy", 1)
    high_message = ring(to_down, "gy", -1)
    middle = [ring(m, "gy", s + 2) for s, m in enumerate(middle)]

    if split:
        packed_early = call(
            functools.partial(early_body, plan),
            pack(early),
            (own, spectral_weight),
            specs=[ANY, HBM],
            out_specs=[FAR],
            scratch=hold(early),
            moved=2e6,
        )
        own = after(own, packed_early)

    y_out = (devices_x, cg, plan.ky) if split else (1, cg, plan.my)
    planes = shape((3, ny + 4, CP, LANES), BF16)
    y_spec, near, far, volume = call(
        functools.partial(forward_y_body, plan),
        (shape(y_out + (LANES,), BF16), planes, planes, shape((nx, ny + 4, CP, LANES), BF16)),
        (own, low_message, high_message, *middle, coarse, y_table, y_swap),
        out_specs=[PLAIN, FAR, FAR, VMEM],
        scratch=[pltpu.VMEM((devices_y, part, LANES), BF16)],
    )
    if not split:
        y_spec = jnp.transpose(y_spec.reshape(cg, devices_x, plan.ky, LANES), (1, 0, 2, 3))
    pencil = lax.all_to_all(y_spec, "gx", 0, 0, tiled=True)

    filters = jnp.pad(
        conv_weight.reshape(3, 3, 9, channels, channels),
        ((0, 0), (0, 0), (0, 0), (0, CP - channels), (0, CP - channels)),
    )
    filters = jnp.transpose(filters, (0, 1, 3, 2, 4)).reshape(3, 3 * CP, 9 * CP)
    wide = (ny + 2) * LANES
    small = (
        shape((nx, 3 * CP, wide), F32),
        shape((channels * half, channels * half + half // 2 * CP), BF16),
    )
    local = (volume, filters, jnp.transpose(point_weight))
    if split:
        tables = (plan.forward_x(), plan.inverse_x())
        packed_late, partial_own, lift, forward_x, inverse_x = call(
            functools.partial(window_body, plan, early),
            (pack(late),) + small + tuple(shape(t.shape, BF16) for t in tables),
            (y_spec,) + local + (spectral_weight,) + tables,
            specs=[ANY] + [VMEM, PLAIN, PLAIN] + [HBM] * 3,
            out_specs=[FAR, FAR, FAR, VMEM, VMEM],
            scratch=hold(late) + [pltpu.SemaphoreType.DMA((2,))],
            vmem=12,
            flops=4e9,
            moved=8e6,
        )
    else:
        partial_own, lift = call(
            functools.partial(conv_own_body, plan),
            small,
            local,
            specs=[VMEM, PLAIN, PLAIN],
            out_specs=[FAR, FAR],
            flops=2e9,
        )
    near, far = after((near, far), partial_own)
    pairs = [(i, i ^ 1) for i in range(devices_x)]
    near = lax.ppermute(near, "gx", pairs)
    pairs = [(i, i + 1) for i in range(1, devices_x - 1, 2)]
    far = lax.ppermute(far, "gx", pairs + [(t, s) for s, t in pairs])

    if split:
        back = call(
            functools.partial(x_body, plan),
            shape((devices_x, cg, plan.ky, LANES), BF16),
            (pencil, forward_x, packed_early, packed_late, inverse_x, spectral_weight),
            specs=[VMEM, VMEM, HBM, HBM, VMEM, HBM],
            out_specs=[PLAIN],
            scratch=[
                pltpu.VMEM((early + late, 2, channels, plan.ky, LANES), BF16),
                pltpu.SemaphoreType.DMA((2,)),
            ]
            + hold(channels - early - late)
            + [pltpu.VMEM((2, channels, plan.ky, LANES), F32)] * 2,
            vmem=20,
        )
    else:
        back = x_stage_general(plan, pencil, spectral_weight)
    line = lax.all_to_all(back, "gx", 0, 0, tiled=True)

    tables = (plan.inverse_y(), plan.swap(-1.0))
    second, inverse_table, inverse_swap = call(
        functools.partial(conv_middle_body, plan),
        [shape((nx + 2, ny + 4, CP, LANES), F32)] + [shape(t.shape, BF16) for t in tables],
        (back, near, far, partial_own, filters) + tables,
        scratch=[
            pltpu.VMEM((nx + 6, 3 * CP, wide), F32),
            pltpu.VMEM((nx + 4, ny + 4, CP, LANES), F32),
            pltpu.SemaphoreType.DMA((2,)),
        ],
        specs=[ANY, PLAIN, PLAIN, FAR, PLAIN, HBM, HBM],
        out_specs=[PLAIN, VMEM, VMEM],
        vmem=8,
        flops=6e9,
    )
    if not split:
        line = jnp.transpose(line, (1, 0, 2, 3)).reshape(1, cg, plan.my, LANES)
    own, *messages = call(
        functools.partial(inverse_y_body, plan),
        [chunk] * devices_y,
        (line, inverse_table, inverse_swap),
        scratch=[pltpu.VMEM((devices_y, part, LANES), BF16)],
    )
    arrived = [ring(m, "gy", s + 1) for s, m in enumerate(messages)]
    tables = (features, lift, plan.regroup(devices_y, plan.groups), plan.inverse_z())
    third, *tables = call(
        functools.partial(conv_last_body, plan),
        [shape((nx, 2 * ny, CP, cz), BF16)] + [shape(t.shape, BF16) for t in tables],
        (own, second, filters) + tables,
        scratch=[
            pltpu.VMEM((nx + 2, 3 * CP, ny * LANES), F32), pltpu.SemaphoreType.DMA((4,))
        ],
        specs=[ANY, PLAIN, PLAIN] + [HBM] * 4,
        out_specs=[PLAIN] + [VMEM] * 4,
        flops=3e9,
    )
    near = lambda array: pltpu.with_memory_space_constraint(array, pltpu.VMEM)
    field, lift, regroup, inverse_z = (near(t) for t in tables)

    return call(
        functools.partial(final_body, plan),
        shape(features.shape, BF16),
        (field, third, lift, regroup, inverse_z, own, *arrived),
        pin=False,
        grid=(nx,),
        specs=[VMEM] * (5 + devices_y),
        out_specs=[pl.BlockSpec((channels, 2, cy, cz), lambda s: (0, s, 0, 0))],
        scratch=[
            pltpu.VMEM((devices_y, part, LANES), BF16),
            pltpu.VMEM((channels * cy, devices_y * plan.unit), BF16),
        ],
        vmem=12,
    )


def solution(mesh):
    in_specs = (P(None, ("grp", "gx"), "gy", None), P(None, None, None, "gy", "gx", None), P(), P())
    out_specs = P(None, ("grp", "gx"), "gy", None)
    return jax.shard_map(
        on_device, mesh=mesh, in_specs=in_specs, out_specs=out_specs, check_vma=False
    )
```

```python
import functools
import math

import jax
import jax.numpy as jnp
import numpy as np
from jax import lax
from jax.experimental import pallas as pl
from jax.experimental.pallas import tpu as pltpu
from jax.sharding import PartitionSpec as P

LANES = 128
CP = 24
BF16 = jnp.bfloat16
F32 = jnp.float32
MIB = 1024 * 1024


def dot(left, right):
    return jnp.dot(left, right, preferred_element_type=F32)


def signed_modes(count):
    position = np.arange(count)
    return np.where(position < count // 2, position, position - count)


def phase(frequency, length):
    index = np.mod(frequency[:, None] * np.arange(length)[None, :], length)
    angle = index.astype(np.float32) * np.float32(2.0 * math.pi / length)
    return (
        np.cos(angle).astype(BF16).astype(np.float32),
        np.sin(angle).astype(BF16).astype(np.float32),
    )


def const(array):
    return np.asarray(array, np.float32).astype(BF16)


class Plan:
    def __init__(self, features, spectral_weight, devices_x, devices_y):
        self.channels, self.cx, self.cy, self.cz = features
        self.dx, self.dy = devices_x, devices_y
        self.kz, self.ky, self.kx = spectral_weight[3:]
        self.gx, self.gy = self.cx * self.dx, self.cy * self.dy
        self.my = self.ky * self.dx
        self.mz = self.kz * self.dy
        self.unit = 2 * self.kz * self.cx
        self.groups = LANES // self.unit
        self.cg = self.channels // self.groups

    def forward_z(self):
        cos, sin = phase(np.arange(self.mz), self.cz)
        table = np.stack([cos, -sin], 0).reshape(2, self.dy, self.kz, self.cz)
        out = np.einsum("pdkz,xw->xzdpkw", table, np.eye(self.cx))
        return const(out.reshape(self.cx * self.cz, self.dy * self.unit))

    def inverse_z(self):
        cos, sin = phase(np.arange(self.mz), self.cz)
        scale = np.where(np.arange(self.mz) == 0, 1.0, 2.0) / float(self.gx * self.gy * self.cz)
        table = np.stack([cos, -sin], 0) * scale[None, :, None]
        table = table.reshape(2, self.dy, self.kz, self.cz)
        out = np.einsum("pdkz,xw->dpkxwz", table, np.eye(self.cx))
        return const(out.reshape(self.dy * self.unit, self.cx * self.cz))

    def regroup(self, outer, inner):
        out = np.einsum("ac,bd,lm->abldcm", np.eye(outer), np.eye(inner), np.eye(self.unit))
        size = outer * inner * self.unit
        return const(out.reshape(size, size))

    def swap(self, sign):
        turn = np.array([[0.0, -sign], [sign, 0.0]])
        half = self.unit // 2
        return const(np.kron(np.eye(self.groups), np.kron(turn, np.eye(half))))

    def forward_y(self):
        cos, sin = phase(signed_modes(self.my), self.gy)
        return const(np.concatenate([cos, sin], 1))

    def inverse_y(self):
        cos, sin = phase(signed_modes(self.my), self.gy)
        return const(np.concatenate([cos.T, sin.T], 1))

    def turn_x(self, sign):
        cos, sin = phase(signed_modes(self.kx), self.gx)
        turn = np.stack([np.stack([cos, -sign * sin]), np.stack([sign * sin, cos])])
        return turn.reshape(2, 2, self.kx, self.dx, self.cx)

    def forward_x(self):
        out = np.einsum("pqjsx,g,kl->sgpkxqlj", self.turn_x(1.0), np.ones(self.groups), np.eye(self.kz))
        return const(out.reshape(self.dx * LANES, self.kz * 2 * self.kx))

    def inverse_x(self):
        out = np.einsum("pqjsx,h,kl->pkjshqlx", self.turn_x(-1.0), np.ones(self.groups), np.eye(self.kz))
        return const(out.reshape(self.kz * 2 * self.kx, self.dx * LANES))


VMEM = pl.BlockSpec(memory_space=pltpu.VMEM)
PLAIN = pl.BlockSpec(memory_space=pltpu.VMEM)
FAR = pl.BlockSpec(memory_space=pltpu.VMEM)


ANY = pl.BlockSpec(memory_space=pl.ANY)
HBM = pl.BlockSpec(memory_space=pltpu.HBM)


def pinned(value, spec):
    if spec is HBM or spec is FAR:
        return pltpu.with_memory_space_constraint(jnp.asarray(value), pltpu.HBM)
    if spec is ANY or spec is PLAIN or isinstance(value, np.ndarray):
        return value
    return pltpu.with_memory_space_constraint(value, pltpu.VMEM)


def call(
    body, outs, inputs, scratch=(), specs=None, out_specs=None, vmem=8, flops=1e9, moved=1e6,
    pin=True, **kw,
):
    single = not isinstance(outs, (tuple, list))
    outs = [outs] if single else list(outs)
    specs = specs or [VMEM] * len(inputs)
    out_specs = out_specs or [VMEM] * len(outs)
    if pin:
        inputs = [pinned(value, spec) for value, spec in zip(inputs, specs)]
        outs = [
            pltpu.VMEM(o.shape, o.dtype)
            if spec is VMEM
            else pltpu.HBM(o.shape, o.dtype) if spec is FAR else o
            for o, spec in zip(outs, out_specs)
        ]
    result = pl.pallas_call(
        body,
        out_shape=outs,
        in_specs=specs,
        out_specs=out_specs,
        scratch_shapes=scratch,
        compiler_params=pltpu.CompilerParams(vmem_limit_bytes=vmem * MIB),
        cost_estimate=pl.CostEstimate(
            flops=int(flops), bytes_accessed=int(moved), transcendentals=0
        ),
        **kw,
    )(*inputs)
    return result[0] if single else result


def turn(index, shift, count):
    return lax.rem(index + shift + count, count)


def first_body(
    plan, field_in, table_in, regroup_in, rows_in, pair_in, ytable_in, swap_in, *rest
):
    own, low_message, high_message, *rest = rest
    middle = rest[: plan.dy - 3]
    coarse, ytable, swap, field, table, regroup, rows_table, pair_table, chunks, sems = rest[
        plan.dy - 3 :
    ]
    middle_channel = plan.channels // 2
    lower = pl.ds(0, middle_channel)
    upper = pl.ds(middle_channel, plan.channels - middle_channel)
    sources = (
        table_in, field_in.at[lower], field_in.at[upper],
        regroup_in, rows_in, pair_in, ytable_in, swap_in,
    )
    targets = (
        table, field.at[lower], field.at[upper], regroup, rows_table, pair_table, ytable, swap
    )
    copies = [
        pltpu.make_async_copy(s, t, sems.at[n]) for n, (s, t) in enumerate(zip(sources, targets))
    ]
    for copy in copies:
        copy.start()
    copies[0].wait()
    pieces = []
    for n, (low, high) in enumerate(((0, middle_channel), (middle_channel, plan.channels))):
        copies[1 + n].wait()
        rows = (high - low) * plan.cy
        lhs = jnp.concatenate(
            [field[low:high, x].reshape(rows, plan.cz) for x in range(plan.cx)], axis=1
        )
        pieces.append(dot(lhs, table[...]).astype(BF16))
    modes = jnp.concatenate(pieces, axis=0)
    copies[3].wait()
    part = plan.cg * plan.cy
    lanes = jnp.concatenate(
        [modes[g * part : (g + 1) * part] for g in range(plan.groups)], axis=1
    )
    result = dot(lanes, regroup[...]).astype(BF16)
    for d in range(plan.dy):
        chunks[d] = result[:, d * LANES : (d + 1) * LANES]
    for copy in copies[4:]:
        copy.wait()
    pool_body(plan, field, rows_table, pair_table, coarse)
    here = lax.axis_index("gy")
    own[...] = chunks[here]
    low_message[:part] = chunks[turn(here, 1, plan.dy)]
    high_message[:part] = chunks[turn(here, plan.dy - 1, plan.dy)]
    for s, message in enumerate(middle):
        message[...] = chunks[turn(here, s + 2, plan.dy)]
    tiles = plan.cy // 4
    index = 0
    for x in range(plan.cx // 2):
        for j in range(2):
            at = slice(part + index * CP, part + (index + 1) * CP)
            low_message[at] = coarse[x, tiles - 2 + j]
            high_message[at] = coarse[x, j]
            index += 1


def y_transform(plan, line, table, swap):
    columns = []
    for value in line:
        turned = dot(value, swap[...]).astype(BF16)
        columns.append(jnp.concatenate([value, turned], axis=0))
    return dot(table[...], jnp.concatenate(columns, axis=1)).astype(BF16)


def forward_y_body(plan, own, low_message, high_message, *rest):
    middle = rest[: plan.dy - 3]
    coarse, table, swap, out, near, far, volume, line = rest[plan.dy - 3 :]
    part = plan.cg * plan.cy
    here = lax.axis_index("gy")
    line[here] = own[...]
    line[turn(here, -1, plan.dy)] = low_message[:part]
    line[turn(here, 1, plan.dy)] = high_message[:part]
    for s, message in enumerate(middle):
        line[turn(here, -(s + 2), plan.dy)] = message[...]
    values = [
        jnp.concatenate(
            [line[s, c * plan.cy : (c + 1) * plan.cy] for s in range(plan.dy)], axis=0
        )
        for c in range(plan.cg)
    ]
    result = y_transform(plan, values, table, swap)
    targets, _, rows_out, _ = out.shape
    for d in range(targets):
        for c in range(plan.cg):
            out[d, c] = result[
                d * rows_out : (d + 1) * rows_out, c * LANES : (c + 1) * LANES
            ]
    nx = plan.cx // 2
    tiles = plan.cy // 4
    for x in range(nx):
        for j in range(2):
            at = slice(part + (x * 2 + j) * CP, part + (x * 2 + j + 1) * CP)
            none = jnp.zeros((CP, LANES), BF16)
            volume[x, j] = jnp.where(here > 0, low_message[at], none)
            volume[x, 2 + tiles + j] = jnp.where(here < plan.dy - 1, high_message[at], none)
        for j in range(tiles):
            volume[x, 2 + j] = coarse[x, j]
    even = lax.rem(lax.axis_index("gx"), 2) == 0
    first_plane = jnp.where(even, nx - 3, 0)
    last_plane = jnp.where(even, 0, nx - 3)
    for x in range(3):
        near[x] = volume[first_plane + x]
        far[x] = volume[last_plane + x]


def inverse_y_body(plan, line, table, swap, own, *rest):
    messages = rest[: plan.dy - 1]
    chunks = rest[plan.dy - 1]
    sources = line.shape[0]
    values = [
        jnp.concatenate([line[s, c] for s in range(sources)], axis=0) for c in range(plan.cg)
    ]
    result = y_transform(plan, values, table, swap)
    for d in range(plan.dy):
        for c in range(plan.cg):
            chunks[d, c * plan.cy : (c + 1) * plan.cy] = result[
                d * plan.cy : (d + 1) * plan.cy, c * LANES : (c + 1) * LANES
            ]
    here = lax.axis_index("gy")
    own[...] = chunks[here]
    for s, message in enumerate(messages):
        message[...] = chunks[turn(here, s + 1, plan.dy)]


def mix(plan, spec, weight, mixed):
    def step(o, carry):
        for k in range(plan.kz):
            real = jnp.zeros((plan.ky, plan.kx), F32)
            imag = jnp.zeros((plan.ky, plan.kx), F32)
            for i in range(plan.channels):
                wr = weight[0, i, o, k]
                wi = weight[1, i, o, k]
                xr = spec[0, k, i]
                xi = spec[1, k, i]
                real += xr * wr - xi * wi
                imag += xr * wi + xi * wr
            mixed[k, o] = jnp.concatenate([real, imag], axis=1)
        return carry

    lax.fori_loop(0, plan.channels, step, 0)


def weight_copy(weight, held, sems, begin, n):
    return pltpu.make_async_copy(weight.at[:, begin + n], held.at[n], sems.at[n])


def start_weights(weight, held, sems, begin):
    def one(n, carry):
        weight_copy(weight, held, sems, begin, n).start()
        return carry

    lax.fori_loop(0, held.shape[0], one, 0)


def pack_weights(plan, weight, held, sems, begin, packed):
    def one(n, carry):
        weight_copy(weight, held, sems, begin, n).wait()
        for p in range(2):
            for o in range(plan.channels):
                packed[n, p, o] = jnp.concatenate(
                    [held[n, p, o, k] for k in range(plan.kz)], axis=1
                ).astype(BF16)
        return carry

    lax.fori_loop(0, held.shape[0], one, 0)


def early_body(plan, after, weight, packed, held, sems):
    start_weights(weight, held, sems, 0)
    pack_weights(plan, weight, held, sems, 0, packed)


def window_body(
    plan, begin, after, volume, filters, point, weight, forward_in, inverse_in,
    packed, partial, lift, forward, inverse, held, sems, table_sems,
):
    copies = prefetches((forward_in, inverse_in), (forward, inverse), table_sems)
    for copy in copies:
        copy.start()
    start_weights(weight, held, sems, begin)
    conv_own_body(plan, volume, filters, point, partial, lift)
    pack_weights(plan, weight, held, sems, begin, packed)
    for copy in copies:
        copy.wait()


def lane_group(plan, shape):
    return (lax.broadcasted_iota(jnp.int32, shape, 1) % LANES) // plan.unit


def by_group(plan, lanes):
    owner = lane_group(plan, lanes.shape)
    return jnp.concatenate(
        [jnp.where(owner == g, lanes, jnp.zeros_like(lanes)) for g in range(plan.groups)], axis=0
    )


def one_group(plan, stacked):
    rows = stacked.shape[0] // plan.groups
    owner = lane_group(plan, (rows, stacked.shape[1]))
    result = stacked[:rows]
    for g in range(1, plan.groups):
        result = jnp.where(owner == g, stacked[g * rows : (g + 1) * rows], result)
    return result


def x_body(
    plan, pencil, forward, packed_early, packed_late, inverse, weight, out,
    packed, sems, held, held_sems, spec, mixed,
):
    early = packed_early.shape[0]
    ready = packed.shape[0]
    copies = [
        pltpu.make_async_copy(packed_early, packed.at[pl.ds(0, early)], sems.at[0]),
        pltpu.make_async_copy(packed_late, packed.at[pl.ds(early, ready - early)], sems.at[1]),
    ]
    for copy in copies:
        copy.start()
    start_weights(weight, held, held_sems, ready)
    rows = plan.cg * plan.ky
    wide = plan.kz * plan.kx
    lhs = jnp.concatenate([pencil[s].reshape(rows, LANES) for s in range(plan.dx)], axis=1)
    spectrum = dot(by_group(plan, lhs), forward[...])
    for g in range(plan.groups):
        for p in range(2):
            modes = spectrum[g * rows : (g + 1) * rows, p * wide : (p + 1) * wide]
            spec[p, g * plan.cg : (g + 1) * plan.cg] = modes.reshape(plan.cg, plan.ky, wide)

    def step(o, carry):
        real = jnp.zeros((plan.ky, wide), F32)
        imag = jnp.zeros((plan.ky, wide), F32)
        for i in range(ready):
            wr = packed[i, 0, o].astype(F32)
            wi = packed[i, 1, o].astype(F32)
            xr = spec[0, i]
            xi = spec[1, i]
            real += xr * wr - xi * wi
            imag += xr * wi + xi * wr
        mixed[0, o] = real
        mixed[1, o] = imag
        return carry

    def streamed(n, carry):
        weight_copy(weight, held, held_sems, ready, n).wait()
        xr = spec[0, ready + n]
        xi = spec[1, ready + n]
        for o in range(plan.channels):
            wr, wi = (
                jnp.concatenate([held[n, p, o, k] for k in range(plan.kz)], axis=1)
                for p in range(2)
            )
            mixed[0, o] += xr * wr - xi * wi
            mixed[1, o] += xr * wi + xi * wr
        return carry

    for copy in copies:
        copy.wait()
    lax.fori_loop(0, plan.channels, step, 0, unroll=2)
    lax.fori_loop(0, plan.channels - ready, streamed, 0)
    back = jnp.concatenate(
        [
            jnp.concatenate(
                [
                    mixed[p, g * plan.cg : (g + 1) * plan.cg].reshape(rows, wide).astype(BF16)
                    for p in range(2)
                ],
                axis=1,
            )
            for g in range(plan.groups)
        ],
        axis=0,
    )
    result = one_group(plan, dot(back, inverse[...])).astype(BF16)
    for d in range(plan.dx):
        out[d] = result[:, d * LANES : (d + 1) * LANES].reshape(plan.cg, plan.ky, LANES)


def x_stage_general(plan, pencil, weight):
    groups, cg, ky, kz, kx = plan.groups, plan.cg, plan.ky, plan.kz, plan.kx
    lhs = jnp.transpose(pencil, (1, 2, 0, 3)).reshape(cg * ky, plan.dx * LANES)
    spectrum = dot(by_group(plan, lhs), plan.forward_x()).reshape(groups, cg, ky, 2, kz, kx)
    spectrum = jnp.transpose(spectrum, (3, 4, 0, 1, 2, 5)).reshape(2, kz, groups * cg, ky, kx)
    mixed = call(
        functools.partial(mix, plan),
        jax.ShapeDtypeStruct((kz, groups * cg, ky, 2 * kx), F32),
        (spectrum, weight),
        vmem=32,
        pin=False,
    )
    back = jnp.transpose(mixed.reshape(kz, groups, cg, ky, 2, kx), (1, 2, 3, 4, 0, 5))
    back = back.reshape(groups * cg * ky, kz * 2 * kx).astype(BF16)
    back = one_group(plan, dot(back, plan.inverse_x())).astype(BF16)
    back = back.reshape(cg, ky, plan.dx, LANES)
    return jnp.transpose(back, (2, 0, 1, 3))


def gelu(value):
    return 0.5 * value * (1.0 + lax.erf(value * (0.5**0.5)))


def pool_tables(plan):
    half = plan.cy // 2
    quarter = half // 2
    rows = np.einsum(
        "cC,yY->ycCY", np.eye(CP)[:, : plan.channels], np.kron(np.eye(quarter), np.ones((1, 2)))
    ).reshape(quarter * CP, plan.channels * half)
    rows = np.concatenate([rows, rows], 1)
    pairs = np.kron(np.eye(plan.cz), np.full((2, 1), 0.125))
    return const(rows), const(pairs)


def pool_body(plan, field, rows_table, pair_table, out):
    half = plan.cy // 2
    quarter = half // 2
    cells = plan.channels * half
    for h in range(2):
        columns = []
        for x in range(plan.cx // 2):
            columns.append(
                jnp.concatenate(
                    [
                        field[:, 2 * x + e, h * half : (h + 1) * half].reshape(cells, plan.cz)
                        for e in range(2)
                    ],
                    axis=0,
                )
            )
        summed = dot(rows_table[...], jnp.concatenate(columns, axis=1))
        blocks = []
        for x in range(plan.cx // 2):
            for j in range(quarter // 2):
                blocks.append(
                    jnp.concatenate(
                        [
                            summed[
                                (2 * j + e) * CP : (2 * j + e + 1) * CP,
                                x * plan.cz : (x + 1) * plan.cz,
                            ]
                            for e in range(2)
                        ],
                        axis=1,
                    )
                )
        block = jnp.concatenate(blocks, axis=0)
        high = block.astype(BF16)
        low = (block - high.astype(F32)).astype(BF16)
        result = dot(high, pair_table[...]) + dot(low, pair_table[...])
        index = 0
        for x in range(plan.cx // 2):
            for j in range(quarter // 2):
                out[x, h * (quarter // 2) + j] = result[index * CP : (index + 1) * CP].astype(BF16)
                index += 1


def tap_columns(volume, x, tiles):
    lane = lax.broadcasted_iota(jnp.int32, (CP, LANES), 1)
    z = lane % (LANES // 2)
    lower = lane < LANES // 2
    shifted = {}
    for j in range(tiles[0] - 1, tiles[1] + 1):
        value = volume[x, j].astype(F32)
        versions = (
            jnp.where(z == 0, 0.0, pltpu.roll(value, 1, 1)),
            value,
            jnp.where(z == LANES // 2 - 1, 0.0, pltpu.roll(value, LANES - 1, 1)),
        )
        shifted[j] = (versions, [pltpu.roll(v, LANES // 2, 1) for v in versions])
    columns = []
    for j in range(tiles[0], tiles[1]):
        pieces = []
        for e in range(3):
            pieces.append(jnp.where(lower, shifted[j - 1][1][e], shifted[j][1][e]))
        for e in range(3):
            pieces.append(shifted[j][0][e])
        for e in range(3):
            pieces.append(jnp.where(lower, shifted[j][1][e], shifted[j + 1][1][e]))
        columns.append(jnp.concatenate(pieces, axis=0).astype(BF16))
    return jnp.concatenate(columns, axis=1)


def combined(partial, x, cols):
    return (
        partial[x, 0:CP, cols]
        + partial[x + 1, CP : 2 * CP, cols]
        + partial[x + 2, 2 * CP : 3 * CP, cols]
    )


def activate(plan, planes, tiles, partial, volume):
    nx = plan.cx // 2
    ny = plan.cy // 4
    here_x = lax.axis_index("gx")
    here_y = lax.axis_index("gy")
    one = jnp.float32(1.0)
    zero = jnp.float32(0.0)
    below_x = jnp.where(here_x > 0, one, zero)
    above_x = jnp.where(here_x < plan.dx - 1, one, zero)
    below_y = jnp.where(here_y > 0, one, zero)
    above_y = jnp.where(here_y < plan.dy - 1, one, zero)
    margin = (planes - nx) // 2

    def body(x, carry):
        inside = jnp.where(x < margin, below_x, one) * jnp.where(x >= margin + nx, above_x, one)
        for j in range(tiles[0], tiles[1]):
            cols = slice((j - tiles[0]) * LANES, (j - tiles[0] + 1) * LANES)
            scale = inside
            if j < 2:
                scale = scale * below_y
            if j >= 2 + ny:
                scale = scale * above_y
            value = gelu(combined(partial, x, cols)) * scale
            volume[x, j] = value.astype(volume.dtype)
        return carry

    lax.fori_loop(0, planes, body, 0, unroll=2)


def where_bf16(mask):
    return jnp.where(mask, 1.0, 0.0).astype(BF16)


def iota(shape, dim):
    return lax.broadcasted_iota(jnp.int32, shape, dim)


def make_lift(plan, point, lift):
    half = plan.cy // 2
    cells = plan.channels * half
    tall = (cells, plan.channels)
    flat = (plan.channels, cells)
    square = (cells, cells)
    pick_o = where_bf16(iota(tall, 0) // half == iota(tall, 1))
    pick_i = where_bf16(iota(flat, 1) // half == iota(flat, 0))
    expanded = dot(dot(pick_o, point[...]).astype(BF16), pick_i)
    diagonal = iota(square, 0) % half == iota(square, 1) % half
    lift[:, :cells] = jnp.where(diagonal, expanded, 0.0).astype(BF16)
    coarse = (cells, half // 2 * CP)
    row, col = iota(coarse, 0), iota(coarse, 1)
    lift[:, cells:] = where_bf16(
        (row // half == col % CP) & ((row % half) // 2 == col // CP)
    )


def conv_own_body(plan, volume_in, filters, point, partial, lift):
    nx = plan.cx // 2
    ny = plan.cy // 4
    make_lift(plan, point, lift)

    def body(x, carry):
        partial[x] = dot(filters[0], tap_columns(volume_in, x, (1, ny + 3)))
        return carry

    lax.fori_loop(0, nx, body, 0, unroll=2)


def prefetches(sources, targets, sems):
    return [
        pltpu.make_async_copy(s, t, sems.at[n]) for n, (s, t) in enumerate(zip(sources, targets))
    ]


def conv_middle_body(
    plan, after, near, far, own, filters, table_in, swap_in,
    second, table, swap, partial, volume, sems,
):
    copies = prefetches((table_in, swap_in), (table, swap), sems)
    for copy in copies:
        copy.start()
    nx = plan.cx // 2
    ny = plan.cy // 4
    wide = ny + 4
    tiles = (1, ny + 3)

    even = lax.rem(lax.axis_index("gx"), 2) == 0
    near_at = jnp.where(even, 3 + nx, 0)
    far_at = jnp.where(even, 0, 3 + nx)

    def edges(x, carry):
        partial[near_at + x] = dot(filters[0], tap_columns(near, x, tiles))
        partial[far_at + x] = dot(filters[0], tap_columns(far, x, tiles))
        return carry

    lax.fori_loop(0, 3, edges, 0)
    for x in range(nx):
        partial[x + 3] = own[x]
    activate(plan, nx + 4, tiles, partial, volume)
    zero = jnp.zeros((CP, LANES), volume.dtype)
    for x in range(nx + 4):
        volume[x, 0] = zero
        volume[x, wide - 1] = zero

    def body(x, carry):
        partial[x] = dot(filters[1], tap_columns(volume, x, tiles))
        return carry

    lax.fori_loop(0, nx + 4, body, 0, unroll=2)
    activate(plan, nx + 2, tiles, partial, second)
    for copy in copies:
        copy.wait()


def conv_last_body(plan, after, second, filters, *rest):
    sources, third, targets, partial, sems = rest[:4], rest[4], rest[5:9], rest[9], rest[10]
    copies = prefetches(sources, targets, sems)
    for copy in copies:
        copy.start()
    nx = plan.cx // 2
    ny = plan.cy // 4
    tiles = (2, ny + 2)

    def body(x, carry):
        partial[x] = dot(filters[2], tap_columns(second, x, tiles))
        return carry

    lax.fori_loop(0, nx + 2, body, 0, unroll=True)

    square = (LANES, 2 * LANES)
    spread = where_bf16(iota(square, 1) // 2 == iota(square, 0))

    def up(x, carry):
        for j in range(ny):
            total = combined(partial, x, slice(j * LANES, (j + 1) * LANES))
            wide = dot(total.astype(BF16), spread).astype(BF16)
            third[x, 2 * j] = wide[:, : plan.cz]
            third[x, 2 * j + 1] = wide[:, plan.cz :]
        return carry

    lax.fori_loop(0, nx, up, 0, unroll=True)
    for copy in copies:
        copy.wait()


def final_body(plan, field, third, lift, regroup, inverse, own, *rest):
    messages = rest[: plan.dy - 1]
    out, line, lanes = rest[plan.dy - 1 :]
    step = pl.program_id(0)
    half = plan.cy // 2
    part = plan.cg * plan.cy

    @pl.when(step == 0)
    def _():
        here = lax.axis_index("gy")
        line[here] = own[...]
        for s, message in enumerate(messages):
            line[turn(here, -(s + 1), plan.dy)] = message[...]
        gathered = jnp.concatenate([line[s] for s in range(plan.dy)], axis=1)
        result = dot(gathered, regroup[...]).astype(BF16)
        width = plan.dy * plan.unit
        for g in range(plan.groups):
            lanes[g * part : (g + 1) * part] = result[:, g * width : (g + 1) * width]

    cells = plan.channels * half
    columns = []
    planes = out.shape[1]
    for e in range(planes):
        for h in range(2):
            cols = third[step * (planes // 2) + e // 2, h * (half // 2) : (h + 1) * (half // 2)]
            columns.append(
                jnp.concatenate(
                    [
                        field[:, planes * step + e, h * half : (h + 1) * half].reshape(cells, plan.cz),
                        cols.astype(F32).reshape(half // 2 * CP, plan.cz).astype(BF16),
                    ],
                    axis=0,
                )
            )
    local = dot(lift[...], jnp.concatenate(columns, axis=1))
    at = pl.multiple_of(step * planes * plan.cz, planes * plan.cz)
    spectral = dot(lanes[...], inverse[:, pl.ds(at, planes * plan.cz)]).reshape(
        plan.channels, plan.cy, planes * plan.cz
    )
    for e in range(planes):
        for h in range(2):
            index = e * 2 + h
            total = local[:, index * plan.cz : (index + 1) * plan.cz].reshape(
                plan.channels, half, plan.cz
            ) + spectral[:, h * half : (h + 1) * half, e * plan.cz : (e + 1) * plan.cz]
            out[:, e, h * half : (h + 1) * half] = gelu(total).astype(BF16)


def after(values, marker):
    return lax.optimization_barrier((values, marker))[0]


def ring(value, axis, shift):
    count = lax.axis_size(axis)
    return lax.ppermute(value, axis, [(i, (i + shift) % count) for i in range(count)])


def on_device(features, spectral_weight, conv_weight, point_weight):
    devices_x = lax.axis_size("gx")
    devices_y = lax.axis_size("gy")
    plan = Plan(features.shape, spectral_weight.shape, devices_x, devices_y)
    channels, cx, cy, cz = features.shape
    shape = jax.ShapeDtypeStruct
    cg = plan.cg
    nx, ny = cx // 2, cy // 4
    part = cg * cy
    split = plan.ky % 16 == 0 and plan.kz * plan.kx == LANES
    half = cy // 2

    rows_table, pair_table = pool_tables(plan)
    tables = (
        plan.forward_z(), plan.regroup(plan.groups, devices_y), rows_table, pair_table,
        plan.forward_y(), plan.swap(1.0),
    )
    chunk = shape((part, LANES), BF16)
    message = shape((part + nx * 2 * CP, LANES), BF16)
    outs = [chunk, message, message] + [chunk] * (devices_y - 3)
    outs += [shape((nx, ny, CP, cz), BF16)] + [shape(t.shape, BF16) for t in tables[4:]]
    if split:
        early, late = channels // 6, channels // 4
        pack = lambda n: shape((n, 2, channels, plan.ky, LANES), BF16)
        hold = lambda n: [
            pltpu.VMEM((n, 2) + spectral_weight.shape[2:], F32), pltpu.SemaphoreType.DMA((n,))
        ]
    first = call(
        functools.partial(first_body, plan),
        outs,
        (features,) + tables,
        scratch=[pltpu.VMEM(features.shape, BF16)]
        + [pltpu.VMEM(t.shape, BF16) for t in tables[:4]]
        + [pltpu.VMEM((devices_y, part, LANES), BF16), pltpu.SemaphoreType.DMA((8,))],
        specs=[HBM] * 7,
        vmem=16,
    )
    own, to_up, to_down = first[:3]
    middle = first[3:-3]
    coarse, y_table, y_swap = first[-3:]
    low_message = ring(to_up, "gy", 1)
    high_message = ring(to_down, "gy", -1)
    middle = [ring(m, "gy", s + 2) for s, m in enumerate(middle)]

    if split:
        packed_early = call(
            functools.partial(early_body, plan),
            pack(early),
            (own, spectral_weight),
            specs=[ANY, HBM],
            out_specs=[FAR],
            scratch=hold(early),
            moved=2e6,
        )
        own = after(own, packed_early)

    y_out = (devices_x, cg, plan.ky) if split else (1, cg, plan.my)
    planes = shape((3, ny + 4, CP, LANES), BF16)
    y_spec, near, far, volume = call(
        functools.partial(forward_y_body, plan),
        (shape(y_out + (LANES,), BF16), planes, planes, shape((nx, ny + 4, CP, LANES), BF16)),
        (own, low_message, high_message, *middle, coarse, y_table, y_swap),
        out_specs=[PLAIN, FAR, FAR, VMEM],
        scratch=[pltpu.VMEM((devices_y, part, LANES), BF16)],
    )
    if not split:
        y_spec = jnp.transpose(y_spec.reshape(cg, devices_x, plan.ky, LANES), (1, 0, 2, 3))
    pencil = lax.all_to_all(y_spec, "gx", 0, 0, tiled=True)

    filters = jnp.pad(
        conv_weight.reshape(3, 3, 9, channels, channels),
        ((0, 0), (0, 0), (0, 0), (0, CP - channels), (0, CP - channels)),
    )
    filters = jnp.transpose(filters, (0, 1, 3, 2, 4)).reshape(3, 3 * CP, 9 * CP)
    wide = (ny + 2) * LANES
    small = (
        shape((nx, 3 * CP, wide), F32),
        shape((channels * half, channels * half + half // 2 * CP), BF16),
    )
    local = (volume, filters, jnp.transpose(point_weight))
    if split:
        tables = (plan.forward_x(), plan.inverse_x())
        packed_late, partial_own, lift, forward_x, inverse_x = call(
            functools.partial(window_body, plan, early),
            (pack(late),) + small + tuple(shape(t.shape, BF16) for t in tables),
            (y_spec,) + local + (spectral_weight,) + tables,
            specs=[ANY] + [VMEM, PLAIN, PLAIN] + [HBM] * 3,
            out_specs=[FAR, FAR, FAR, VMEM, VMEM],
            scratch=hold(late) + [pltpu.SemaphoreType.DMA((2,))],
            vmem=12,
            flops=4e9,
            moved=8e6,
        )
    else:
        partial_own, lift = call(
            functools.partial(conv_own_body, plan),
            small,
            local,
            specs=[VMEM, PLAIN, PLAIN],
            out_specs=[FAR, FAR],
            flops=2e9,
        )
    near, far = after((near, far), partial_own)
    pairs = [(i, i ^ 1) for i in range(devices_x)]
    near = lax.ppermute(near, "gx", pairs)
    pairs = [(i, i + 1) for i in range(1, devices_x - 1, 2)]
    far = lax.ppermute(far, "gx", pairs + [(t, s) for s, t in pairs])

    if split:
        back = call(
            functools.partial(x_body, plan),
            shape((devices_x, cg, plan.ky, LANES), BF16),
            (pencil, forward_x, packed_early, packed_late, inverse_x, spectral_weight),
            specs=[VMEM, VMEM, HBM, HBM, VMEM, HBM],
            out_specs=[PLAIN],
            scratch=[
                pltpu.VMEM((early + late, 2, channels, plan.ky, LANES), BF16),
                pltpu.SemaphoreType.DMA((2,)),
            ]
            + hold(channels - early - late)
            + [pltpu.VMEM((2, channels, plan.ky, LANES), F32)] * 2,
            vmem=20,
        )
    else:
        back = x_stage_general(plan, pencil, spectral_weight)
    line = lax.all_to_all(back, "gx", 0, 0, tiled=True)

    tables = (plan.inverse_y(), plan.swap(-1.0))
    second, inverse_table, inverse_swap = call(
        functools.partial(conv_middle_body, plan),
        [shape((nx + 2, ny + 4, CP, LANES), F32)] + [shape(t.shape, BF16) for t in tables],
        (back, near, far, partial_own, filters) + tables,
        scratch=[
            pltpu.VMEM((nx + 6, 3 * CP, wide), F32),
            pltpu.VMEM((nx + 4, ny + 4, CP, LANES), F32),
            pltpu.SemaphoreType.DMA((2,)),
        ],
        specs=[ANY, PLAIN, PLAIN, FAR, PLAIN, HBM, HBM],
        out_specs=[PLAIN, VMEM, VMEM],
        vmem=8,
        flops=6e9,
    )
    if not split:
        line = jnp.transpose(line, (1, 0, 2, 3)).reshape(1, cg, plan.my, LANES)
    own, *messages = call(
        functools.partial(inverse_y_body, plan),
        [chunk] * devices_y,
        (line, inverse_table, inverse_swap),
        scratch=[pltpu.VMEM((devices_y, part, LANES), BF16)],
    )
    arrived = [ring(m, "gy", s + 1) for s, m in enumerate(messages)]
    tables = (features, lift, plan.regroup(devices_y, plan.groups), plan.inverse_z())
    third, *tables = call(
        functools.partial(conv_last_body, plan),
        [shape((nx, 2 * ny, CP, cz), BF16)] + [shape(t.shape, BF16) for t in tables],
        (own, second, filters) + tables,
        scratch=[
            pltpu.VMEM((nx + 2, 3 * CP, ny * LANES), F32), pltpu.SemaphoreType.DMA((4,))
        ],
        specs=[ANY, PLAIN, PLAIN] + [HBM] * 4,
        out_specs=[PLAIN] + [VMEM] * 4,
        flops=3e9,
    )
    near = lambda array: pltpu.with_memory_space_constraint(array, pltpu.VMEM)
    field, lift, regroup, inverse_z = (near(t) for t in tables)

    return call(
        functools.partial(final_body, plan),
        shape(features.shape, BF16),
        (field, third, lift, regroup, inverse_z, own, *arrived),
        pin=False,
        grid=(nx // 2,),
        specs=[VMEM] * (5 + devices_y),
        out_specs=[pl.BlockSpec((channels, 4, cy, cz), lambda s: (0, s, 0, 0))],
        scratch=[
            pltpu.VMEM((devices_y, part, LANES), BF16),
            pltpu.VMEM((channels * cy, devices_y * plan.unit), BF16),
        ],
        vmem=12,
    )


def solution(mesh):
    in_specs = (P(None, ("grp", "gx"), "gy", None), P(None, None, None, "gy", "gx", None), P(), P())
    out_specs = P(None, ("grp", "gx"), "gy", None)
    return jax.shard_map(
        on_device, mesh=mesh, in_specs=in_specs, out_specs=out_specs, check_vma=False
    )
```

```python
import functools
import math

import jax
import jax.numpy as jnp
import numpy as np
from jax import lax
from jax.experimental import pallas as pl
from jax.experimental.pallas import tpu as pltpu
from jax.sharding import PartitionSpec as P

LANES = 128
CP = 24
TALL = 32
BF16 = jnp.bfloat16
F32 = jnp.float32
MIB = 1024 * 1024


def dot(left, right):
    return jnp.dot(left, right, preferred_element_type=F32)


def signed_modes(count):
    position = np.arange(count)
    return np.where(position < count // 2, position, position - count)


def phase(frequency, length):
    index = np.mod(frequency[:, None] * np.arange(length)[None, :], length)
    angle = index.astype(np.float32) * np.float32(2.0 * math.pi / length)
    return (
        np.cos(angle).astype(BF16).astype(np.float32),
        np.sin(angle).astype(BF16).astype(np.float32),
    )


def const(array):
    return np.asarray(array, np.float32).astype(BF16)


class Plan:
    def __init__(self, features, spectral_weight, devices_x, devices_y):
        self.channels, self.cx, self.cy, self.cz = features
        self.dx, self.dy = devices_x, devices_y
        self.kz, self.ky, self.kx = spectral_weight[3:]
        self.gx, self.gy = self.cx * self.dx, self.cy * self.dy
        self.my = self.ky * self.dx
        self.mz = self.kz * self.dy
        self.unit = 2 * self.kz * self.cx
        self.groups = LANES // self.unit
        self.cg = self.channels // self.groups

    def forward_z(self):
        cos, sin = phase(np.arange(self.mz), self.cz)
        table = np.stack([cos, -sin], 0).reshape(2, self.dy, self.kz, self.cz)
        out = np.einsum("pdkz,xw->xzdpkw", table, np.eye(self.cx))
        return const(out.reshape(self.cx * self.cz, self.dy * self.unit))

    def inverse_z(self):
        cos, sin = phase(np.arange(self.mz), self.cz)
        scale = np.where(np.arange(self.mz) == 0, 1.0, 2.0) / float(self.gx * self.gy * self.cz)
        table = np.stack([cos, -sin], 0) * scale[None, :, None]
        table = table.reshape(2, self.dy, self.kz, self.cz)
        out = np.einsum("pdkz,xw->dpkxwz", table, np.eye(self.cx))
        return const(out.reshape(self.dy * self.unit, self.cx * self.cz))

    def regroup(self, outer, inner):
        out = np.einsum("ac,bd,lm->abldcm", np.eye(outer), np.eye(inner), np.eye(self.unit))
        size = outer * inner * self.unit
        return const(out.reshape(size, size))

    def swap(self, sign):
        turn = np.array([[0.0, -sign], [sign, 0.0]])
        half = self.unit // 2
        return const(np.kron(np.eye(self.groups), np.kron(turn, np.eye(half))))

    def forward_y(self):
        cos, sin = phase(signed_modes(self.my), self.gy)
        return const(np.concatenate([cos, sin], 1))

    def inverse_y(self):
        cos, sin = phase(signed_modes(self.my), self.gy)
        return const(np.concatenate([cos.T, sin.T], 1))

    def turn_x(self, sign):
        cos, sin = phase(signed_modes(self.kx), self.gx)
        turn = np.stack([np.stack([cos, -sign * sin]), np.stack([sign * sin, cos])])
        return turn.reshape(2, 2, self.kx, self.dx, self.cx)

    def forward_x(self):
        out = np.einsum("pqjsx,g,kl->sgpkxqlj", self.turn_x(1.0), np.ones(self.groups), np.eye(self.kz))
        return const(out.reshape(self.dx * LANES, self.kz * 2 * self.kx))

    def inverse_x(self):
        out = np.einsum("pqjsx,h,kl->pkjshqlx", self.turn_x(-1.0), np.ones(self.groups), np.eye(self.kz))
        return const(out.reshape(self.kz * 2 * self.kx, self.dx * LANES))


VMEM = pl.BlockSpec(memory_space=pltpu.VMEM)
PLAIN = pl.BlockSpec(memory_space=pltpu.VMEM)
FAR = pl.BlockSpec(memory_space=pltpu.VMEM)


ANY = pl.BlockSpec(memory_space=pl.ANY)
HBM = pl.BlockSpec(memory_space=pltpu.HBM)


def pinned(value, spec):
    if spec is HBM or spec is FAR:
        return pltpu.with_memory_space_constraint(jnp.asarray(value), pltpu.HBM)
    if spec is ANY or spec is PLAIN or isinstance(value, np.ndarray):
        return value
    return pltpu.with_memory_space_constraint(value, pltpu.VMEM)


def call(
    body, outs, inputs, scratch=(), specs=None, out_specs=None, vmem=8, flops=1e9, moved=1e6,
    pin=True, **kw,
):
    single = not isinstance(outs, (tuple, list))
    outs = [outs] if single else list(outs)
    specs = specs or [VMEM] * len(inputs)
    out_specs = out_specs or [VMEM] * len(outs)
    if pin:
        inputs = [pinned(value, spec) for value, spec in zip(inputs, specs)]
        outs = [
            pltpu.VMEM(o.shape, o.dtype)
            if spec is VMEM
            else pltpu.HBM(o.shape, o.dtype) if spec is FAR else o
            for o, spec in zip(outs, out_specs)
        ]
    result = pl.pallas_call(
        body,
        out_shape=outs,
        in_specs=specs,
        out_specs=out_specs,
        scratch_shapes=scratch,
        compiler_params=pltpu.CompilerParams(vmem_limit_bytes=vmem * MIB),
        cost_estimate=pl.CostEstimate(
            flops=int(flops), bytes_accessed=int(moved), transcendentals=0
        ),
        **kw,
    )(*inputs)
    return result[0] if single else result


def turn(index, shift, count):
    return lax.rem(index + shift + count, count)


def taller(tile):
    none = jnp.zeros((TALL - CP, LANES), F32)
    return jnp.concatenate([tile.astype(F32), none], axis=0).astype(BF16)


def first_body(
    plan, field_in, table_in, regroup_in, rows_in, pair_in, ytable_in, swap_in, *rest
):
    own, low_message, high_message, *rest = rest
    middle = rest[: plan.dy - 3]
    coarse, ytable, swap, field, table, regroup, rows_table, pair_table, chunks, sems = rest[
        plan.dy - 3 :
    ]
    middle_channel = plan.channels // 2
    lower = pl.ds(0, middle_channel)
    upper = pl.ds(middle_channel, plan.channels - middle_channel)
    sources = (
        table_in, field_in.at[lower], field_in.at[upper],
        regroup_in, rows_in, pair_in, ytable_in, swap_in,
    )
    targets = (
        table, field.at[lower], field.at[upper], regroup, rows_table, pair_table, ytable, swap
    )
    copies = [
        pltpu.make_async_copy(s, t, sems.at[n]) for n, (s, t) in enumerate(zip(sources, targets))
    ]
    for copy in copies:
        copy.start()
    copies[0].wait()
    pieces = []
    for n, (low, high) in enumerate(((0, middle_channel), (middle_channel, plan.channels))):
        copies[1 + n].wait()
        rows = (high - low) * plan.cy
        lhs = jnp.concatenate(
            [field[low:high, x].reshape(rows, plan.cz) for x in range(plan.cx)], axis=1
        )
        pieces.append(dot(lhs, table[...]).astype(BF16))
    modes = jnp.concatenate(pieces, axis=0)
    copies[3].wait()
    part = plan.cg * plan.cy
    lanes = jnp.concatenate(
        [modes[g * part : (g + 1) * part] for g in range(plan.groups)], axis=1
    )
    result = dot(lanes, regroup[...]).astype(BF16)
    for d in range(plan.dy):
        chunks[d] = result[:, d * LANES : (d + 1) * LANES]
    for copy in copies[4:]:
        copy.wait()
    pool_body(plan, field, rows_table, pair_table, coarse)
    here = lax.axis_index("gy")
    own[...] = chunks[here]
    low_message[:part] = chunks[turn(here, 1, plan.dy)]
    high_message[:part] = chunks[turn(here, plan.dy - 1, plan.dy)]
    for s, message in enumerate(middle):
        message[...] = chunks[turn(here, s + 2, plan.dy)]
    tiles = plan.cy // 4
    index = 0
    for x in range(plan.cx // 2):
        for j in range(2):
            at = slice(part + index * TALL, part + (index + 1) * TALL)
            low_message[at] = taller(coarse[x, tiles - 2 + j])
            high_message[at] = taller(coarse[x, j])
            index += 1


def y_transform(plan, line, table, swap):
    columns = []
    for value in line:
        turned = dot(value, swap[...]).astype(BF16)
        columns.append(jnp.concatenate([value, turned], axis=0))
    return dot(table[...], jnp.concatenate(columns, axis=1)).astype(BF16)


def forward_y_body(plan, own, low_message, high_message, *rest):
    middle = rest[: plan.dy - 3]
    coarse, table, swap, out, near, far, volume, line = rest[plan.dy - 3 :]
    part = plan.cg * plan.cy
    here = lax.axis_index("gy")
    line[here] = own[...]
    line[turn(here, -1, plan.dy)] = low_message[:part]
    line[turn(here, 1, plan.dy)] = high_message[:part]
    for s, message in enumerate(middle):
        line[turn(here, -(s + 2), plan.dy)] = message[...]
    values = [
        jnp.concatenate(
            [line[s, c * plan.cy : (c + 1) * plan.cy] for s in range(plan.dy)], axis=0
        )
        for c in range(plan.cg)
    ]
    result = y_transform(plan, values, table, swap)
    targets, _, rows_out, _ = out.shape
    for d in range(targets):
        for c in range(plan.cg):
            out[d, c] = result[
                d * rows_out : (d + 1) * rows_out, c * LANES : (c + 1) * LANES
            ]
    nx = plan.cx // 2
    tiles = plan.cy // 4
    for x in range(nx):
        for j in range(2):
            at = slice(part + (x * 2 + j) * TALL, part + (x * 2 + j + 1) * TALL)
            low = low_message[at].astype(F32)[:CP]
            high = high_message[at].astype(F32)[:CP]
            volume[x, j] = jnp.where(here > 0, low, 0.0).astype(BF16)
            volume[x, 2 + tiles + j] = jnp.where(here < plan.dy - 1, high, 0.0).astype(BF16)
        for j in range(tiles):
            volume[x, 2 + j] = coarse[x, j]
    even = lax.rem(lax.axis_index("gx"), 2) == 0
    first_plane = jnp.where(even, nx - 3, 0)
    last_plane = jnp.where(even, 0, nx - 3)
    for x in range(3):
        near[x] = volume[first_plane + x]
        far[x] = volume[last_plane + x]


def inverse_y_body(plan, line, table, swap, own, *rest):
    messages = rest[: plan.dy - 1]
    chunks = rest[plan.dy - 1]
    sources = line.shape[0]
    values = [
        jnp.concatenate([line[s, c] for s in range(sources)], axis=0) for c in range(plan.cg)
    ]
    result = y_transform(plan, values, table, swap)
    for d in range(plan.dy):
        for c in range(plan.cg):
            chunks[d, c * plan.cy : (c + 1) * plan.cy] = result[
                d * plan.cy : (d + 1) * plan.cy, c * LANES : (c + 1) * LANES
            ]
    here = lax.axis_index("gy")
    own[...] = chunks[here]
    for s, message in enumerate(messages):
        message[...] = chunks[turn(here, s + 1, plan.dy)]


def mix(plan, spec, weight, mixed):
    def step(o, carry):
        for k in range(plan.kz):
            real = jnp.zeros((plan.ky, plan.kx), F32)
            imag = jnp.zeros((plan.ky, plan.kx), F32)
            for i in range(plan.channels):
                wr = weight[0, i, o, k]
                wi = weight[1, i, o, k]
                xr = spec[0, k, i]
                xi = spec[1, k, i]
                real += xr * wr - xi * wi
                imag += xr * wi + xi * wr
            mixed[k, o] = jnp.concatenate([real, imag], axis=1)
        return carry

    lax.fori_loop(0, plan.channels, step, 0)


def weight_copy(weight, held, sems, begin, n):
    return pltpu.make_async_copy(weight.at[:, begin + n], held.at[n], sems.at[n])


def start_weights(weight, held, sems, begin):
    def one(n, carry):
        weight_copy(weight, held, sems, begin, n).start()
        return carry

    lax.fori_loop(0, held.shape[0], one, 0)


def pack_weights(plan, weight, held, sems, begin, packed):
    def one(n, carry):
        weight_copy(weight, held, sems, begin, n).wait()
        for p in range(2):
            for o in range(plan.channels):
                packed[n, p, o] = jnp.concatenate(
                    [held[n, p, o, k] for k in range(plan.kz)], axis=1
                ).astype(BF16)
        return carry

    lax.fori_loop(0, held.shape[0], one, 0)


def early_body(plan, after, weight, packed, held, sems):
    start_weights(weight, held, sems, 0)
    pack_weights(plan, weight, held, sems, 0, packed)


def window_body(
    plan, begin, after, volume, filters, point, weight, forward_in, inverse_in,
    packed, partial, lift, forward, inverse, held, sems, table_sems,
):
    copies = prefetches((forward_in, inverse_in), (forward, inverse), table_sems)
    for copy in copies:
        copy.start()
    start_weights(weight, held, sems, begin)
    conv_own_body(plan, volume, filters, point, partial, lift)
    pack_weights(plan, weight, held, sems, begin, packed)
    for copy in copies:
        copy.wait()


def lane_group(plan, shape):
    return (lax.broadcasted_iota(jnp.int32, shape, 1) % LANES) // plan.unit


def by_group(plan, lanes):
    owner = lane_group(plan, lanes.shape)
    return jnp.concatenate(
        [jnp.where(owner == g, lanes, jnp.zeros_like(lanes)) for g in range(plan.groups)], axis=0
    )


def one_group(plan, stacked):
    rows = stacked.shape[0] // plan.groups
    owner = lane_group(plan, (rows, stacked.shape[1]))
    result = stacked[:rows]
    for g in range(1, plan.groups):
        result = jnp.where(owner == g, stacked[g * rows : (g + 1) * rows], result)
    return result


def x_body(
    plan, pencil, forward, packed_early, packed_late, inverse, weight, out,
    packed, sems, held, held_sems, spec, mixed,
):
    early = packed_early.shape[0]
    ready = packed.shape[0]
    copies = [
        pltpu.make_async_copy(packed_early, packed.at[pl.ds(0, early)], sems.at[0]),
        pltpu.make_async_copy(packed_late, packed.at[pl.ds(early, ready - early)], sems.at[1]),
    ]
    for copy in copies:
        copy.start()
    start_weights(weight, held, held_sems, ready)
    rows = plan.cg * plan.ky
    wide = plan.kz * plan.kx
    lhs = jnp.concatenate([pencil[s].reshape(rows, LANES) for s in range(plan.dx)], axis=1)
    spectrum = dot(by_group(plan, lhs), forward[...])
    for g in range(plan.groups):
        for p in range(2):
            modes = spectrum[g * rows : (g + 1) * rows, p * wide : (p + 1) * wide]
            spec[p, g * plan.cg : (g + 1) * plan.cg] = modes.reshape(plan.cg, plan.ky, wide)

    def step(o, carry):
        real = jnp.zeros((plan.ky, wide), F32)
        imag = jnp.zeros((plan.ky, wide), F32)
        for i in range(ready):
            wr = packed[i, 0, o].astype(F32)
            wi = packed[i, 1, o].astype(F32)
            xr = spec[0, i]
            xi = spec[1, i]
            real += xr * wr - xi * wi
            imag += xr * wi + xi * wr
        mixed[0, o] = real
        mixed[1, o] = imag
        return carry

    def streamed(n, carry):
        weight_copy(weight, held, held_sems, ready, n).wait()
        xr = spec[0, ready + n]
        xi = spec[1, ready + n]
        for o in range(plan.channels):
            wr, wi = (
                jnp.concatenate([held[n, p, o, k] for k in range(plan.kz)], axis=1)
                for p in range(2)
            )
            mixed[0, o] += xr * wr - xi * wi
            mixed[1, o] += xr * wi + xi * wr
        return carry

    for copy in copies:
        copy.wait()
    lax.fori_loop(0, plan.channels, step, 0, unroll=2)
    lax.fori_loop(0, plan.channels - ready, streamed, 0)
    back = jnp.concatenate(
        [
            jnp.concatenate(
                [
                    mixed[p, g * plan.cg : (g + 1) * plan.cg].reshape(rows, wide).astype(BF16)
                    for p in range(2)
                ],
                axis=1,
            )
            for g in range(plan.groups)
        ],
        axis=0,
    )
    result = one_group(plan, dot(back, inverse[...])).astype(BF16)
    for d in range(plan.dx):
        out[d] = result[:, d * LANES : (d + 1) * LANES].reshape(plan.cg, plan.ky, LANES)


def x_stage_general(plan, pencil, weight):
    groups, cg, ky, kz, kx = plan.groups, plan.cg, plan.ky, plan.kz, plan.kx
    lhs = jnp.transpose(pencil, (1, 2, 0, 3)).reshape(cg * ky, plan.dx * LANES)
    spectrum = dot(by_group(plan, lhs), plan.forward_x()).reshape(groups, cg, ky, 2, kz, kx)
    spectrum = jnp.transpose(spectrum, (3, 4, 0, 1, 2, 5)).reshape(2, kz, groups * cg, ky, kx)
    mixed = call(
        functools.partial(mix, plan),
        jax.ShapeDtypeStruct((kz, groups * cg, ky, 2 * kx), F32),
        (spectrum, weight),
        vmem=32,
        pin=False,
    )
    back = jnp.transpose(mixed.reshape(kz, groups, cg, ky, 2, kx), (1, 2, 3, 4, 0, 5))
    back = back.reshape(groups * cg * ky, kz * 2 * kx).astype(BF16)
    back = one_group(plan, dot(back, plan.inverse_x())).astype(BF16)
    back = back.reshape(cg, ky, plan.dx, LANES)
    return jnp.transpose(back, (2, 0, 1, 3))


def gelu(value):
    return 0.5 * value * (1.0 + lax.erf(value * (0.5**0.5)))


def pool_tables(plan):
    half = plan.cy // 2
    quarter = half // 2
    rows = np.einsum(
        "cC,yY->ycCY", np.eye(CP)[:, : plan.channels], np.kron(np.eye(quarter), np.ones((1, 2)))
    ).reshape(quarter * CP, plan.channels * half)
    rows = np.concatenate([rows, rows], 1)
    pairs = np.kron(np.eye(plan.cz), np.full((2, 1), 0.125))
    return const(rows), const(pairs)


def pool_body(plan, field, rows_table, pair_table, out):
    half = plan.cy // 2
    quarter = half // 2
    cells = plan.channels * half
    for h in range(2):
        columns = []
        for x in range(plan.cx // 2):
            columns.append(
                jnp.concatenate(
                    [
                        field[:, 2 * x + e, h * half : (h + 1) * half].reshape(cells, plan.cz)
                        for e in range(2)
                    ],
                    axis=0,
                )
            )
        summed = dot(rows_table[...], jnp.concatenate(columns, axis=1))
        blocks = []
        for x in range(plan.cx // 2):
            for j in range(quarter // 2):
                blocks.append(
                    jnp.concatenate(
                        [
                            summed[
                                (2 * j + e) * CP : (2 * j + e + 1) * CP,
                                x * plan.cz : (x + 1) * plan.cz,
                            ]
                            for e in range(2)
                        ],
                        axis=1,
                    )
                )
        block = jnp.concatenate(blocks, axis=0)
        high = block.astype(BF16)
        low = (block - high.astype(F32)).astype(BF16)
        result = dot(high, pair_table[...]) + dot(low, pair_table[...])
        index = 0
        for x in range(plan.cx // 2):
            for j in range(quarter // 2):
                out[x, h * (quarter // 2) + j] = result[index * CP : (index + 1) * CP].astype(BF16)
                index += 1


def tap_columns(volume, x, tiles):
    lane = lax.broadcasted_iota(jnp.int32, (CP, LANES), 1)
    z = lane % (LANES // 2)
    lower = lane < LANES // 2
    shifted = {}
    for j in range(tiles[0] - 1, tiles[1] + 1):
        value = volume[x, j].astype(F32)
        versions = (
            jnp.where(z == 0, 0.0, pltpu.roll(value, 1, 1)),
            value,
            jnp.where(z == LANES // 2 - 1, 0.0, pltpu.roll(value, LANES - 1, 1)),
        )
        shifted[j] = (versions, [pltpu.roll(v, LANES // 2, 1) for v in versions])
    columns = []
    for j in range(tiles[0], tiles[1]):
        pieces = []
        for e in range(3):
            pieces.append(jnp.where(lower, shifted[j - 1][1][e], shifted[j][1][e]))
        for e in range(3):
            pieces.append(shifted[j][0][e])
        for e in range(3):
            pieces.append(jnp.where(lower, shifted[j][1][e], shifted[j + 1][1][e]))
        columns.append(jnp.concatenate(pieces, axis=0).astype(BF16))
    return jnp.concatenate(columns, axis=1)


def combined(partial, x, cols):
    return (
        partial[x, 0:CP, cols]
        + partial[x + 1, CP : 2 * CP, cols]
        + partial[x + 2, 2 * CP : 3 * CP, cols]
    )


def activate(plan, planes, tiles, partial, volume):
    nx = plan.cx // 2
    ny = plan.cy // 4
    here_x = lax.axis_index("gx")
    here_y = lax.axis_index("gy")
    one = jnp.float32(1.0)
    zero = jnp.float32(0.0)
    below_x = jnp.where(here_x > 0, one, zero)
    above_x = jnp.where(here_x < plan.dx - 1, one, zero)
    below_y = jnp.where(here_y > 0, one, zero)
    above_y = jnp.where(here_y < plan.dy - 1, one, zero)
    margin = (planes - nx) // 2

    def body(x, carry):
        inside = jnp.where(x < margin, below_x, one) * jnp.where(x >= margin + nx, above_x, one)
        for j in range(tiles[0], tiles[1]):
            cols = slice((j - tiles[0]) * LANES, (j - tiles[0] + 1) * LANES)
            scale = inside
            if j < 2:
                scale = scale * below_y
            if j >= 2 + ny:
                scale = scale * above_y
            value = gelu(combined(partial, x, cols)) * scale
            volume[x, j] = value.astype(volume.dtype)
        return carry

    lax.fori_loop(0, planes, body, 0, unroll=2)


def where_bf16(mask):
    return jnp.where(mask, 1.0, 0.0).astype(BF16)


def iota(shape, dim):
    return lax.broadcasted_iota(jnp.int32, shape, dim)


def make_lift(plan, point, lift):
    half = plan.cy // 2
    cells = plan.channels * half
    tall = (cells, plan.channels)
    flat = (plan.channels, cells)
    square = (cells, cells)
    pick_o = where_bf16(iota(tall, 0) // half == iota(tall, 1))
    pick_i = where_bf16(iota(flat, 1) // half == iota(flat, 0))
    expanded = dot(dot(pick_o, point[...]).astype(BF16), pick_i)
    diagonal = iota(square, 0) % half == iota(square, 1) % half
    lift[:, :cells] = jnp.where(diagonal, expanded, 0.0).astype(BF16)
    coarse = (cells, half // 2 * CP)
    row, col = iota(coarse, 0), iota(coarse, 1)
    lift[:, cells:] = where_bf16(
        (row // half == col % CP) & ((row % half) // 2 == col // CP)
    )


def conv_own_body(plan, volume_in, filters, point, partial, lift):
    nx = plan.cx // 2
    ny = plan.cy // 4
    make_lift(plan, point, lift)

    def body(x, carry):
        partial[x] = dot(filters[0], tap_columns(volume_in, x, (1, ny + 3)))
        return carry

    lax.fori_loop(0, nx, body, 0, unroll=2)


def prefetches(sources, targets, sems):
    return [
        pltpu.make_async_copy(s, t, sems.at[n]) for n, (s, t) in enumerate(zip(sources, targets))
    ]


def conv_middle_body(
    plan, after, near, far, own, filters, table_in, swap_in,
    second, table, swap, partial, volume, sems,
):
    copies = prefetches((table_in, swap_in), (table, swap), sems)
    for copy in copies:
        copy.start()
    nx = plan.cx // 2
    ny = plan.cy // 4
    wide = ny + 4
    tiles = (1, ny + 3)

    even = lax.rem(lax.axis_index("gx"), 2) == 0
    near_at = jnp.where(even, 3 + nx, 0)
    far_at = jnp.where(even, 0, 3 + nx)

    def edges(x, carry):
        partial[near_at + x] = dot(filters[0], tap_columns(near, x, tiles))
        partial[far_at + x] = dot(filters[0], tap_columns(far, x, tiles))
        return carry

    lax.fori_loop(0, 3, edges, 0)
    for x in range(nx):
        partial[x + 3] = own[x]
    activate(plan, nx + 4, tiles, partial, volume)
    zero = jnp.zeros((CP, LANES), volume.dtype)
    for x in range(nx + 4):
        volume[x, 0] = zero
        volume[x, wide - 1] = zero

    def body(x, carry):
        partial[x] = dot(filters[1], tap_columns(volume, x, tiles))
        return carry

    lax.fori_loop(0, nx + 4, body, 0, unroll=2)
    activate(plan, nx + 2, tiles, partial, second)
    for copy in copies:
        copy.wait()


def conv_last_body(plan, after, second, filters, *rest):
    sources, third, targets, partial, sems = rest[:4], rest[4], rest[5:9], rest[9], rest[10]
    copies = prefetches(sources, targets, sems)
    for copy in copies:
        copy.start()
    nx = plan.cx // 2
    ny = plan.cy // 4
    tiles = (2, ny + 2)

    def body(x, carry):
        partial[x] = dot(filters[2], tap_columns(second, x, tiles))
        return carry

    lax.fori_loop(0, nx + 2, body, 0, unroll=True)

    square = (LANES, 2 * LANES)
    spread = where_bf16(iota(square, 1) // 2 == iota(square, 0))

    def up(x, carry):
        for j in range(ny):
            total = combined(partial, x, slice(j * LANES, (j + 1) * LANES))
            wide = dot(total.astype(BF16), spread).astype(BF16)
            third[x, 2 * j] = wide[:, : plan.cz]
            third[x, 2 * j + 1] = wide[:, plan.cz :]
        return carry

    lax.fori_loop(0, nx, up, 0, unroll=True)
    for copy in copies:
        copy.wait()


def final_body(plan, field, third, lift, regroup, inverse, own, *rest):
    messages = rest[: plan.dy - 1]
    out, line, lanes = rest[plan.dy - 1 :]
    step = pl.program_id(0)
    half = plan.cy // 2
    part = plan.cg * plan.cy

    @pl.when(step == 0)
    def _():
        here = lax.axis_index("gy")
        line[here] = own[...]
        for s, message in enumerate(messages):
            line[turn(here, -(s + 1), plan.dy)] = message[...]
        gathered = jnp.concatenate([line[s] for s in range(plan.dy)], axis=1)
        result = dot(gathered, regroup[...]).astype(BF16)
        width = plan.dy * plan.unit
        for g in range(plan.groups):
            lanes[g * part : (g + 1) * part] = result[:, g * width : (g + 1) * width]

    cells = plan.channels * half
    columns = []
    planes = out.shape[1]
    for e in range(planes):
        for h in range(2):
            cols = third[step * (planes // 2) + e // 2, h * (half // 2) : (h + 1) * (half // 2)]
            columns.append(
                jnp.concatenate(
                    [
                        field[:, planes * step + e, h * half : (h + 1) * half].reshape(cells, plan.cz),
                        cols.astype(F32).reshape(half // 2 * CP, plan.cz).astype(BF16),
                    ],
                    axis=0,
                )
            )
    local = dot(lift[...], jnp.concatenate(columns, axis=1))
    at = pl.multiple_of(step * planes * plan.cz, planes * plan.cz)
    spectral = dot(lanes[...], inverse[:, pl.ds(at, planes * plan.cz)]).reshape(
        plan.channels, plan.cy, planes * plan.cz
    )
    for e in range(planes):
        for h in range(2):
            index = e * 2 + h
            total = local[:, index * plan.cz : (index + 1) * plan.cz].reshape(
                plan.channels, half, plan.cz
            ) + spectral[:, h * half : (h + 1) * half, e * plan.cz : (e + 1) * plan.cz]
            out[:, e, h * half : (h + 1) * half] = gelu(total).astype(BF16)


def after(values, marker):
    return lax.optimization_barrier((values, marker))[0]


def ring(value, axis, shift):
    count = lax.axis_size(axis)
    return lax.ppermute(value, axis, [(i, (i + shift) % count) for i in range(count)])


def on_device(features, spectral_weight, conv_weight, point_weight):
    devices_x = lax.axis_size("gx")
    devices_y = lax.axis_size("gy")
    plan = Plan(features.shape, spectral_weight.shape, devices_x, devices_y)
    channels, cx, cy, cz = features.shape
    shape = jax.ShapeDtypeStruct
    cg = plan.cg
    nx, ny = cx // 2, cy // 4
    part = cg * cy
    split = plan.ky % 16 == 0 and plan.kz * plan.kx == LANES
    half = cy // 2

    rows_table, pair_table = pool_tables(plan)
    tables = (
        plan.forward_z(), plan.regroup(plan.groups, devices_y), rows_table, pair_table,
        plan.forward_y(), plan.swap(1.0),
    )
    chunk = shape((part, LANES), BF16)
    message = shape((part + nx * 2 * TALL, LANES), BF16)
    outs = [chunk, message, message] + [chunk] * (devices_y - 3)
    outs += [shape((nx, ny, CP, cz), BF16)] + [shape(t.shape, BF16) for t in tables[4:]]
    if split:
        early, late = channels // 6, channels // 4
        pack = lambda n: shape((n, 2, channels, plan.ky, LANES), BF16)
        hold = lambda n: [
            pltpu.VMEM((n, 2) + spectral_weight.shape[2:], F32), pltpu.SemaphoreType.DMA((n,))
        ]
    first = call(
        functools.partial(first_body, plan),
        outs,
        (features,) + tables,
        scratch=[pltpu.VMEM(features.shape, BF16)]
        + [pltpu.VMEM(t.shape, BF16) for t in tables[:4]]
        + [pltpu.VMEM((devices_y, part, LANES), BF16), pltpu.SemaphoreType.DMA((8,))],
        specs=[HBM] * 7,
        vmem=16,
    )
    own, to_up, to_down = first[:3]
    middle = first[3:-3]
    coarse, y_table, y_swap = first[-3:]
    low_message = ring(to_up, "gy", 1)
    high_message = ring(to_down, "gy", -1)
    middle = [ring(m, "gy", s + 2) for s, m in enumerate(middle)]

    if split:
        packed_early = call(
            functools.partial(early_body, plan),
            pack(early),
            (own, spectral_weight),
            specs=[ANY, HBM],
            out_specs=[FAR],
            scratch=hold(early),
            moved=2e6,
        )
        own = after(own, packed_early)

    y_out = (devices_x, cg, plan.ky) if split else (1, cg, plan.my)
    planes = shape((3, ny + 4, CP, LANES), BF16)
    y_spec, near, far, volume = call(
        functools.partial(forward_y_body, plan),
        (shape(y_out + (LANES,), BF16), planes, planes, shape((nx, ny + 4, CP, LANES), BF16)),
        (own, low_message, high_message, *middle, coarse, y_table, y_swap),
        out_specs=[PLAIN, FAR, FAR, VMEM],
        scratch=[pltpu.VMEM((devices_y, part, LANES), BF16)],
    )
    if not split:
        y_spec = jnp.transpose(y_spec.reshape(cg, devices_x, plan.ky, LANES), (1, 0, 2, 3))
    pencil = lax.all_to_all(y_spec, "gx", 0, 0, tiled=True)

    filters = jnp.pad(
        conv_weight.reshape(3, 3, 9, channels, channels),
        ((0, 0), (0, 0), (0, 0), (0, CP - channels), (0, CP - channels)),
    )
    filters = jnp.transpose(filters, (0, 1, 3, 2, 4)).reshape(3, 3 * CP, 9 * CP)
    wide = (ny + 2) * LANES
    small = (
        shape((nx, 3 * CP, wide), F32),
        shape((channels * half, channels * half + half // 2 * CP), BF16),
    )
    local = (volume, filters, jnp.transpose(point_weight))
    if split:
        tables = (plan.forward_x(), plan.inverse_x())
        packed_late, partial_own, lift, forward_x, inverse_x = call(
            functools.partial(window_body, plan, early),
            (pack(late),) + small + tuple(shape(t.shape, BF16) for t in tables),
            (y_spec,) + local + (spectral_weight,) + tables,
            specs=[ANY] + [VMEM, PLAIN, PLAIN] + [HBM] * 3,
            out_specs=[FAR, FAR, FAR, VMEM, VMEM],
            scratch=hold(late) + [pltpu.SemaphoreType.DMA((2,))],
            vmem=12,
            flops=4e9,
            moved=8e6,
        )
    else:
        partial_own, lift = call(
            functools.partial(conv_own_body, plan),
            small,
            local,
            specs=[VMEM, PLAIN, PLAIN],
            out_specs=[FAR, FAR],
            flops=2e9,
        )
    near, far = after((near, far), partial_own)
    pairs = [(i, i ^ 1) for i in range(devices_x)]
    near = lax.ppermute(near, "gx", pairs)
    pairs = [(i, i + 1) for i in range(1, devices_x - 1, 2)]
    far = lax.ppermute(far, "gx", pairs + [(t, s) for s, t in pairs])

    if split:
        back = call(
            functools.partial(x_body, plan),
            shape((devices_x, cg, plan.ky, LANES), BF16),
            (pencil, forward_x, packed_early, packed_late, inverse_x, spectral_weight),
            specs=[VMEM, VMEM, HBM, HBM, VMEM, HBM],
            out_specs=[PLAIN],
            scratch=[
                pltpu.VMEM((early + late, 2, channels, plan.ky, LANES), BF16),
                pltpu.SemaphoreType.DMA((2,)),
            ]
            + hold(channels - early - late)
            + [pltpu.VMEM((2, channels, plan.ky, LANES), F32)] * 2,
            vmem=20,
        )
    else:
        back = x_stage_general(plan, pencil, spectral_weight)
    line = lax.all_to_all(back, "gx", 0, 0, tiled=True)

    tables = (plan.inverse_y(), plan.swap(-1.0))
    second, inverse_table, inverse_swap = call(
        functools.partial(conv_middle_body, plan),
        [shape((nx + 2, ny + 4, CP, LANES), F32)] + [shape(t.shape, BF16) for t in tables],
        (back, near, far, partial_own, filters) + tables,
        scratch=[
            pltpu.VMEM((nx + 6, 3 * CP, wide), F32),
            pltpu.VMEM((nx + 4, ny + 4, CP, LANES), F32),
            pltpu.SemaphoreType.DMA((2,)),
        ],
        specs=[ANY, PLAIN, PLAIN, FAR, PLAIN, HBM, HBM],
        out_specs=[PLAIN, VMEM, VMEM],
        vmem=8,
        flops=6e9,
    )
    if not split:
        line = jnp.transpose(line, (1, 0, 2, 3)).reshape(1, cg, plan.my, LANES)
    own, *messages = call(
        functools.partial(inverse_y_body, plan),
        [chunk] * devices_y,
        (line, inverse_table, inverse_swap),
        scratch=[pltpu.VMEM((devices_y, part, LANES), BF16)],
    )
    arrived = [ring(m, "gy", s + 1) for s, m in enumerate(messages)]
    tables = (features, lift, plan.regroup(devices_y, plan.groups), plan.inverse_z())
    third, *tables = call(
        functools.partial(conv_last_body, plan),
        [shape((nx, 2 * ny, CP, cz), BF16)] + [shape(t.shape, BF16) for t in tables],
        (own, second, filters) + tables,
        scratch=[
            pltpu.VMEM((nx + 2, 3 * CP, ny * LANES), F32), pltpu.SemaphoreType.DMA((4,))
        ],
        specs=[ANY, PLAIN, PLAIN] + [HBM] * 4,
        out_specs=[PLAIN] + [VMEM] * 4,
        flops=3e9,
    )
    near = lambda array: pltpu.with_memory_space_constraint(array, pltpu.VMEM)
    field, lift, regroup, inverse_z = (near(t) for t in tables)

    return call(
        functools.partial(final_body, plan),
        shape(features.shape, BF16),
        (field, third, lift, regroup, inverse_z, own, *arrived),
        pin=False,
        grid=(nx // 2,),
        specs=[VMEM] * (5 + devices_y),
        out_specs=[pl.BlockSpec((channels, 4, cy, cz), lambda s: (0, s, 0, 0))],
        scratch=[
            pltpu.VMEM((devices_y, part, LANES), BF16),
            pltpu.VMEM((channels * cy, devices_y * plan.unit), BF16),
        ],
        vmem=12,
    )


def solution(mesh):
    in_specs = (P(None, ("grp", "gx"), "gy", None), P(None, None, None, "gy", "gx", None), P(), P())
    out_specs = P(None, ("grp", "gx"), "gy", None)
    return jax.shard_map(
        on_device, mesh=mesh, in_specs=in_specs, out_specs=out_specs, check_vma=False
    )
```

```python
import functools
import math

import jax
import jax.numpy as jnp
import numpy as np
from jax import lax
from jax.experimental import pallas as pl
from jax.experimental.pallas import tpu as pltpu
from jax.sharding import PartitionSpec as P

LANES = 128
CP = 24
TALL = 32
BF16 = jnp.bfloat16
F32 = jnp.float32
MIB = 1024 * 1024


def dot(left, right):
    return jnp.dot(left, right, preferred_element_type=F32)


def signed_modes(count):
    position = np.arange(count)
    return np.where(position < count // 2, position, position - count)


def phase(frequency, length):
    index = np.mod(frequency[:, None] * np.arange(length)[None, :], length)
    angle = index.astype(np.float32) * np.float32(2.0 * math.pi / length)
    return (
        np.cos(angle).astype(BF16).astype(np.float32),
        np.sin(angle).astype(BF16).astype(np.float32),
    )


def const(array):
    return np.asarray(array, np.float32).astype(BF16)


class Plan:
    def __init__(self, features, spectral_weight, devices_x, devices_y):
        self.channels, self.cx, self.cy, self.cz = features
        self.dx, self.dy = devices_x, devices_y
        self.kz, self.ky, self.kx = spectral_weight[3:]
        self.gx, self.gy = self.cx * self.dx, self.cy * self.dy
        self.my = self.ky * self.dx
        self.mz = self.kz * self.dy
        self.unit = 2 * self.kz * self.cx
        self.groups = LANES // self.unit
        self.cg = self.channels // self.groups

    def forward_z(self):
        cos, sin = phase(np.arange(self.mz), self.cz)
        table = np.stack([cos, -sin], 0).reshape(2, self.dy, self.kz, self.cz)
        out = np.einsum("pdkz,xw->xzdpkw", table, np.eye(self.cx))
        return const(out.reshape(self.cx * self.cz, self.dy * self.unit))

    def inverse_z(self):
        cos, sin = phase(np.arange(self.mz), self.cz)
        scale = np.where(np.arange(self.mz) == 0, 1.0, 2.0) / float(self.gx * self.gy * self.cz)
        table = np.stack([cos, -sin], 0) * scale[None, :, None]
        table = table.reshape(2, self.dy, self.kz, self.cz)
        out = np.einsum("pdkz,xw->dpkxwz", table, np.eye(self.cx))
        return const(out.reshape(self.dy * self.unit, self.cx * self.cz))

    def regroup(self, outer, inner):
        out = np.einsum("ac,bd,lm->abldcm", np.eye(outer), np.eye(inner), np.eye(self.unit))
        size = outer * inner * self.unit
        return const(out.reshape(size, size))

    def swap(self, sign):
        turn = np.array([[0.0, -sign], [sign, 0.0]])
        half = self.unit // 2
        return const(np.kron(np.eye(self.groups), np.kron(turn, np.eye(half))))

    def forward_y(self):
        cos, sin = phase(signed_modes(self.my), self.gy)
        return const(np.concatenate([cos, sin], 1))

    def inverse_y(self):
        cos, sin = phase(signed_modes(self.my), self.gy)
        return const(np.concatenate([cos.T, sin.T], 1))

    def turn_x(self, sign):
        cos, sin = phase(signed_modes(self.kx), self.gx)
        turn = np.stack([np.stack([cos, -sign * sin]), np.stack([sign * sin, cos])])
        return turn.reshape(2, 2, self.kx, self.dx, self.cx)

    def forward_x(self):
        out = np.einsum("pqjsx,g,kl->sgpkxqlj", self.turn_x(1.0), np.ones(self.groups), np.eye(self.kz))
        return const(out.reshape(self.dx * LANES, self.kz * 2 * self.kx))

    def inverse_x(self):
        out = np.einsum("pqjsx,h,kl->pkjshqlx", self.turn_x(-1.0), np.ones(self.groups), np.eye(self.kz))
        return const(out.reshape(self.kz * 2 * self.kx, self.dx * LANES))


VMEM = pl.BlockSpec(memory_space=pltpu.VMEM)
PLAIN = pl.BlockSpec(memory_space=pltpu.VMEM)
FAR = pl.BlockSpec(memory_space=pltpu.VMEM)


ANY = pl.BlockSpec(memory_space=pl.ANY)
HBM = pl.BlockSpec(memory_space=pltpu.HBM)


def pinned(value, spec):
    if spec is HBM or spec is FAR:
        return pltpu.with_memory_space_constraint(jnp.asarray(value), pltpu.HBM)
    if spec is ANY or spec is PLAIN or isinstance(value, np.ndarray):
        return value
    return pltpu.with_memory_space_constraint(value, pltpu.VMEM)


def call(
    body, outs, inputs, scratch=(), specs=None, out_specs=None, vmem=8, flops=1e9, moved=1e6,
    pin=True, **kw,
):
    single = not isinstance(outs, (tuple, list))
    outs = [outs] if single else list(outs)
    specs = specs or [VMEM] * len(inputs)
    out_specs = out_specs or [VMEM] * len(outs)
    if pin:
        inputs = [pinned(value, spec) for value, spec in zip(inputs, specs)]
        outs = [
            pltpu.VMEM(o.shape, o.dtype)
            if spec is VMEM
            else pltpu.HBM(o.shape, o.dtype) if spec is FAR else o
            for o, spec in zip(outs, out_specs)
        ]
    result = pl.pallas_call(
        body,
        out_shape=outs,
        in_specs=specs,
        out_specs=out_specs,
        scratch_shapes=scratch,
        compiler_params=pltpu.CompilerParams(vmem_limit_bytes=vmem * MIB),
        cost_estimate=pl.CostEstimate(
            flops=int(flops), bytes_accessed=int(moved), transcendentals=0
        ),
        **kw,
    )(*inputs)
    return result[0] if single else result


def turn(index, shift, count):
    return lax.rem(index + shift + count, count)


def taller(tile):
    none = jnp.zeros((TALL - CP, LANES), F32)
    return jnp.concatenate([tile.astype(F32), none], axis=0).astype(BF16)


def first_body(
    plan, field_in, table_in, regroup_in, rows_in, pair_in, ytable_in, swap_in, *rest
):
    own, low_message, high_message, *rest = rest
    middle = rest[: plan.dy - 3]
    coarse, ytable, swap, field, table, regroup, rows_table, pair_table, chunks, sems = rest[
        plan.dy - 3 :
    ]
    middle_channel = plan.channels // 2
    lower = pl.ds(0, middle_channel)
    upper = pl.ds(middle_channel, plan.channels - middle_channel)
    sources = (
        table_in, field_in.at[lower], field_in.at[upper],
        regroup_in, rows_in, pair_in, ytable_in, swap_in,
    )
    targets = (
        table, field.at[lower], field.at[upper], regroup, rows_table, pair_table, ytable, swap
    )
    copies = [
        pltpu.make_async_copy(s, t, sems.at[n]) for n, (s, t) in enumerate(zip(sources, targets))
    ]
    for copy in copies:
        copy.start()
    copies[0].wait()
    pieces = []
    for n, (low, high) in enumerate(((0, middle_channel), (middle_channel, plan.channels))):
        copies[1 + n].wait()
        rows = (high - low) * plan.cy
        lhs = jnp.concatenate(
            [field[low:high, x].reshape(rows, plan.cz) for x in range(plan.cx)], axis=1
        )
        pieces.append(dot(lhs, table[...]).astype(BF16))
    modes = jnp.concatenate(pieces, axis=0)
    copies[3].wait()
    part = plan.cg * plan.cy
    lanes = jnp.concatenate(
        [modes[g * part : (g + 1) * part] for g in range(plan.groups)], axis=1
    )
    result = dot(lanes, regroup[...]).astype(BF16)
    for d in range(plan.dy):
        chunks[d] = result[:, d * LANES : (d + 1) * LANES]
    for copy in copies[4:]:
        copy.wait()
    pool_body(plan, field, rows_table, pair_table, coarse)
    here = lax.axis_index("gy")
    own[...] = chunks[here]
    low_message[:part] = chunks[turn(here, 1, plan.dy)]
    high_message[:part] = chunks[turn(here, plan.dy - 1, plan.dy)]
    for s, message in enumerate(middle):
        message[...] = chunks[turn(here, s + 2, plan.dy)]
    tiles = plan.cy // 4
    index = 0
    for x in range(plan.cx // 2):
        for j in range(2):
            at = slice(part + index * TALL, part + (index + 1) * TALL)
            low_message[at] = taller(coarse[x, tiles - 2 + j])
            high_message[at] = taller(coarse[x, j])
            index += 1


def y_transform(plan, line, table, swap):
    columns = []
    for value in line:
        turned = dot(value, swap[...]).astype(BF16)
        columns.append(jnp.concatenate([value, turned], axis=0))
    return dot(table[...], jnp.concatenate(columns, axis=1)).astype(BF16)


def forward_y_body(plan, own, low_message, high_message, *rest):
    middle = rest[: plan.dy - 3]
    coarse, table, swap, out, near, far, volume, line = rest[plan.dy - 3 :]
    part = plan.cg * plan.cy
    here = lax.axis_index("gy")
    line[here] = own[...]
    line[turn(here, -1, plan.dy)] = low_message[:part]
    line[turn(here, 1, plan.dy)] = high_message[:part]
    for s, message in enumerate(middle):
        line[turn(here, -(s + 2), plan.dy)] = message[...]
    values = [
        jnp.concatenate(
            [line[s, c * plan.cy : (c + 1) * plan.cy] for s in range(plan.dy)], axis=0
        )
        for c in range(plan.cg)
    ]
    result = y_transform(plan, values, table, swap)
    targets, _, rows_out, _ = out.shape
    for d in range(targets):
        for c in range(plan.cg):
            out[d, c] = result[
                d * rows_out : (d + 1) * rows_out, c * LANES : (c + 1) * LANES
            ]
    nx = plan.cx // 2
    tiles = plan.cy // 4
    for x in range(nx):
        for j in range(2):
            at = slice(part + (x * 2 + j) * TALL, part + (x * 2 + j + 1) * TALL)
            low = low_message[at].astype(F32)[:CP]
            high = high_message[at].astype(F32)[:CP]
            volume[x, j] = jnp.where(here > 0, low, 0.0).astype(BF16)
            volume[x, 2 + tiles + j] = jnp.where(here < plan.dy - 1, high, 0.0).astype(BF16)
        for j in range(tiles):
            volume[x, 2 + j] = coarse[x, j]
    even = lax.rem(lax.axis_index("gx"), 2) == 0
    first_plane = jnp.where(even, nx - 3, 0)
    last_plane = jnp.where(even, 0, nx - 3)
    for x in range(3):
        near[x] = volume[first_plane + x]
        far[x] = volume[last_plane + x]


def inverse_y_body(plan, line, table, swap, own, *rest):
    messages = rest[: plan.dy - 1]
    chunks = rest[plan.dy - 1]
    sources = line.shape[0]
    values = [
        jnp.concatenate([line[s, c] for s in range(sources)], axis=0) for c in range(plan.cg)
    ]
    result = y_transform(plan, values, table, swap)
    for d in range(plan.dy):
        for c in range(plan.cg):
            chunks[d, c * plan.cy : (c + 1) * plan.cy] = result[
                d * plan.cy : (d + 1) * plan.cy, c * LANES : (c + 1) * LANES
            ]
    here = lax.axis_index("gy")
    own[...] = chunks[here]
    for s, message in enumerate(messages):
        message[...] = chunks[turn(here, s + 1, plan.dy)]


def mix(plan, spec, weight, mixed):
    def step(o, carry):
        for k in range(plan.kz):
            real = jnp.zeros((plan.ky, plan.kx), F32)
            imag = jnp.zeros((plan.ky, plan.kx), F32)
            for i in range(plan.channels):
                wr = weight[0, i, o, k]
                wi = weight[1, i, o, k]
                xr = spec[0, k, i]
                xi = spec[1, k, i]
                real += xr * wr - xi * wi
                imag += xr * wi + xi * wr
            mixed[k, o] = jnp.concatenate([real, imag], axis=1)
        return carry

    lax.fori_loop(0, plan.channels, step, 0)


def weight_copy(weight, held, sems, begin, n):
    return pltpu.make_async_copy(weight.at[:, begin + n], held.at[n], sems.at[n])


def start_weights(weight, held, sems, begin):
    def one(n, carry):
        weight_copy(weight, held, sems, begin, n).start()
        return carry

    lax.fori_loop(0, held.shape[0], one, 0)


def pack_weights(plan, weight, held, sems, begin, packed):
    def one(n, carry):
        weight_copy(weight, held, sems, begin, n).wait()
        for p in range(2):
            for o in range(plan.channels):
                packed[n, p, o] = jnp.concatenate(
                    [held[n, p, o, k] for k in range(plan.kz)], axis=1
                ).astype(BF16)
        return carry

    lax.fori_loop(0, held.shape[0], one, 0)


def early_body(plan, after, weight, packed, held, sems):
    start_weights(weight, held, sems, 0)
    pack_weights(plan, weight, held, sems, 0, packed)


def window_body(
    plan, begin, after, volume, filters, point, weight, forward_in, inverse_in,
    packed, partial, lift, forward, inverse, held, sems, table_sems,
):
    copies = prefetches((forward_in, inverse_in), (forward, inverse), table_sems)
    for copy in copies:
        copy.start()
    start_weights(weight, held, sems, begin)
    conv_own_body(plan, volume, filters, point, partial, lift)
    pack_weights(plan, weight, held, sems, begin, packed)
    for copy in copies:
        copy.wait()


def lane_group(plan, shape):
    return (lax.broadcasted_iota(jnp.int32, shape, 1) % LANES) // plan.unit


def by_group(plan, lanes):
    owner = lane_group(plan, lanes.shape)
    return jnp.concatenate(
        [jnp.where(owner == g, lanes, jnp.zeros_like(lanes)) for g in range(plan.groups)], axis=0
    )


def one_group(plan, stacked):
    rows = stacked.shape[0] // plan.groups
    owner = lane_group(plan, (rows, stacked.shape[1]))
    result = stacked[:rows]
    for g in range(1, plan.groups):
        result = jnp.where(owner == g, stacked[g * rows : (g + 1) * rows], result)
    return result


def x_body(
    plan, pencil, forward, packed_early, packed_late, inverse, weight, out,
    packed, sems, held, held_sems, spec, mixed,
):
    early = packed_early.shape[0]
    ready = packed.shape[0]
    copies = [
        pltpu.make_async_copy(packed_early, packed.at[pl.ds(0, early)], sems.at[0]),
        pltpu.make_async_copy(packed_late, packed.at[pl.ds(early, ready - early)], sems.at[1]),
    ]
    for copy in copies:
        copy.start()
    start_weights(weight, held, held_sems, ready)
    rows = plan.cg * plan.ky
    wide = plan.kz * plan.kx
    lhs = jnp.concatenate([pencil[s].reshape(rows, LANES) for s in range(plan.dx)], axis=1)
    spectrum = dot(by_group(plan, lhs), forward[...])
    for g in range(plan.groups):
        for p in range(2):
            modes = spectrum[g * rows : (g + 1) * rows, p * wide : (p + 1) * wide]
            spec[p, g * plan.cg : (g + 1) * plan.cg] = modes.reshape(plan.cg, plan.ky, wide)

    def step(o, carry):
        real = jnp.zeros((plan.ky, wide), F32)
        imag = jnp.zeros((plan.ky, wide), F32)
        for i in range(ready):
            wr = packed[i, 0, o].astype(F32)
            wi = packed[i, 1, o].astype(F32)
            xr = spec[0, i]
            xi = spec[1, i]
            real += xr * wr - xi * wi
            imag += xr * wi + xi * wr
        mixed[0, o] = real
        mixed[1, o] = imag
        return carry

    def streamed(n, carry):
        weight_copy(weight, held, held_sems, ready, n).wait()
        xr = spec[0, ready + n]
        xi = spec[1, ready + n]
        for o in range(plan.channels):
            wr, wi = (
                jnp.concatenate([held[n, p, o, k] for k in range(plan.kz)], axis=1)
                for p in range(2)
            )
            mixed[0, o] += xr * wr - xi * wi
            mixed[1, o] += xr * wi + xi * wr
        return carry

    for copy in copies:
        copy.wait()
    lax.fori_loop(0, plan.channels, step, 0, unroll=2)
    lax.fori_loop(0, plan.channels - ready, streamed, 0)
    back = jnp.concatenate(
        [
            jnp.concatenate(
                [
                    mixed[p, g * plan.cg : (g + 1) * plan.cg].reshape(rows, wide).astype(BF16)
                    for p in range(2)
                ],
                axis=1,
            )
            for g in range(plan.groups)
        ],
        axis=0,
    )
    result = one_group(plan, dot(back, inverse[...])).astype(BF16)
    for d in range(plan.dx):
        out[d] = result[:, d * LANES : (d + 1) * LANES].reshape(plan.cg, plan.ky, LANES)


def x_stage_general(plan, pencil, weight):
    groups, cg, ky, kz, kx = plan.groups, plan.cg, plan.ky, plan.kz, plan.kx
    lhs = jnp.transpose(pencil, (1, 2, 0, 3)).reshape(cg * ky, plan.dx * LANES)
    spectrum = dot(by_group(plan, lhs), plan.forward_x()).reshape(groups, cg, ky, 2, kz, kx)
    spectrum = jnp.transpose(spectrum, (3, 4, 0, 1, 2, 5)).reshape(2, kz, groups * cg, ky, kx)
    mixed = call(
        functools.partial(mix, plan),
        jax.ShapeDtypeStruct((kz, groups * cg, ky, 2 * kx), F32),
        (spectrum, weight),
        vmem=32,
        pin=False,
    )
    back = jnp.transpose(mixed.reshape(kz, groups, cg, ky, 2, kx), (1, 2, 3, 4, 0, 5))
    back = back.reshape(groups * cg * ky, kz * 2 * kx).astype(BF16)
    back = one_group(plan, dot(back, plan.inverse_x())).astype(BF16)
    back = back.reshape(cg, ky, plan.dx, LANES)
    return jnp.transpose(back, (2, 0, 1, 3))


def gelu(value):
    return 0.5 * value * (1.0 + lax.erf(value * (0.5**0.5)))


def pool_tables(plan):
    half = plan.cy // 2
    quarter = half // 2
    rows = np.einsum(
        "cC,yY->ycCY", np.eye(CP)[:, : plan.channels], np.kron(np.eye(quarter), np.ones((1, 2)))
    ).reshape(quarter * CP, plan.channels * half)
    rows = np.concatenate([rows, rows], 1)
    pairs = np.kron(np.eye(plan.cz), np.full((2, 1), 0.125))
    return const(rows), const(pairs)


def pool_body(plan, field, rows_table, pair_table, out):
    half = plan.cy // 2
    quarter = half // 2
    cells = plan.channels * half
    for h in range(2):
        columns = []
        for x in range(plan.cx // 2):
            columns.append(
                jnp.concatenate(
                    [
                        field[:, 2 * x + e, h * half : (h + 1) * half].reshape(cells, plan.cz)
                        for e in range(2)
                    ],
                    axis=0,
                )
            )
        summed = dot(rows_table[...], jnp.concatenate(columns, axis=1))
        blocks = []
        for x in range(plan.cx // 2):
            for j in range(quarter // 2):
                blocks.append(
                    jnp.concatenate(
                        [
                            summed[
                                (2 * j + e) * CP : (2 * j + e + 1) * CP,
                                x * plan.cz : (x + 1) * plan.cz,
                            ]
                            for e in range(2)
                        ],
                        axis=1,
                    )
                )
        block = jnp.concatenate(blocks, axis=0)
        high = block.astype(BF16)
        low = (block - high.astype(F32)).astype(BF16)
        result = dot(high, pair_table[...]) + dot(low, pair_table[...])
        index = 0
        for x in range(plan.cx // 2):
            for j in range(quarter // 2):
                out[x, h * (quarter // 2) + j] = result[index * CP : (index + 1) * CP].astype(BF16)
                index += 1


def tap_columns(volume, x, tiles):
    lane = lax.broadcasted_iota(jnp.int32, (CP, LANES), 1)
    z = lane % (LANES // 2)
    lower = lane < LANES // 2
    shifted = {}
    for j in range(tiles[0] - 1, tiles[1] + 1):
        value = volume[x, j].astype(F32)
        versions = (
            jnp.where(z == 0, 0.0, pltpu.roll(value, 1, 1)),
            value,
            jnp.where(z == LANES // 2 - 1, 0.0, pltpu.roll(value, LANES - 1, 1)),
        )
        shifted[j] = (versions, [pltpu.roll(v, LANES // 2, 1) for v in versions])
    columns = []
    for j in range(tiles[0], tiles[1]):
        pieces = []
        for e in range(3):
            pieces.append(jnp.where(lower, shifted[j - 1][1][e], shifted[j][1][e]))
        for e in range(3):
            pieces.append(shifted[j][0][e])
        for e in range(3):
            pieces.append(jnp.where(lower, shifted[j][1][e], shifted[j + 1][1][e]))
        columns.append(jnp.concatenate(pieces, axis=0).astype(BF16))
    return jnp.concatenate(columns, axis=1)


def combined(partial, x, cols):
    return (
        partial[x, 0:CP, cols]
        + partial[x + 1, CP : 2 * CP, cols]
        + partial[x + 2, 2 * CP : 3 * CP, cols]
    )


def activate(plan, planes, tiles, partial, volume):
    nx = plan.cx // 2
    ny = plan.cy // 4
    here_x = lax.axis_index("gx")
    here_y = lax.axis_index("gy")
    one = jnp.float32(1.0)
    zero = jnp.float32(0.0)
    below_x = jnp.where(here_x > 0, one, zero)
    above_x = jnp.where(here_x < plan.dx - 1, one, zero)
    below_y = jnp.where(here_y > 0, one, zero)
    above_y = jnp.where(here_y < plan.dy - 1, one, zero)
    margin = (planes - nx) // 2

    def body(x, carry):
        inside = jnp.where(x < margin, below_x, one) * jnp.where(x >= margin + nx, above_x, one)
        for j in range(tiles[0], tiles[1]):
            cols = slice((j - tiles[0]) * LANES, (j - tiles[0] + 1) * LANES)
            scale = inside
            if j < 2:
                scale = scale * below_y
            if j >= 2 + ny:
                scale = scale * above_y
            value = gelu(combined(partial, x, cols)) * scale
            volume[x, j] = value.astype(volume.dtype)
        return carry

    lax.fori_loop(0, planes, body, 0, unroll=2)


def where_bf16(mask):
    return jnp.where(mask, 1.0, 0.0).astype(BF16)


def iota(shape, dim):
    return lax.broadcasted_iota(jnp.int32, shape, dim)


def make_lift(plan, point, lift):
    half = plan.cy // 2
    cells = plan.channels * half
    tall = (cells, plan.channels)
    flat = (plan.channels, cells)
    square = (cells, cells)
    pick_o = where_bf16(iota(tall, 0) // half == iota(tall, 1))
    pick_i = where_bf16(iota(flat, 1) // half == iota(flat, 0))
    expanded = dot(dot(pick_o, point[...]).astype(BF16), pick_i)
    diagonal = iota(square, 0) % half == iota(square, 1) % half
    lift[:, :cells] = jnp.where(diagonal, expanded, 0.0).astype(BF16)
    coarse = (cells, half // 2 * CP)
    row, col = iota(coarse, 0), iota(coarse, 1)
    lift[:, cells:] = where_bf16(
        (row // half == col % CP) & ((row % half) // 2 == col // CP)
    )


def conv_own_body(plan, volume_in, filters, point, partial, lift):
    nx = plan.cx // 2
    ny = plan.cy // 4
    make_lift(plan, point, lift)

    def body(x, carry):
        partial[x] = dot(filters[0], tap_columns(volume_in, x, (1, ny + 3)))
        return carry

    lax.fori_loop(0, nx, body, 0, unroll=2)


def prefetches(sources, targets, sems):
    return [
        pltpu.make_async_copy(s, t, sems.at[n]) for n, (s, t) in enumerate(zip(sources, targets))
    ]


def conv_middle_body(
    plan, after, near, far, own, filters, table_in, swap_in,
    second, table, swap, partial, volume, sems,
):
    copies = prefetches((table_in, swap_in), (table, swap), sems)
    for copy in copies:
        copy.start()
    nx = plan.cx // 2
    ny = plan.cy // 4
    wide = ny + 4
    tiles = (1, ny + 3)

    even = lax.rem(lax.axis_index("gx"), 2) == 0
    near_at = jnp.where(even, 3 + nx, 0)
    far_at = jnp.where(even, 0, 3 + nx)

    def edges(x, carry):
        partial[near_at + x] = dot(filters[0], tap_columns(near, x, tiles))
        partial[far_at + x] = dot(filters[0], tap_columns(far, x, tiles))
        return carry

    lax.fori_loop(0, 3, edges, 0)
    for x in range(nx):
        partial[x + 3] = own[x]
    activate(plan, nx + 4, tiles, partial, volume)
    zero = jnp.zeros((CP, LANES), volume.dtype)
    for x in range(nx + 4):
        volume[x, 0] = zero
        volume[x, wide - 1] = zero

    def body(x, carry):
        partial[x] = dot(filters[1], tap_columns(volume, x, tiles))
        return carry

    lax.fori_loop(0, nx + 4, body, 0, unroll=2)
    activate(plan, nx + 2, tiles, partial, second)
    for copy in copies:
        copy.wait()


def conv_last_body(plan, after, second, filters, *rest):
    sources, third, targets, partial, sems = rest[:4], rest[4], rest[5:9], rest[9], rest[10]
    copies = prefetches(sources, targets, sems)
    for copy in copies:
        copy.start()
    nx = plan.cx // 2
    ny = plan.cy // 4
    tiles = (2, ny + 2)

    def body(x, carry):
        partial[x] = dot(filters[2], tap_columns(second, x, tiles))
        return carry

    lax.fori_loop(0, nx + 2, body, 0, unroll=True)

    square = (LANES, 2 * LANES)
    spread = where_bf16(iota(square, 1) // 2 == iota(square, 0))

    def up(x, carry):
        for j in range(ny):
            total = combined(partial, x, slice(j * LANES, (j + 1) * LANES))
            wide = dot(total.astype(BF16), spread).astype(BF16)
            third[x, 2 * j] = wide[:, : plan.cz]
            third[x, 2 * j + 1] = wide[:, plan.cz :]
        return carry

    lax.fori_loop(0, nx, up, 0, unroll=True)
    for copy in copies:
        copy.wait()


def final_body(plan, field, third, lift, regroup, inverse, own, *rest):
    messages = rest[: plan.dy - 1]
    out, line, lanes = rest[plan.dy - 1 :]
    step = pl.program_id(0)
    half = plan.cy // 2
    part = plan.cg * plan.cy

    @pl.when(step == 0)
    def _():
        here = lax.axis_index("gy")
        line[here] = own[...]
        for s, message in enumerate(messages):
            line[turn(here, -(s + 1), plan.dy)] = message[...]
        gathered = jnp.concatenate([line[s] for s in range(plan.dy)], axis=1)
        result = dot(gathered, regroup[...]).astype(BF16)
        width = plan.dy * plan.unit
        for g in range(plan.groups):
            lanes[g * part : (g + 1) * part] = result[:, g * width : (g + 1) * width]

    cells = plan.channels * half
    columns = []
    planes = out.shape[1]
    for e in range(planes):
        for h in range(2):
            cols = third[step * (planes // 2) + e // 2, h * (half // 2) : (h + 1) * (half // 2)]
            columns.append(
                jnp.concatenate(
                    [
                        field[:, planes * step + e, h * half : (h + 1) * half].reshape(cells, plan.cz),
                        cols.astype(F32).reshape(half // 2 * CP, plan.cz).astype(BF16),
                    ],
                    axis=0,
                )
            )
    local = dot(lift[...], jnp.concatenate(columns, axis=1))
    at = pl.multiple_of(step * planes * plan.cz, planes * plan.cz)
    spectral = dot(lanes[...], inverse[:, pl.ds(at, planes * plan.cz)]).reshape(
        plan.channels, plan.cy, planes * plan.cz
    )
    for e in range(planes):
        for h in range(2):
            index = e * 2 + h
            total = local[:, index * plan.cz : (index + 1) * plan.cz].reshape(
                plan.channels, half, plan.cz
            ) + spectral[:, h * half : (h + 1) * half, e * plan.cz : (e + 1) * plan.cz]
            out[:, e, h * half : (h + 1) * half] = gelu(total).astype(BF16)


def after(values, marker):
    return lax.optimization_barrier((values, marker))[0]


def ring(value, axis, shift):
    count = lax.axis_size(axis)
    return lax.ppermute(value, axis, [(i, (i + shift) % count) for i in range(count)])


def on_device(features, spectral_weight, conv_weight, point_weight):
    devices_x = lax.axis_size("gx")
    devices_y = lax.axis_size("gy")
    plan = Plan(features.shape, spectral_weight.shape, devices_x, devices_y)
    channels, cx, cy, cz = features.shape
    shape = jax.ShapeDtypeStruct
    cg = plan.cg
    nx, ny = cx // 2, cy // 4
    part = cg * cy
    split = plan.ky % 16 == 0 and plan.kz * plan.kx == LANES
    half = cy // 2

    rows_table, pair_table = pool_tables(plan)
    tables = (
        plan.forward_z(), plan.regroup(plan.groups, devices_y), rows_table, pair_table,
        plan.forward_y(), plan.swap(1.0),
    )
    chunk = shape((part, LANES), BF16)
    message = shape((part + nx * 2 * TALL, LANES), BF16)
    outs = [chunk, message, message] + [chunk] * (devices_y - 3)
    outs += [shape((nx, ny, CP, cz), BF16)] + [shape(t.shape, BF16) for t in tables[4:]]
    if split:
        early, late = channels // 10, 3 * channels // 10
        pack = lambda n: shape((n, 2, channels, plan.ky, LANES), BF16)
        hold = lambda n: [
            pltpu.VMEM((n, 2) + spectral_weight.shape[2:], F32), pltpu.SemaphoreType.DMA((n,))
        ]
    first = call(
        functools.partial(first_body, plan),
        outs,
        (features,) + tables,
        scratch=[pltpu.VMEM(features.shape, BF16)]
        + [pltpu.VMEM(t.shape, BF16) for t in tables[:4]]
        + [pltpu.VMEM((devices_y, part, LANES), BF16), pltpu.SemaphoreType.DMA((8,))],
        specs=[HBM] * 7,
        vmem=16,
    )
    own, to_up, to_down = first[:3]
    middle = first[3:-3]
    coarse, y_table, y_swap = first[-3:]
    low_message = ring(to_up, "gy", 1)
    high_message = ring(to_down, "gy", -1)
    middle = [ring(m, "gy", s + 2) for s, m in enumerate(middle)]

    if split:
        packed_early = call(
            functools.partial(early_body, plan),
            pack(early),
            (own, spectral_weight),
            specs=[ANY, HBM],
            out_specs=[FAR],
            scratch=hold(early),
            moved=2e6,
        )
        own = after(own, packed_early)

    y_out = (devices_x, cg, plan.ky) if split else (1, cg, plan.my)
    planes = shape((3, ny + 4, CP, LANES), BF16)
    y_spec, near, far, volume = call(
        functools.partial(forward_y_body, plan),
        (shape(y_out + (LANES,), BF16), planes, planes, shape((nx, ny + 4, CP, LANES), BF16)),
        (own, low_message, high_message, *middle, coarse, y_table, y_swap),
        out_specs=[PLAIN, FAR, FAR, VMEM],
        scratch=[pltpu.VMEM((devices_y, part, LANES), BF16)],
    )
    if not split:
        y_spec = jnp.transpose(y_spec.reshape(cg, devices_x, plan.ky, LANES), (1, 0, 2, 3))
    pencil = lax.all_to_all(y_spec, "gx", 0, 0, tiled=True)

    filters = jnp.pad(
        conv_weight.reshape(3, 3, 9, channels, channels),
        ((0, 0), (0, 0), (0, 0), (0, CP - channels), (0, CP - channels)),
    )
    filters = jnp.transpose(filters, (0, 1, 3, 2, 4)).reshape(3, 3 * CP, 9 * CP)
    wide = (ny + 2) * LANES
    small = (
        shape((nx, 3 * CP, wide), F32),
        shape((channels * half, channels * half + half // 2 * CP), BF16),
    )
    local = (volume, filters, jnp.transpose(point_weight))
    if split:
        tables = (plan.forward_x(), plan.inverse_x())
        packed_late, partial_own, lift, forward_x, inverse_x = call(
            functools.partial(window_body, plan, early),
            (pack(late),) + small + tuple(shape(t.shape, BF16) for t in tables),
            (y_spec,) + local + (spectral_weight,) + tables,
            specs=[ANY] + [VMEM, PLAIN, PLAIN] + [HBM] * 3,
            out_specs=[FAR, FAR, FAR, VMEM, VMEM],
            scratch=hold(late) + [pltpu.SemaphoreType.DMA((2,))],
            vmem=12,
            flops=4e9,
            moved=8e6,
        )
    else:
        partial_own, lift = call(
            functools.partial(conv_own_body, plan),
            small,
            local,
            specs=[VMEM, PLAIN, PLAIN],
            out_specs=[FAR, FAR],
            flops=2e9,
        )
    near, far = after((near, far), partial_own)
    pairs = [(i, i ^ 1) for i in range(devices_x)]
    near = lax.ppermute(near, "gx", pairs)
    pairs = [(i, i + 1) for i in range(1, devices_x - 1, 2)]
    far = lax.ppermute(far, "gx", pairs + [(t, s) for s, t in pairs])

    if split:
        back = call(
            functools.partial(x_body, plan),
            shape((devices_x, cg, plan.ky, LANES), BF16),
            (pencil, forward_x, packed_early, packed_late, inverse_x, spectral_weight),
            specs=[VMEM, VMEM, HBM, HBM, VMEM, HBM],
            out_specs=[PLAIN],
            scratch=[
                pltpu.VMEM((early + late, 2, channels, plan.ky, LANES), BF16),
                pltpu.SemaphoreType.DMA((2,)),
            ]
            + hold(channels - early - late)
            + [pltpu.VMEM((2, channels, plan.ky, LANES), F32)] * 2,
            vmem=20,
        )
    else:
        back = x_stage_general(plan, pencil, spectral_weight)
    line = lax.all_to_all(back, "gx", 0, 0, tiled=True)

    tables = (plan.inverse_y(), plan.swap(-1.0))
    second, inverse_table, inverse_swap = call(
        functools.partial(conv_middle_body, plan),
        [shape((nx + 2, ny + 4, CP, LANES), F32)] + [shape(t.shape, BF16) for t in tables],
        (back, near, far, partial_own, filters) + tables,
        scratch=[
            pltpu.VMEM((nx + 6, 3 * CP, wide), F32),
            pltpu.VMEM((nx + 4, ny + 4, CP, LANES), F32),
            pltpu.SemaphoreType.DMA((2,)),
        ],
        specs=[ANY, PLAIN, PLAIN, FAR, PLAIN, HBM, HBM],
        out_specs=[PLAIN, VMEM, VMEM],
        vmem=8,
        flops=6e9,
    )
    if not split:
        line = jnp.transpose(line, (1, 0, 2, 3)).reshape(1, cg, plan.my, LANES)
    own, *messages = call(
        functools.partial(inverse_y_body, plan),
        [chunk] * devices_y,
        (line, inverse_table, inverse_swap),
        scratch=[pltpu.VMEM((devices_y, part, LANES), BF16)],
    )
    arrived = [ring(m, "gy", s + 1) for s, m in enumerate(messages)]
    tables = (features, lift, plan.regroup(devices_y, plan.groups), plan.inverse_z())
    third, *tables = call(
        functools.partial(conv_last_body, plan),
        [shape((nx, 2 * ny, CP, cz), BF16)] + [shape(t.shape, BF16) for t in tables],
        (own, second, filters) + tables,
        scratch=[
            pltpu.VMEM((nx + 2, 3 * CP, ny * LANES), F32), pltpu.SemaphoreType.DMA((4,))
        ],
        specs=[ANY, PLAIN, PLAIN] + [HBM] * 4,
        out_specs=[PLAIN] + [VMEM] * 4,
        flops=3e9,
    )
    near = lambda array: pltpu.with_memory_space_constraint(array, pltpu.VMEM)
    field, lift, regroup, inverse_z = (near(t) for t in tables)

    return call(
        functools.partial(final_body, plan),
        shape(features.shape, BF16),
        (field, third, lift, regroup, inverse_z, own, *arrived),
        pin=False,
        grid=(nx // 2,),
        specs=[VMEM] * (5 + devices_y),
        out_specs=[pl.BlockSpec((channels, 4, cy, cz), lambda s: (0, s, 0, 0))],
        scratch=[
            pltpu.VMEM((devices_y, part, LANES), BF16),
            pltpu.VMEM((channels * cy, devices_y * plan.unit), BF16),
        ],
        vmem=12,
    )


def solution(mesh):
    in_specs = (P(None, ("grp", "gx"), "gy", None), P(None, None, None, "gy", "gx", None), P(), P())
    out_specs = P(None, ("grp", "gx"), "gy", None)
    return jax.shard_map(
        on_device, mesh=mesh, in_specs=in_specs, out_specs=out_specs, check_vma=False
    )
```

```python
import functools
import math

import jax
import jax.numpy as jnp
import numpy as np
from jax import lax
from jax.experimental import pallas as pl
from jax.experimental.pallas import tpu as pltpu
from jax.sharding import PartitionSpec as P

LANES = 128
CP = 24
TALL = 32
BF16 = jnp.bfloat16
F32 = jnp.float32
MIB = 1024 * 1024


def dot(left, right):
    return jnp.dot(left, right, preferred_element_type=F32)


def signed_modes(count):
    position = np.arange(count)
    return np.where(position < count // 2, position, position - count)


def phase(frequency, length):
    index = np.mod(frequency[:, None] * np.arange(length)[None, :], length)
    angle = index.astype(np.float32) * np.float32(2.0 * math.pi / length)
    return (
        np.cos(angle).astype(BF16).astype(np.float32),
        np.sin(angle).astype(BF16).astype(np.float32),
    )


def const(array):
    return np.asarray(array, np.float32).astype(BF16)


class Plan:
    def __init__(self, features, spectral_weight, devices_x, devices_y):
        self.channels, self.cx, self.cy, self.cz = features
        self.dx, self.dy = devices_x, devices_y
        self.kz, self.ky, self.kx = spectral_weight[3:]
        self.gx, self.gy = self.cx * self.dx, self.cy * self.dy
        self.my = self.ky * self.dx
        self.mz = self.kz * self.dy
        self.unit = 2 * self.kz * self.cx
        self.groups = LANES // self.unit
        self.cg = self.channels // self.groups

    def forward_z(self):
        cos, sin = phase(np.arange(self.mz), self.cz)
        table = np.stack([cos, -sin], 0).reshape(2, self.dy, self.kz, self.cz)
        out = np.einsum("pdkz,xw->xzdpkw", table, np.eye(self.cx))
        return const(out.reshape(self.cx * self.cz, self.dy * self.unit))

    def inverse_z(self):
        cos, sin = phase(np.arange(self.mz), self.cz)
        scale = np.where(np.arange(self.mz) == 0, 1.0, 2.0) / float(self.gx * self.gy * self.cz)
        table = np.stack([cos, -sin], 0) * scale[None, :, None]
        table = table.reshape(2, self.dy, self.kz, self.cz)
        out = np.einsum("pdkz,xw->dpkxwz", table, np.eye(self.cx))
        return const(out.reshape(self.dy * self.unit, self.cx * self.cz))

    def regroup(self, outer, inner):
        out = np.einsum("ac,bd,lm->abldcm", np.eye(outer), np.eye(inner), np.eye(self.unit))
        size = outer * inner * self.unit
        return const(out.reshape(size, size))

    def swap(self, sign):
        turn = np.array([[0.0, -sign], [sign, 0.0]])
        half = self.unit // 2
        return const(np.kron(np.eye(self.groups), np.kron(turn, np.eye(half))))

    def forward_y(self):
        cos, sin = phase(signed_modes(self.my), self.gy)
        return const(np.concatenate([cos, sin], 1))

    def inverse_y(self):
        cos, sin = phase(signed_modes(self.my), self.gy)
        return const(np.concatenate([cos.T, sin.T], 1))

    def turn_x(self, sign):
        cos, sin = phase(signed_modes(self.kx), self.gx)
        turn = np.stack([np.stack([cos, -sign * sin]), np.stack([sign * sin, cos])])
        return turn.reshape(2, 2, self.kx, self.dx, self.cx)

    def forward_x(self):
        out = np.einsum("pqjsx,g,kl->sgpkxqlj", self.turn_x(1.0), np.ones(self.groups), np.eye(self.kz))
        return const(out.reshape(self.dx * LANES, self.kz * 2 * self.kx))

    def inverse_x(self):
        out = np.einsum("pqjsx,h,kl->pkjshqlx", self.turn_x(-1.0), np.ones(self.groups), np.eye(self.kz))
        return const(out.reshape(self.kz * 2 * self.kx, self.dx * LANES))


VMEM = pl.BlockSpec(memory_space=pltpu.VMEM)
PLAIN = pl.BlockSpec(memory_space=pltpu.VMEM)
FAR = pl.BlockSpec(memory_space=pltpu.VMEM)


ANY = pl.BlockSpec(memory_space=pl.ANY)
HBM = pl.BlockSpec(memory_space=pltpu.HBM)


def pinned(value, spec):
    if spec is HBM or spec is FAR:
        return pltpu.with_memory_space_constraint(jnp.asarray(value), pltpu.HBM)
    if spec is ANY or spec is PLAIN or isinstance(value, np.ndarray):
        return value
    return pltpu.with_memory_space_constraint(value, pltpu.VMEM)


def call(
    body, outs, inputs, scratch=(), specs=None, out_specs=None, vmem=8, flops=1e9, moved=1e6,
    pin=True, **kw,
):
    single = not isinstance(outs, (tuple, list))
    outs = [outs] if single else list(outs)
    specs = specs or [VMEM] * len(inputs)
    out_specs = out_specs or [VMEM] * len(outs)
    if pin:
        inputs = [pinned(value, spec) for value, spec in zip(inputs, specs)]
        outs = [
            pltpu.VMEM(o.shape, o.dtype)
            if spec is VMEM
            else pltpu.HBM(o.shape, o.dtype) if spec is FAR else o
            for o, spec in zip(outs, out_specs)
        ]
    result = pl.pallas_call(
        body,
        out_shape=outs,
        in_specs=specs,
        out_specs=out_specs,
        scratch_shapes=scratch,
        compiler_params=pltpu.CompilerParams(vmem_limit_bytes=vmem * MIB),
        cost_estimate=pl.CostEstimate(
            flops=int(flops), bytes_accessed=int(moved), transcendentals=0
        ),
        **kw,
    )(*inputs)
    return result[0] if single else result


def turn(index, shift, count):
    return lax.rem(index + shift + count, count)


def taller(tile):
    none = jnp.zeros((TALL - CP, LANES), F32)
    return jnp.concatenate([tile.astype(F32), none], axis=0).astype(BF16)


def first_body(
    plan, field_in, table_in, regroup_in, rows_in, pair_in, ytable_in, swap_in, *rest
):
    own, low_message, high_message, *rest = rest
    middle = rest[: plan.dy - 3]
    coarse, ytable, swap, field, table, regroup, rows_table, pair_table, chunks, sems = rest[
        plan.dy - 3 :
    ]
    middle_channel = plan.channels // 2
    lower = pl.ds(0, middle_channel)
    upper = pl.ds(middle_channel, plan.channels - middle_channel)
    sources = (
        table_in, field_in.at[lower], field_in.at[upper],
        regroup_in, rows_in, pair_in, ytable_in, swap_in,
    )
    targets = (
        table, field.at[lower], field.at[upper], regroup, rows_table, pair_table, ytable, swap
    )
    copies = [
        pltpu.make_async_copy(s, t, sems.at[n]) for n, (s, t) in enumerate(zip(sources, targets))
    ]
    for copy in copies:
        copy.start()
    copies[0].wait()
    pieces = []
    for n, (low, high) in enumerate(((0, middle_channel), (middle_channel, plan.channels))):
        copies[1 + n].wait()
        rows = (high - low) * plan.cy
        lhs = jnp.concatenate(
            [field[low:high, x].reshape(rows, plan.cz) for x in range(plan.cx)], axis=1
        )
        pieces.append(dot(lhs, table[...]).astype(BF16))
    modes = jnp.concatenate(pieces, axis=0)
    copies[3].wait()
    part = plan.cg * plan.cy
    lanes = jnp.concatenate(
        [modes[g * part : (g + 1) * part] for g in range(plan.groups)], axis=1
    )
    result = dot(lanes, regroup[...]).astype(BF16)
    for d in range(plan.dy):
        chunks[d] = result[:, d * LANES : (d + 1) * LANES]
    for copy in copies[4:]:
        copy.wait()
    pool_body(plan, field, rows_table, pair_table, coarse)
    here = lax.axis_index("gy")
    own[...] = chunks[here]
    low_message[:part] = chunks[turn(here, 1, plan.dy)]
    high_message[:part] = chunks[turn(here, plan.dy - 1, plan.dy)]
    for s, message in enumerate(middle):
        message[...] = chunks[turn(here, s + 2, plan.dy)]
    tiles = plan.cy // 4
    index = 0
    for x in range(plan.cx // 2):
        for j in range(2):
            at = slice(part + index * TALL, part + (index + 1) * TALL)
            low_message[at] = taller(coarse[x, tiles - 2 + j])
            high_message[at] = taller(coarse[x, j])
            index += 1


def y_transform(plan, line, table, swap):
    columns = []
    for value in line:
        turned = dot(value, swap[...]).astype(BF16)
        columns.append(jnp.concatenate([value, turned], axis=0))
    return dot(table[...], jnp.concatenate(columns, axis=1)).astype(BF16)


def forward_y_body(plan, own, low_message, high_message, *rest):
    middle = rest[: plan.dy - 3]
    coarse, table, swap, out, near, far, volume, line = rest[plan.dy - 3 :]
    part = plan.cg * plan.cy
    here = lax.axis_index("gy")
    line[here] = own[...]
    line[turn(here, -1, plan.dy)] = low_message[:part]
    line[turn(here, 1, plan.dy)] = high_message[:part]
    for s, message in enumerate(middle):
        line[turn(here, -(s + 2), plan.dy)] = message[...]
    values = [
        jnp.concatenate(
            [line[s, c * plan.cy : (c + 1) * plan.cy] for s in range(plan.dy)], axis=0
        )
        for c in range(plan.cg)
    ]
    result = y_transform(plan, values, table, swap)
    targets, _, rows_out, _ = out.shape
    for d in range(targets):
        for c in range(plan.cg):
            out[d, c] = result[
                d * rows_out : (d + 1) * rows_out, c * LANES : (c + 1) * LANES
            ]
    nx = plan.cx // 2
    tiles = plan.cy // 4
    for x in range(nx):
        for j in range(2):
            at = slice(part + (x * 2 + j) * TALL, part + (x * 2 + j + 1) * TALL)
            low = low_message[at].astype(F32)[:CP]
            high = high_message[at].astype(F32)[:CP]
            volume[x, j] = jnp.where(here > 0, low, 0.0).astype(BF16)
            volume[x, 2 + tiles + j] = jnp.where(here < plan.dy - 1, high, 0.0).astype(BF16)
        for j in range(tiles):
            volume[x, 2 + j] = coarse[x, j]
    even = lax.rem(lax.axis_index("gx"), 2) == 0
    first_plane = jnp.where(even, nx - 3, 0)
    last_plane = jnp.where(even, 0, nx - 3)
    for x in range(3):
        near[x] = volume[first_plane + x]
        far[x] = volume[last_plane + x]


def inverse_y_body(plan, line, table, swap, own, *rest):
    messages = rest[: plan.dy - 1]
    chunks = rest[plan.dy - 1]
    sources = line.shape[0]
    values = [
        jnp.concatenate([line[s, c] for s in range(sources)], axis=0) for c in range(plan.cg)
    ]
    result = y_transform(plan, values, table, swap)
    for d in range(plan.dy):
        for c in range(plan.cg):
            chunks[d, c * plan.cy : (c + 1) * plan.cy] = result[
                d * plan.cy : (d + 1) * plan.cy, c * LANES : (c + 1) * LANES
            ]
    here = lax.axis_index("gy")
    own[...] = chunks[here]
    for s, message in enumerate(messages):
        message[...] = chunks[turn(here, s + 1, plan.dy)]


def mix(plan, spec, weight, mixed):
    def step(o, carry):
        for k in range(plan.kz):
            real = jnp.zeros((plan.ky, plan.kx), F32)
            imag = jnp.zeros((plan.ky, plan.kx), F32)
            for i in range(plan.channels):
                wr = weight[0, i, o, k]
                wi = weight[1, i, o, k]
                xr = spec[0, k, i]
                xi = spec[1, k, i]
                real += xr * wr - xi * wi
                imag += xr * wi + xi * wr
            mixed[k, o] = jnp.concatenate([real, imag], axis=1)
        return carry

    lax.fori_loop(0, plan.channels, step, 0)


def weight_copy(weight, held, sems, begin, n):
    return pltpu.make_async_copy(weight.at[:, begin + n], held.at[n], sems.at[n])


def start_weights(weight, held, sems, begin):
    def one(n, carry):
        weight_copy(weight, held, sems, begin, n).start()
        return carry

    lax.fori_loop(0, held.shape[0], one, 0)


def pack_weights(plan, weight, held, sems, begin, packed):
    def one(n, carry):
        weight_copy(weight, held, sems, begin, n).wait()
        for p in range(2):
            for o in range(plan.channels):
                packed[n, p, o] = jnp.concatenate(
                    [held[n, p, o, k] for k in range(plan.kz)], axis=1
                ).astype(BF16)
        return carry

    lax.fori_loop(0, held.shape[0], one, 0)


def early_body(plan, after, weight, packed, held, sems):
    start_weights(weight, held, sems, 0)
    pack_weights(plan, weight, held, sems, 0, packed)


def window_body(
    plan, begin, after, volume, filters, point, weight, forward_in, inverse_in,
    packed, partial, lift, forward, inverse, held, sems, table_sems,
):
    copies = prefetches((forward_in, inverse_in), (forward, inverse), table_sems)
    for copy in copies:
        copy.start()
    start_weights(weight, held, sems, begin)
    conv_own_body(plan, volume, filters, point, partial, lift)
    pack_weights(plan, weight, held, sems, begin, packed)
    for copy in copies:
        copy.wait()


def lane_group(plan, shape):
    return (lax.broadcasted_iota(jnp.int32, shape, 1) % LANES) // plan.unit


def by_group(plan, lanes):
    owner = lane_group(plan, lanes.shape)
    return jnp.concatenate(
        [jnp.where(owner == g, lanes, jnp.zeros_like(lanes)) for g in range(plan.groups)], axis=0
    )


def one_group(plan, stacked):
    rows = stacked.shape[0] // plan.groups
    owner = lane_group(plan, (rows, stacked.shape[1]))
    result = stacked[:rows]
    for g in range(1, plan.groups):
        result = jnp.where(owner == g, stacked[g * rows : (g + 1) * rows], result)
    return result


def x_body(
    plan, pencil, forward, packed_early, packed_late, inverse, weight, out,
    packed, sems, held, held_sems, spec, mixed,
):
    early = packed_early.shape[0]
    ready = packed.shape[0]
    copies = [
        pltpu.make_async_copy(packed_early, packed.at[pl.ds(0, early)], sems.at[0]),
        pltpu.make_async_copy(packed_late, packed.at[pl.ds(early, ready - early)], sems.at[1]),
    ]
    for copy in copies:
        copy.start()
    start_weights(weight, held, held_sems, ready)
    rows = plan.cg * plan.ky
    wide = plan.kz * plan.kx
    lhs = jnp.concatenate([pencil[s].reshape(rows, LANES) for s in range(plan.dx)], axis=1)
    spectrum = dot(by_group(plan, lhs), forward[...])
    for g in range(plan.groups):
        for p in range(2):
            modes = spectrum[g * rows : (g + 1) * rows, p * wide : (p + 1) * wide]
            spec[p, g * plan.cg : (g + 1) * plan.cg] = modes.reshape(plan.cg, plan.ky, wide)

    def step(o, carry):
        real = jnp.zeros((plan.ky, wide), F32)
        imag = jnp.zeros((plan.ky, wide), F32)
        for i in range(ready):
            wr = packed[i, 0, o].astype(F32)
            wi = packed[i, 1, o].astype(F32)
            xr = spec[0, i]
            xi = spec[1, i]
            real += xr * wr - xi * wi
            imag += xr * wi + xi * wr
        mixed[0, o] = real
        mixed[1, o] = imag
        return carry

    def streamed(n, carry):
        weight_copy(weight, held, held_sems, ready, n).wait()
        xr = spec[0, ready + n]
        xi = spec[1, ready + n]
        for o in range(plan.channels):
            wr, wi = (
                jnp.concatenate([held[n, p, o, k] for k in range(plan.kz)], axis=1)
                for p in range(2)
            )
            mixed[0, o] += xr * wr - xi * wi
            mixed[1, o] += xr * wi + xi * wr
        return carry

    for copy in copies:
        copy.wait()
    lax.fori_loop(0, plan.channels, step, 0, unroll=4)
    lax.fori_loop(0, plan.channels - ready, streamed, 0)
    back = jnp.concatenate(
        [
            jnp.concatenate(
                [
                    mixed[p, g * plan.cg : (g + 1) * plan.cg].reshape(rows, wide).astype(BF16)
                    for p in range(2)
                ],
                axis=1,
            )
            for g in range(plan.groups)
        ],
        axis=0,
    )
    result = one_group(plan, dot(back, inverse[...])).astype(BF16)
    for d in range(plan.dx):
        out[d] = result[:, d * LANES : (d + 1) * LANES].reshape(plan.cg, plan.ky, LANES)


def x_stage_general(plan, pencil, weight):
    groups, cg, ky, kz, kx = plan.groups, plan.cg, plan.ky, plan.kz, plan.kx
    lhs = jnp.transpose(pencil, (1, 2, 0, 3)).reshape(cg * ky, plan.dx * LANES)
    spectrum = dot(by_group(plan, lhs), plan.forward_x()).reshape(groups, cg, ky, 2, kz, kx)
    spectrum = jnp.transpose(spectrum, (3, 4, 0, 1, 2, 5)).reshape(2, kz, groups * cg, ky, kx)
    mixed = call(
        functools.partial(mix, plan),
        jax.ShapeDtypeStruct((kz, groups * cg, ky, 2 * kx), F32),
        (spectrum, weight),
        vmem=32,
        pin=False,
    )
    back = jnp.transpose(mixed.reshape(kz, groups, cg, ky, 2, kx), (1, 2, 3, 4, 0, 5))
    back = back.reshape(groups * cg * ky, kz * 2 * kx).astype(BF16)
    back = one_group(plan, dot(back, plan.inverse_x())).astype(BF16)
    back = back.reshape(cg, ky, plan.dx, LANES)
    return jnp.transpose(back, (2, 0, 1, 3))


def gelu(value):
    return 0.5 * value * (1.0 + lax.erf(value * (0.5**0.5)))


def pool_tables(plan):
    half = plan.cy // 2
    quarter = half // 2
    rows = np.einsum(
        "cC,yY->ycCY", np.eye(CP)[:, : plan.channels], np.kron(np.eye(quarter), np.ones((1, 2)))
    ).reshape(quarter * CP, plan.channels * half)
    rows = np.concatenate([rows, rows], 1)
    pairs = np.kron(np.eye(plan.cz), np.full((2, 1), 0.125))
    return const(rows), const(pairs)


def pool_body(plan, field, rows_table, pair_table, out):
    half = plan.cy // 2
    quarter = half // 2
    cells = plan.channels * half
    for h in range(2):
        columns = []
        for x in range(plan.cx // 2):
            columns.append(
                jnp.concatenate(
                    [
                        field[:, 2 * x + e, h * half : (h + 1) * half].reshape(cells, plan.cz)
                        for e in range(2)
                    ],
                    axis=0,
                )
            )
        summed = dot(rows_table[...], jnp.concatenate(columns, axis=1))
        blocks = []
        for x in range(plan.cx // 2):
            for j in range(quarter // 2):
                blocks.append(
                    jnp.concatenate(
                        [
                            summed[
                                (2 * j + e) * CP : (2 * j + e + 1) * CP,
                                x * plan.cz : (x + 1) * plan.cz,
                            ]
                            for e in range(2)
                        ],
                        axis=1,
                    )
                )
        block = jnp.concatenate(blocks, axis=0)
        high = block.astype(BF16)
        low = (block - high.astype(F32)).astype(BF16)
        result = dot(high, pair_table[...]) + dot(low, pair_table[...])
        index = 0
        for x in range(plan.cx // 2):
            for j in range(quarter // 2):
                out[x, h * (quarter // 2) + j] = result[index * CP : (index + 1) * CP].astype(BF16)
                index += 1


def tap_columns(volume, x, tiles):
    lane = lax.broadcasted_iota(jnp.int32, (CP, LANES), 1)
    z = lane % (LANES // 2)
    lower = lane < LANES // 2
    shifted = {}
    for j in range(tiles[0] - 1, tiles[1] + 1):
        value = volume[x, j].astype(F32)
        versions = (
            jnp.where(z == 0, 0.0, pltpu.roll(value, 1, 1)),
            value,
            jnp.where(z == LANES // 2 - 1, 0.0, pltpu.roll(value, LANES - 1, 1)),
        )
        shifted[j] = (versions, [pltpu.roll(v, LANES // 2, 1) for v in versions])
    columns = []
    for j in range(tiles[0], tiles[1]):
        pieces = []
        for e in range(3):
            pieces.append(jnp.where(lower, shifted[j - 1][1][e], shifted[j][1][e]))
        for e in range(3):
            pieces.append(shifted[j][0][e])
        for e in range(3):
            pieces.append(jnp.where(lower, shifted[j][1][e], shifted[j + 1][1][e]))
        columns.append(jnp.concatenate(pieces, axis=0).astype(BF16))
    return jnp.concatenate(columns, axis=1)


def combined(partial, x, cols):
    return (
        partial[x, 0:CP, cols]
        + partial[x + 1, CP : 2 * CP, cols]
        + partial[x + 2, 2 * CP : 3 * CP, cols]
    )


def activate(plan, planes, tiles, partial, volume):
    nx = plan.cx // 2
    ny = plan.cy // 4
    here_x = lax.axis_index("gx")
    here_y = lax.axis_index("gy")
    one = jnp.float32(1.0)
    zero = jnp.float32(0.0)
    below_x = jnp.where(here_x > 0, one, zero)
    above_x = jnp.where(here_x < plan.dx - 1, one, zero)
    below_y = jnp.where(here_y > 0, one, zero)
    above_y = jnp.where(here_y < plan.dy - 1, one, zero)
    margin = (planes - nx) // 2

    def body(x, carry):
        inside = jnp.where(x < margin, below_x, one) * jnp.where(x >= margin + nx, above_x, one)
        for j in range(tiles[0], tiles[1]):
            cols = slice((j - tiles[0]) * LANES, (j - tiles[0] + 1) * LANES)
            scale = inside
            if j < 2:
                scale = scale * below_y
            if j >= 2 + ny:
                scale = scale * above_y
            value = gelu(combined(partial, x, cols)) * scale
            volume[x, j] = value.astype(volume.dtype)
        return carry

    lax.fori_loop(0, planes, body, 0, unroll=2)


def where_bf16(mask):
    return jnp.where(mask, 1.0, 0.0).astype(BF16)


def iota(shape, dim):
    return lax.broadcasted_iota(jnp.int32, shape, dim)


def make_lift(plan, point, lift):
    half = plan.cy // 2
    cells = plan.channels * half
    tall = (cells, plan.channels)
    flat = (plan.channels, cells)
    square = (cells, cells)
    pick_o = where_bf16(iota(tall, 0) // half == iota(tall, 1))
    pick_i = where_bf16(iota(flat, 1) // half == iota(flat, 0))
    expanded = dot(dot(pick_o, point[...]).astype(BF16), pick_i)
    diagonal = iota(square, 0) % half == iota(square, 1) % half
    lift[:, :cells] = jnp.where(diagonal, expanded, 0.0).astype(BF16)
    coarse = (cells, half // 2 * CP)
    row, col = iota(coarse, 0), iota(coarse, 1)
    lift[:, cells:] = where_bf16(
        (row // half == col % CP) & ((row % half) // 2 == col // CP)
    )


def conv_own_body(plan, volume_in, filters, point, partial, lift):
    nx = plan.cx // 2
    ny = plan.cy // 4
    make_lift(plan, point, lift)

    def body(x, carry):
        partial[x] = dot(filters[0], tap_columns(volume_in, x, (1, ny + 3)))
        return carry

    lax.fori_loop(0, nx, body, 0, unroll=2)


def prefetches(sources, targets, sems):
    return [
        pltpu.make_async_copy(s, t, sems.at[n]) for n, (s, t) in enumerate(zip(sources, targets))
    ]


def conv_middle_body(
    plan, after, near, far, own, filters, table_in, swap_in,
    second, table, swap, partial, volume, sems,
):
    copies = prefetches((table_in, swap_in), (table, swap), sems)
    for copy in copies:
        copy.start()
    nx = plan.cx // 2
    ny = plan.cy // 4
    wide = ny + 4
    tiles = (1, ny + 3)

    even = lax.rem(lax.axis_index("gx"), 2) == 0
    near_at = jnp.where(even, 3 + nx, 0)
    far_at = jnp.where(even, 0, 3 + nx)

    def edges(x, carry):
        partial[near_at + x] = dot(filters[0], tap_columns(near, x, tiles))
        partial[far_at + x] = dot(filters[0], tap_columns(far, x, tiles))
        return carry

    lax.fori_loop(0, 3, edges, 0)
    for x in range(nx):
        partial[x + 3] = own[x]
    activate(plan, nx + 4, tiles, partial, volume)
    zero = jnp.zeros((CP, LANES), volume.dtype)
    for x in range(nx + 4):
        volume[x, 0] = zero
        volume[x, wide - 1] = zero

    def body(x, carry):
        partial[x] = dot(filters[1], tap_columns(volume, x, tiles))
        return carry

    lax.fori_loop(0, nx + 4, body, 0, unroll=2)
    activate(plan, nx + 2, tiles, partial, second)
    for copy in copies:
        copy.wait()


def conv_last_body(plan, after, second, filters, *rest):
    sources, third, targets, partial, sems = rest[:4], rest[4], rest[5:9], rest[9], rest[10]
    copies = prefetches(sources, targets, sems)
    for copy in copies:
        copy.start()
    nx = plan.cx // 2
    ny = plan.cy // 4
    tiles = (2, ny + 2)

    def body(x, carry):
        partial[x] = dot(filters[2], tap_columns(second, x, tiles))
        return carry

    lax.fori_loop(0, nx + 2, body, 0, unroll=True)

    square = (LANES, 2 * LANES)
    spread = where_bf16(iota(square, 1) // 2 == iota(square, 0))

    def up(x, carry):
        for j in range(ny):
            total = combined(partial, x, slice(j * LANES, (j + 1) * LANES))
            wide = dot(total.astype(BF16), spread).astype(BF16)
            third[x, 2 * j] = wide[:, : plan.cz]
            third[x, 2 * j + 1] = wide[:, plan.cz :]
        return carry

    lax.fori_loop(0, nx, up, 0, unroll=True)
    for copy in copies:
        copy.wait()


def final_body(plan, field, third, lift, regroup, inverse, own, *rest):
    messages = rest[: plan.dy - 1]
    out, line, lanes = rest[plan.dy - 1 :]
    step = pl.program_id(0)
    half = plan.cy // 2
    part = plan.cg * plan.cy

    @pl.when(step == 0)
    def _():
        here = lax.axis_index("gy")
        line[here] = own[...]
        for s, message in enumerate(messages):
            line[turn(here, -(s + 1), plan.dy)] = message[...]
        gathered = jnp.concatenate([line[s] for s in range(plan.dy)], axis=1)
        result = dot(gathered, regroup[...]).astype(BF16)
        width = plan.dy * plan.unit
        for g in range(plan.groups):
            lanes[g * part : (g + 1) * part] = result[:, g * width : (g + 1) * width]

    cells = plan.channels * half
    columns = []
    planes = out.shape[1]
    for e in range(planes):
        for h in range(2):
            cols = third[step * (planes // 2) + e // 2, h * (half // 2) : (h + 1) * (half // 2)]
            columns.append(
                jnp.concatenate(
                    [
                        field[:, planes * step + e, h * half : (h + 1) * half].reshape(cells, plan.cz),
                        cols.astype(F32).reshape(half // 2 * CP, plan.cz).astype(BF16),
                    ],
                    axis=0,
                )
            )
    local = dot(lift[...], jnp.concatenate(columns, axis=1))
    at = pl.multiple_of(step * planes * plan.cz, planes * plan.cz)
    spectral = dot(lanes[...], inverse[:, pl.ds(at, planes * plan.cz)]).reshape(
        plan.channels, plan.cy, planes * plan.cz
    )
    for e in range(planes):
        for h in range(2):
            index = e * 2 + h
            total = local[:, index * plan.cz : (index + 1) * plan.cz].reshape(
                plan.channels, half, plan.cz
            ) + spectral[:, h * half : (h + 1) * half, e * plan.cz : (e + 1) * plan.cz]
            out[:, e, h * half : (h + 1) * half] = gelu(total).astype(BF16)


def after(values, marker):
    return lax.optimization_barrier((values, marker))[0]


def ring(value, axis, shift):
    count = lax.axis_size(axis)
    return lax.ppermute(value, axis, [(i, (i + shift) % count) for i in range(count)])


def on_device(features, spectral_weight, conv_weight, point_weight):
    devices_x = lax.axis_size("gx")
    devices_y = lax.axis_size("gy")
    plan = Plan(features.shape, spectral_weight.shape, devices_x, devices_y)
    channels, cx, cy, cz = features.shape
    shape = jax.ShapeDtypeStruct
    cg = plan.cg
    nx, ny = cx // 2, cy // 4
    part = cg * cy
    split = plan.ky % 16 == 0 and plan.kz * plan.kx == LANES
    half = cy // 2

    rows_table, pair_table = pool_tables(plan)
    tables = (
        plan.forward_z(), plan.regroup(plan.groups, devices_y), rows_table, pair_table,
        plan.forward_y(), plan.swap(1.0),
    )
    chunk = shape((part, LANES), BF16)
    message = shape((part + nx * 2 * TALL, LANES), BF16)
    outs = [chunk, message, message] + [chunk] * (devices_y - 3)
    outs += [shape((nx, ny, CP, cz), BF16)] + [shape(t.shape, BF16) for t in tables[4:]]
    if split:
        early, late = channels // 6, channels // 4
        pack = lambda n: shape((n, 2, channels, plan.ky, LANES), BF16)
        hold = lambda n: [
            pltpu.VMEM((n, 2) + spectral_weight.shape[2:], F32), pltpu.SemaphoreType.DMA((n,))
        ]
    first = call(
        functools.partial(first_body, plan),
        outs,
        (features,) + tables,
        scratch=[pltpu.VMEM(features.shape, BF16)]
        + [pltpu.VMEM(t.shape, BF16) for t in tables[:4]]
        + [pltpu.VMEM((devices_y, part, LANES), BF16), pltpu.SemaphoreType.DMA((8,))],
        specs=[HBM] * 7,
        vmem=16,
    )
    own, to_up, to_down = first[:3]
    middle = first[3:-3]
    coarse, y_table, y_swap = first[-3:]
    low_message = ring(to_up, "gy", 1)
    high_message = ring(to_down, "gy", -1)
    middle = [ring(m, "gy", s + 2) for s, m in enumerate(middle)]

    if split:
        packed_early = call(
            functools.partial(early_body, plan),
            pack(early),
            (own, spectral_weight),
            specs=[ANY, HBM],
            out_specs=[FAR],
            scratch=hold(early),
            moved=2e6,
        )
        own = after(own, packed_early)

    y_out = (devices_x, cg, plan.ky) if split else (1, cg, plan.my)
    planes = shape((3, ny + 4, CP, LANES), BF16)
    y_spec, near, far, volume = call(
        functools.partial(forward_y_body, plan),
        (shape(y_out + (LANES,), BF16), planes, planes, shape((nx, ny + 4, CP, LANES), BF16)),
        (own, low_message, high_message, *middle, coarse, y_table, y_swap),
        out_specs=[PLAIN, FAR, FAR, VMEM],
        scratch=[pltpu.VMEM((devices_y, part, LANES), BF16)],
    )
    if not split:
        y_spec = jnp.transpose(y_spec.reshape(cg, devices_x, plan.ky, LANES), (1, 0, 2, 3))
    pencil = lax.all_to_all(y_spec, "gx", 0, 0, tiled=True)

    filters = jnp.pad(
        conv_weight.reshape(3, 3, 9, channels, channels),
        ((0, 0), (0, 0), (0, 0), (0, CP - channels), (0, CP - channels)),
    )
    filters = jnp.transpose(filters, (0, 1, 3, 2, 4)).reshape(3, 3 * CP, 9 * CP)
    wide = (ny + 2) * LANES
    small = (
        shape((nx, 3 * CP, wide), F32),
        shape((channels * half, channels * half + half // 2 * CP), BF16),
    )
    local = (volume, filters, jnp.transpose(point_weight))
    if split:
        tables = (plan.forward_x(), plan.inverse_x())
        packed_late, partial_own, lift, forward_x, inverse_x = call(
            functools.partial(window_body, plan, early),
            (pack(late),) + small + tuple(shape(t.shape, BF16) for t in tables),
            (y_spec,) + local + (spectral_weight,) + tables,
            specs=[ANY] + [VMEM, PLAIN, PLAIN] + [HBM] * 3,
            out_specs=[FAR, FAR, FAR, VMEM, VMEM],
            scratch=hold(late) + [pltpu.SemaphoreType.DMA((2,))],
            vmem=12,
            flops=4e9,
            moved=8e6,
        )
    else:
        partial_own, lift = call(
            functools.partial(conv_own_body, plan),
            small,
            local,
            specs=[VMEM, PLAIN, PLAIN],
            out_specs=[FAR, FAR],
            flops=2e9,
        )
    near, far = after((near, far), partial_own)
    pairs = [(i, i ^ 1) for i in range(devices_x)]
    near = lax.ppermute(near, "gx", pairs)
    pairs = [(i, i + 1) for i in range(1, devices_x - 1, 2)]
    far = lax.ppermute(far, "gx", pairs + [(t, s) for s, t in pairs])

    if split:
        back = call(
            functools.partial(x_body, plan),
            shape((devices_x, cg, plan.ky, LANES), BF16),
            (pencil, forward_x, packed_early, packed_late, inverse_x, spectral_weight),
            specs=[VMEM, VMEM, HBM, HBM, VMEM, HBM],
            out_specs=[PLAIN],
            scratch=[
                pltpu.VMEM((early + late, 2, channels, plan.ky, LANES), BF16),
                pltpu.SemaphoreType.DMA((2,)),
            ]
            + hold(channels - early - late)
            + [pltpu.VMEM((2, channels, plan.ky, LANES), F32)] * 2,
            vmem=20,
        )
    else:
        back = x_stage_general(plan, pencil, spectral_weight)
    line = lax.all_to_all(back, "gx", 0, 0, tiled=True)

    tables = (plan.inverse_y(), plan.swap(-1.0))
    second, inverse_table, inverse_swap = call(
        functools.partial(conv_middle_body, plan),
        [shape((nx + 2, ny + 4, CP, LANES), F32)] + [shape(t.shape, BF16) for t in tables],
        (back, near, far, partial_own, filters) + tables,
        scratch=[
            pltpu.VMEM((nx + 6, 3 * CP, wide), F32),
            pltpu.VMEM((nx + 4, ny + 4, CP, LANES), F32),
            pltpu.SemaphoreType.DMA((2,)),
        ],
        specs=[ANY, PLAIN, PLAIN, FAR, PLAIN, HBM, HBM],
        out_specs=[PLAIN, VMEM, VMEM],
        vmem=8,
        flops=6e9,
    )
    if not split:
        line = jnp.transpose(line, (1, 0, 2, 3)).reshape(1, cg, plan.my, LANES)
    own, *messages = call(
        functools.partial(inverse_y_body, plan),
        [chunk] * devices_y,
        (line, inverse_table, inverse_swap),
        scratch=[pltpu.VMEM((devices_y, part, LANES), BF16)],
    )
    arrived = [ring(m, "gy", s + 1) for s, m in enumerate(messages)]
    tables = (features, lift, plan.regroup(devices_y, plan.groups), plan.inverse_z())
    third, *tables = call(
        functools.partial(conv_last_body, plan),
        [shape((nx, 2 * ny, CP, cz), BF16)] + [shape(t.shape, BF16) for t in tables],
        (own, second, filters) + tables,
        scratch=[
            pltpu.VMEM((nx + 2, 3 * CP, ny * LANES), F32), pltpu.SemaphoreType.DMA((4,))
        ],
        specs=[ANY, PLAIN, PLAIN] + [HBM] * 4,
        out_specs=[PLAIN] + [VMEM] * 4,
        flops=3e9,
    )
    near = lambda array: pltpu.with_memory_space_constraint(array, pltpu.VMEM)
    field, lift, regroup, inverse_z = (near(t) for t in tables)

    return call(
        functools.partial(final_body, plan),
        shape(features.shape, BF16),
        (field, third, lift, regroup, inverse_z, own, *arrived),
        pin=False,
        grid=(nx // 2,),
        specs=[VMEM] * (5 + devices_y),
        out_specs=[pl.BlockSpec((channels, 4, cy, cz), lambda s: (0, s, 0, 0))],
        scratch=[
            pltpu.VMEM((devices_y, part, LANES), BF16),
            pltpu.VMEM((channels * cy, devices_y * plan.unit), BF16),
        ],
        vmem=12,
    )


def solution(mesh):
    in_specs = (P(None, ("grp", "gx"), "gy", None), P(None, None, None, "gy", "gx", None), P(), P())
    out_specs = P(None, ("grp", "gx"), "gy", None)
    return jax.shard_map(
        on_device, mesh=mesh, in_specs=in_specs, out_specs=out_specs, check_vma=False
    )
```
